256 devices in a mesh: row: 8 (over z), col: 32 (over x, y, core).
Axes of the slice: x: 4, y: 4, z: 8, core: 2. Of those that a mesh axis runs over, the one named last changes fastest.
Arguments:
- anomalies: float32 [28672, 256], P(('col', 'row')), may hold values from -6 to 6
- innovations: float32 [28672, 256], P(('col', 'row')), may hold values from -28 to 28
- obs_var: float32 [28672], P(('col', 'row')), may hold values from 0.5 to 2
- basins: int32 [28672], P(('col', 'row')), may hold values from 0 to 15
- taper_mask: int32 [256, 256], replicated, may hold values from 0 to 1, as said below
Outputs:
- solution_field: float32 [28672, 256], P(('col', 'row'))
- residual: float32 [28672, 256], P(('col', 'row'))
The draws below stay inside these ranges and needn't reach their ends.
Inputs may be any that keep to these rules, and one draw needn't show every extreme that they name: taper_mask is symmetric with ones on its diagonal, and its ones join the blocks into groups: where blocks a, b and blocks b, c are kept, so are a, c.
All inputs are finite; a program needn't handle non-finite values.
Results may differ from the reference program's by a relative error of at most 0.0003.
Values sent between devices are 32-bit elements; how exact they have to be, the bound alone decides.
No kernel may reach another device: no remote copies, remote signals or barrier semaphores. Data moves between devices by JAX's collectives and lax.ppermute only.
A program may use at most 128 MiB of HBM per device.

```python
import math
import jax
import jax.numpy as jnp
from jax import lax

M = 256
BLK = 112
GROUPS = 4
BASINS = 16
ITERS = 3
BLOCKS = 256
GAUGES = 28672


def draw_innovations(key, part):
    key = jax.random.fold_in(key, 11)
    first, second = jax.random.split(key, 2)
    place = jnp.arange(GAUGES, dtype=jnp.float32) / (GAUGES - 1)
    rough = jax.random.uniform(first, (GAUGES,), jnp.float32)
    scale = jnp.exp(jnp.log(3.0) * (place - 0.5) + jnp.log(10.0) * (rough - 0.5))
    values = jnp.clip(jax.random.normal(second, (GAUGES, M), jnp.float32), -5.0, 5.0)
    return values * scale[:, None]


def draw_taper_mask(key, part):
    key = jax.random.fold_in(key, 5)
    group = jax.random.randint(key, (BLOCKS,), 0, GROUPS)
    return (group[:, None] == group[None, :]).astype(jnp.int32)


def touch_ends(values, rng, low, top_value):
    dims = values.shape
    index_at = [jax.random.randint(jax.random.fold_in(rng, axis), (), 0, dims[axis]) for axis in range(len(dims))]
    values = values.at[tuple(index_at)].set(low)
    longest = dims.index(max(dims))
    index_at[longest] = (index_at[longest] + 1) % dims[longest]
    return values.at[tuple(index_at)].set(top_value)


def block_scale(stream_key, extent, shards, least, top_value):
    level, own = 1.0, jax.random.fold_in(stream_key, 6)
    for position, shards_of in shards:
        heights = jnp.exp(jax.random.uniform(jax.random.fold_in(own, position), (shards_of,), jnp.float32, least / len(shards), top_value / len(shards)))
        level = level * jnp.repeat(heights, extent[position] // shards_of).reshape([-1 if axis == position else 1 for axis in range(len(extent))])
    return level


def scatter_about(stream_key, shape, scale, most, cuts=(), kind=jnp.bfloat16):
    loudness = block_scale(stream_key, shape, cuts, -0.22, 0.18) if cuts else 1.0
    drawn = jax.random.normal(stream_key, shape, jnp.float32) * scale * loudness
    return jnp.minimum(jnp.maximum(drawn, -most), most).astype(kind)


def setup_inputs(seed: int = 0) -> dict:
    streams_of = jax.random.split(jax.random.key(seed), 6)
    anomalies = scatter_about(streams_of[0], (GAUGES, M), 1.0, 6.0, ((0, 256),), jnp.float32)
    innovations = draw_innovations(jax.random.fold_in(streams_of[5], 71), 0)
    obs_var = jnp.clip(jnp.exp(math.log(2.0) - 1.3862944 * jax.random.uniform(streams_of[2], (GAUGES,), jnp.float32) ** block_scale(streams_of[2], (GAUGES,), ((0, 256),), -0.2, 0.2)), 0.5, 2.0)
    basins = touch_ends(jax.random.randint(streams_of[3], (GAUGES,), 0, BASINS), jax.random.fold_in(streams_of[3], 1), 0, BASINS - 1).astype(jnp.int32)
    taper_mask = draw_taper_mask(jax.random.fold_in(streams_of[5], 71), 0)
    return {"anomalies": anomalies, "innovations": innovations, "obs_var": obs_var, "basins": basins, "taper_mask": taper_mask}


far_weight = 0.3


def operate(field, anomalies, basins, taper_mask, obs_var):
    gauges = anomalies.shape[0]
    members = anomalies.shape[1]
    rows = math.gcd(gauges, 512)
    block_of = jnp.arange(gauges, dtype=jnp.int32) // BLK

    def one_block(index):
        start = (index * rows).astype(jnp.int32)
        part = lax.dynamic_slice_in_dim(anomalies, start, rows, 0)
        gram = lax.dot_general(part, anomalies, (((1,), (1,)), ((), ())), precision=lax.Precision.HIGHEST, preferred_element_type=jnp.float32) / (members - 1)
        near = jnp.take(taper_mask, lax.dynamic_slice_in_dim(block_of, start, rows, 0), axis=0)
        own = lax.dynamic_slice_in_dim(basins, start, rows, 0)
        weight = jnp.where(own[:, None] == basins[None, :], 1.0, far_weight).astype(jnp.float32)
        tile = (gram * weight).reshape(rows, BLOCKS, BLK) * near.astype(jnp.float32)[:, :, None]
        return jnp.dot(tile.reshape(rows, gauges), field, precision=lax.Precision.HIGHEST, preferred_element_type=jnp.float32)

    image = lax.map(one_block, jnp.arange(gauges // rows, dtype=jnp.int32)).reshape(gauges, members)
    return image + obs_var[:, None] * field


def reference(anomalies, innovations, obs_var, basins, taper_mask):
    solution_field = jnp.zeros_like(innovations)
    residual = innovations
    direction = innovations
    norm_now = jnp.sum(residual * residual, axis=0)
    for step in range(ITERS):
        image = operate(direction, anomalies, basins, taper_mask, obs_var)
        alpha = norm_now / jnp.sum(direction * image, axis=0)
        solution_field = solution_field + alpha * direction
        residual = residual - alpha * image
        norm_next = jnp.sum(residual * residual, axis=0)
        direction = residual + (norm_next / norm_now) * direction
        norm_now = norm_next
    return solution_field, residual
```

```python
import functools

import jax
import jax.numpy as jnp
from jax import lax
from jax.experimental import pallas as pl
from jax.experimental.pallas import tpu as pltpu
from jax.sharding import Mesh
from jax.sharding import PartitionSpec as P

ITERS = 3
BASINS = 16
GROUPS = 4
far_weight = 0.3

LANES = 128
PEERS = ("y", "z")
NT = (((1,), (1,)), ((), ()))


def split(v):
    high = v.astype(jnp.bfloat16)
    return high, (v - high.astype(jnp.float32)).astype(jnp.bfloat16)


def block_of(anom_ref, b):
    high, low = split(anom_ref[b])
    rest = jnp.zeros((LANES - high.shape[0], high.shape[1]), jnp.bfloat16)
    return jnp.concatenate([high, rest], 0), jnp.concatenate([low, rest], 0)


def same_basin(pay_ref, b):
    basin = pay_ref[b, 9:10, :][None]
    ids = lax.broadcasted_iota(jnp.int32, (BASINS, 8, LANES), 0).astype(jnp.float32)
    return ids == basin


def project(pos_ref, gid_ref, anom_ref, pay_ref, field, sums, acc, keep_ref, send_ref):
    blocks = anom_ref.shape[0]
    acc[...] = jnp.zeros_like(acc)

    def body(b, carry):
        spread = jnp.where(same_basin(pay_ref, b), field(b)[None], 0.0)
        high, low = split(spread.reshape(BASINS * 8, LANES))
        a_high, a_low = block_of(anom_ref, b)
        both = jnp.dot(
            jnp.concatenate([high, low], 0), a_high, preferred_element_type=jnp.float32
        )
        third = jnp.dot(high, a_low, preferred_element_type=jnp.float32)
        total = both[: BASINS * 8] + both[BASINS * 8 :] + third
        g = gid_ref[b]
        acc[g] = acc[g] + total.reshape(acc.shape[1:])
        return carry

    lax.fori_loop(0, blocks, body, 0, unroll=4)
    half = acc.shape[2]
    lane = lax.broadcasted_iota(jnp.int32, (8, acc.shape[3]), 1)
    row = jnp.zeros((8, acc.shape[3]), jnp.float32)
    for place, value in enumerate(sums):
        row = jnp.where(lane == place, jnp.sum(value, axis=1, keepdims=True), row)
    me_x, me_c = pos_ref[0], pos_ref[1]
    for k in range(GROUPS):
        g = lax.rem(me_x + k, GROUPS)
        keep_ref[k, :half] = acc[g, me_c]
        send_ref[k, :half] = acc[g, 1 - me_c]
        keep_ref[k, half:] = row
        send_ref[k, half:] = row


def first_kernel(pos_ref, gid_ref, anom_ref, pay_ref, keep_ref, send_ref, acc):
    blocks = anom_ref.shape[0]

    def body(b, carry):
        r, obs = pay_ref[b, 0:8, :], pay_ref[b, 8:9, :]
        return carry[0] + r * r, carry[1] + r * r * obs

    zero = jnp.zeros((8, LANES), jnp.float32)
    sums = lax.fori_loop(0, blocks, body, (zero, zero), unroll=4)
    project(
        pos_ref, gid_ref, anom_ref, pay_ref, lambda b: pay_ref[b, 0:8, :], sums, acc,
        keep_ref, send_ref,
    )


def step_kernel(members, first, last, *refs):
    refs = list(refs)
    pos_ref, gid_ref, anom_ref, pay_ref, own_ref, other_ref = refs[:6]
    del refs[:6]
    if not first:
        x_in, r_in, d_in, dir_in, scal_in = refs[:5]
        del refs[:5]
    if last:
        out_ref = refs.pop(0)
    else:
        x_out, r_out, d_out, dir_out, scal_out, keep_ref, send_ref = refs[:7]
        del refs[:7]
    e_high, e_low = refs[:2]
    if last:
        dir_sum = refs[2]
    else:
        dir_sum, acc = dir_out, refs[2]
    blocks = anom_ref.shape[0]
    wide = anom_ref.shape[2]
    half = BASINS // 2 * 8
    me_x, me_c = pos_ref[0], pos_ref[1]

    row = own_ref[0, half:]
    rr, r_obs_r, r_obs_d = row[:, 0:1], row[:, 1:2], row[:, 2:3]
    if first:
        beta = jnp.zeros_like(rr)
        d_obs_d = r_obs_r
    else:
        beta = rr / scal_in[:, 0:1]
        d_obs_d = r_obs_r + 2.0 * beta * r_obs_d + beta * beta * scal_in[:, 1:2]
    for k in range(GROUPS):
        g = lax.rem(me_x - k + GROUPS, GROUPS)
        mine, theirs = own_ref[k, :half], other_ref[k, :half]
        if not first:
            mine = (mine.reshape(-1, 8, wide) + beta[None] * dir_in[g, me_c].reshape(-1, 8, wide)).reshape(half, wide)
            theirs = (theirs.reshape(-1, 8, wide) + beta[None] * dir_in[g, 1 - me_c].reshape(-1, 8, wide)).reshape(half, wide)
        dir_sum[g, me_c] = mine
        dir_sum[g, 1 - me_c] = theirs
    curve = jnp.zeros((8, wide), jnp.float32)
    for g in range(GROUPS):
        d_g = dir_sum[g].reshape(BASINS, 8, wide)
        every = jnp.sum(d_g, axis=0)
        e_g = ((1.0 - far_weight) / (members - 1)) * d_g + (far_weight / (members - 1)) * every[None]
        curve = curve + jnp.sum(d_g * e_g, axis=0)
        high, low = split(e_g.reshape(BASINS * 8, wide))
        e_high[g] = high
        e_low[g] = low
    alpha = rr / (jnp.sum(curve, axis=1, keepdims=True) + d_obs_d)

    def body(b, carry):
        g = gid_ref[b]
        a_high, a_low = block_of(anom_ref, b)
        both = lax.dot_general(
            jnp.concatenate([e_high[g], e_low[g]], 0), a_high, NT,
            preferred_element_type=jnp.float32,
        )
        third = lax.dot_general(e_high[g], a_low, NT, preferred_element_type=jnp.float32)
        rows = BASINS * 8
        every = (both[:rows] + both[rows:] + third).reshape(BASINS, 8, LANES)
        image = jnp.sum(jnp.where(same_basin(pay_ref, b), every, 0.0), axis=0)
        obs = pay_ref[b, 8:9, :]
        if first:
            r = pay_ref[b, 0:8, :]
            d = r
        else:
            r = r_in[b]
            d = r + beta * d_in[b]
        image = image + obs * d
        x = alpha * d
        if not first:
            x = x_in[b] + x
        r = r - alpha * image
        if last:
            out_ref[b, 0:8] = x
            out_ref[b, 8:16] = r
            return carry
        x_out[b] = x
        r_out[b] = r
        d_out[b] = d
        return carry[0] + r * r, carry[1] + r * r * obs, carry[2] + r * d * obs

    if last:
        lax.fori_loop(0, blocks, body, 0, unroll=4)
        return
    zero = jnp.zeros((8, LANES), jnp.float32)
    sums = lax.fori_loop(0, blocks, body, (zero, zero, zero), unroll=4)
    lane = lax.broadcasted_iota(jnp.int32, (8, LANES), 1)
    scal_out[...] = jnp.where(lane == 0, rr, d_obs_d)
    project(
        pos_ref, gid_ref, anom_ref, pay_ref, lambda b: r_out[b], sums, acc, keep_ref, send_ref
    )


def shift(v, k):
    n = lax.axis_size("x")
    return lax.ppermute(v, "x", [(i, (i + k) % n) for i in range(n)])


def swap(v):
    return lax.ppermute(v, "c", [(0, 1), (1, 0)])


def total_over_gauges(keep, send):
    part = keep + swap(send)
    moved = [shift(part[k], k) for k in range(1, GROUPS)]
    mine = part[0] + moved[0] + moved[1] + moved[2]
    own = jnp.stack([mine] + [shift(mine, k) for k in range(1, GROUPS)])
    return own, swap(own)


def local(anomalies, innovations, obs_var, basins, taper_mask):
    blk, members = anomalies.shape
    peers = lax.axis_size("y") * lax.axis_size("z")
    me_x, me_c = lax.axis_index("x"), lax.axis_index("c")
    nx, ny, nc, nz = (lax.axis_size(a) for a in ("x", "y", "c", "z"))
    nblocks = taper_mask.shape[0]

    near = taper_mask != 0
    place = jnp.arange(nblocks, dtype=jnp.int32)
    leader = jnp.min(jnp.where(near, place[None, :], nblocks), axis=1)
    leads = (leader == place)[None, :] & (place[None, :] < leader[:, None])
    gid = jnp.sum(leads.astype(jnp.int32), axis=1)
    gid = gid.reshape(nx, ny, nc, nz)
    gid = lax.dynamic_slice(gid, (me_x, 0, me_c, 0), (1, ny, 1, nz)).reshape(peers)
    gid = jnp.minimum(gid, GROUPS - 1)
    pos = jnp.stack([me_x, me_c]).astype(jnp.int32)

    lanes = ((0, 0), (0, LANES - blk))
    each = members // peers
    field = jnp.pad(innovations.T, lanes).reshape(peers, each, LANES)
    extra = jnp.pad(jnp.stack([obs_var, basins.astype(jnp.float32)]), ((0, 6), (0, LANES - blk)))
    pay = jnp.concatenate([field, jnp.broadcast_to(extra[None], (peers, 8, LANES))], 1)
    pay = lax.all_to_all(pay, PEERS, 0, 0, tiled=True)
    anoms = lax.all_gather(anomalies, PEERS, axis=0, tiled=False)

    smem = pl.BlockSpec(memory_space=pltpu.SMEM)
    vmem = pl.BlockSpec(memory_space=pltpu.VMEM)
    f32 = functools.partial(jax.ShapeDtypeStruct, dtype=jnp.float32)
    half = BASINS // 2 * each
    shard = f32((GROUPS, half + each, members))
    state = f32((peers, each, LANES))
    sums = (GROUPS, 2, half, members)
    params = pltpu.CompilerParams(vmem_limit_bytes=48 * 2**20)
    common = (pos, gid, anoms, pay)

    keep, send = pl.pallas_call(
        first_kernel,
        out_shape=(shard, shard),
        in_specs=[smem, smem, vmem, vmem],
        out_specs=(vmem, vmem),
        scratch_shapes=[pltpu.VMEM(sums, jnp.float32)],
        compiler_params=params,
        name="project",
    )(*common)
    carried = ()
    for step in range(ITERS):
        first, last = step == 0, step + 1 == ITERS
        own, other = total_over_gauges(keep, send)
        args = (*common, own, other, *carried)
        if last:
            shapes = f32((peers, 2 * each, LANES))
        else:
            shapes = (state, state, state, f32(sums), f32((each, LANES)), shard, shard)
        out = pl.pallas_call(
            functools.partial(step_kernel, members, first, last),
            out_shape=shapes,
            in_specs=[smem, smem] + [vmem] * (len(args) - 2),
            out_specs=vmem if last else (vmem,) * len(shapes),
            scratch_shapes=[
                pltpu.VMEM((GROUPS, BASINS * each, members), jnp.bfloat16),
                pltpu.VMEM((GROUPS, BASINS * each, members), jnp.bfloat16),
                pltpu.VMEM(sums, jnp.float32),
            ],
            compiler_params=params,
            name="finish" if last else "step",
        )(*args)
        if not last:
            carried, (keep, send) = out[:5], out[5:]
    back = lax.all_to_all(out, PEERS, 0, 0, tiled=True)
    solution_field = back[:, :each, :blk].reshape(members, blk).T
    residual = back[:, each:, :blk].reshape(members, blk).T
    return solution_field, residual


def solution(mesh):
    fine = Mesh(mesh.devices.reshape(8, 4, 4, 2), ("z", "x", "y", "c"))
    split_all = ("x", "y", "c", "z")
    placed = (P(split_all, None), P(split_all, None), P(split_all), P(split_all), P())
    return jax.shard_map(
        local,
        mesh=fine,
        in_specs=placed,
        out_specs=(P(split_all, None), P(split_all, None)),
        check_vma=False,
    )
```

```python
import functools

import jax
import jax.numpy as jnp
from jax import lax
from jax.experimental import pallas as pl
from jax.experimental.pallas import tpu as pltpu
from jax.sharding import Mesh
from jax.sharding import PartitionSpec as P

ITERS = 3
BASINS = 16
GROUPS = 4
far_weight = 0.3

LANES = 128
PEERS = ("y", "z")
FIRST_ROWS = 64
UNROLL = 6
NT = (((1,), (1,)), ((), ()))


def split(v):
    high = v.astype(jnp.bfloat16)
    return high, (v - high.astype(jnp.float32)).astype(jnp.bfloat16)


def pair(ref, p, rows=slice(None)):
    return jnp.concatenate([ref[2 * p, rows], ref[2 * p + 1, rows]], 1)


def same_basin(gauge_ref, p):
    basin = pair(gauge_ref, p, slice(9, 10))[None]
    ids = lax.broadcasted_iota(jnp.int32, (BASINS, 8, 2 * LANES), 0).astype(jnp.float32)
    return ids == basin


def project(pos_ref, tab_ref, anom_ref, gauge_ref, field, sums, acc, keep_ref, send_ref):
    pairs = anom_ref.shape[0]
    acc[...] = jnp.zeros_like(acc)

    def body(p, carry):
        spread = jnp.where(same_basin(gauge_ref, p), field(p)[None], 0.0)
        high, low = split(spread.reshape(BASINS * 8, 2 * LANES))
        total = jnp.dot(
            jnp.concatenate([high, high], 1), anom_ref[p], preferred_element_type=jnp.float32
        ) + jnp.dot(low, anom_ref[p, : 2 * LANES], preferred_element_type=jnp.float32)
        g = tab_ref[p]
        acc[g] = acc[g] + total.reshape(acc.shape[1:])
        return carry

    lax.fori_loop(0, pairs, body, 0, unroll=UNROLL)
    half = acc.shape[2]
    lane = lax.broadcasted_iota(jnp.int32, (8, acc.shape[3]), 1)
    row = jnp.zeros((8, acc.shape[3]), jnp.float32)
    for place, value in enumerate(sums):
        row = jnp.where(lane == place, jnp.sum(value, axis=1, keepdims=True), row)
    me_x, me_c = pos_ref[0], pos_ref[1]
    for k in range(GROUPS):
        g = lax.rem(me_x + k, GROUPS)
        keep_ref[k, :half] = acc[g, me_c]
        send_ref[k, :half] = acc[g, 1 - me_c]
        keep_ref[k, half:] = row
        send_ref[k, half:] = row


def first_kernel(
    pos_ref, gid_ref, pay_ref, near_ref, own_ref, below_ref, above_ref, low_ref, high_ref,
    tab_ref, anom_ref, gauge_ref, keep_ref, send_ref, count, acc,
):
    blocks = pay_ref.shape[0]
    slots = gauge_ref.shape[0]
    pairs = slots // 2
    nz = own_ref.shape[0]
    ny = blocks // nz

    for g in range(GROUPS):
        count[g] = 0

    def tally(b, carry):
        g = gid_ref[b]
        count[g] = count[g] + 1
        return carry

    lax.fori_loop(0, blocks, tally, 0, unroll=4)
    start = jnp.int32(0)
    spare = jnp.int32(0)
    for p in range(pairs):
        tab_ref[p] = 0
    empty = []
    for g in range(GROUPS):
        n = count[g]
        count[g] = 2 * start

        def mark(p, carry, g=g):
            tab_ref[p] = g
            return carry

        end = start + lax.div(n + 1, 2)
        lax.fori_loop(start, end, mark, 0)
        odd = lax.rem(n, 2)
        empty.append((odd == 1, 2 * end - 1))
        start = end

    def assign(b, carry):
        g = gid_ref[b]
        s = count[g]
        count[g] = s + 1
        tab_ref[pairs + b] = s
        gauge_ref[s] = pay_ref[b]
        return carry

    lax.fori_loop(0, blocks, assign, 0, unroll=4)

    def put(s, value):
        high, low = split(value)
        p, h = lax.div(s, 2), lax.rem(s, 2)
        anom_ref[p, pl.ds(pl.multiple_of(h * LANES, LANES), LANES)] = high
        anom_ref[p, pl.ds(pl.multiple_of((2 + h) * LANES, LANES), LANES)] = low

    blank = jnp.zeros((LANES, anom_ref.shape[2]), jnp.float32)

    def clear(s):
        put(s, blank)
        gauge_ref[s] = jnp.zeros(gauge_ref.shape[1:], jnp.float32)

    for odd, s in empty:
        pl.when(odd)(functools.partial(clear, s))

    def clear_slot(s, carry):
        clear(s)
        return carry

    lax.fori_loop(2 * start, slots, clear_slot, 0)

    me_y = pos_ref[2]
    rest = jnp.zeros((LANES - near_ref.shape[2] - own_ref.shape[1], near_ref.shape[3]), jnp.float32)
    for k, ref in ((0, own_ref), (ny - 1, below_ref), (1, above_ref), (2, None)):
        y = lax.rem(me_y + k, ny)
        for z in range(nz):
            if ref is not None:
                tail = ref[z]
            elif z < nz // 2:
                tail = low_ref[z]
            else:
                tail = high_ref[z - nz // 2]
            put(
                tab_ref[pairs + y * nz + z],
                jnp.concatenate([near_ref[z, y], tail, rest], 0),
            )

    zero = jnp.zeros((8, 2 * LANES), jnp.float32)
    one, two = zero, zero
    for p in range(pairs):
        r, obs = pair(gauge_ref, p, slice(0, 8)), pair(gauge_ref, p, slice(8, 9))
        one, two = one + r * r, two + r * r * obs
    project(
        pos_ref, tab_ref, anom_ref, gauge_ref, lambda p: pair(gauge_ref, p, slice(0, 8)),
        (one, two), acc, keep_ref, send_ref,
    )


def step_kernel(members, first, last, *refs):
    refs = list(refs)
    pos_ref, tab_ref, anom_ref, gauge_ref, own_ref, other_ref = refs[:6]
    del refs[:6]
    if not first:
        x_in, r_in, d_in, dir_in, scal_in = refs[:5]
        del refs[:5]
    if last:
        out_ref = refs.pop(0)
        e_high, e_low, dir_sum, result = refs
    else:
        x_out, r_out, dir_out, scal_out, keep_ref, send_ref = refs[:6]
        d_out = None if first else refs[6]
        e_high, e_low, acc = refs[-3:]
        dir_sum = dir_out
    pairs = anom_ref.shape[0]
    wide = anom_ref.shape[2]
    rows = BASINS * 8
    half = rows // 2
    me_x, me_c = pos_ref[0], pos_ref[1]

    row = own_ref[0, half:]
    rr, r_obs_r, r_obs_d = row[:, 0:1], row[:, 1:2], row[:, 2:3]
    if first:
        d_obs_d = r_obs_r
    else:
        beta = rr / scal_in[:, 0:1]
        d_obs_d = r_obs_r + 2.0 * beta * r_obs_d + beta * beta * scal_in[:, 1:2]

    def advance(new, old):
        if first:
            return new
        mixed = new.reshape(-1, 8, wide) + beta[None] * old().reshape(-1, 8, wide)
        return mixed.reshape(half, wide)

    for k in range(GROUPS):
        g = lax.rem(me_x - k + GROUPS, GROUPS)
        dir_sum[g, me_c] = advance(own_ref[k, :half], lambda: dir_in[g, me_c])
        dir_sum[g, 1 - me_c] = advance(other_ref[k, :half], lambda: dir_in[g, 1 - me_c])
    curve = jnp.zeros((8, wide), jnp.float32)
    for g in range(GROUPS):
        d_g = dir_sum[g].reshape(BASINS, 8, wide)
        every = jnp.sum(d_g, axis=0)
        e_g = ((1.0 - far_weight) / (members - 1)) * d_g + (far_weight / (members - 1)) * every[None]
        curve = curve + jnp.sum(d_g * e_g, axis=0)
        high, low = split(e_g.reshape(rows, wide))
        e_high[g] = high
        e_low[g] = low
    alpha = rr / (jnp.sum(curve, axis=1, keepdims=True) + d_obs_d)

    def body(p, carry):
        g = tab_ref[p]
        both = lax.dot_general(
            jnp.concatenate([e_high[g], e_low[g]], 0), anom_ref[p, : 2 * LANES], NT,
            preferred_element_type=jnp.float32,
        )
        third = lax.dot_general(
            e_high[g], anom_ref[p, 2 * LANES :], NT, preferred_element_type=jnp.float32
        )
        every = (both[:rows] + both[rows:] + third).reshape(BASINS, 8, 2 * LANES)
        image = jnp.sum(jnp.where(same_basin(gauge_ref, p), every, 0.0), axis=0)
        obs = pair(gauge_ref, p, slice(8, 9))
        if first:
            r = pair(gauge_ref, p, slice(0, 8))
            d = r
        else:
            r = r_in[p]
            d = r + beta * (pair(d_in, p, slice(0, 8)) if d_in.shape[0] == 2 * pairs else d_in[p])
        image = image + obs * d
        x = alpha * d
        if not first:
            x = x_in[p] + x
        r = r - alpha * image
        if last:
            for h in range(2):
                result[2 * p + h, 0:8] = x[:, h * LANES : (h + 1) * LANES]
                result[2 * p + h, 8:16] = r[:, h * LANES : (h + 1) * LANES]
            return carry
        x_out[p] = x
        r_out[p] = r
        if d_out is not None:
            d_out[p] = d
        return carry[0] + r * r, carry[1] + r * r * obs, carry[2] + r * d * obs

    if last:
        lax.fori_loop(0, pairs, body, 0, unroll=UNROLL)
        for b in range(out_ref.shape[0]):
            out_ref[b] = result[tab_ref[pairs + b]]
        return
    zero = jnp.zeros((8, 2 * LANES), jnp.float32)
    sums = lax.fori_loop(0, pairs, body, (zero, zero, zero), unroll=UNROLL)
    lane = lax.broadcasted_iota(jnp.int32, (8, LANES), 1)
    scal_out[...] = jnp.where(lane == 0, rr, d_obs_d)
    project(
        pos_ref, tab_ref, anom_ref, gauge_ref, lambda p: r_out[p], sums, acc, keep_ref, send_ref
    )


def shift(v, axis, k):
    n = lax.axis_size(axis)
    return lax.ppermute(v, axis, [(i, (i + k) % n) for i in range(n)])


def swap(v):
    return lax.ppermute(v, "c", [(0, 1), (1, 0)])


def total_over_gauges(keep, send):
    part = keep + swap(send)
    moved = [shift(part[k], "x", k) for k in range(1, GROUPS)]
    mine = part[0] + moved[0] + moved[1] + moved[2]
    own = jnp.stack([mine] + [shift(mine, "x", k) for k in range(1, GROUPS)])
    return own, swap(own)


def to_all(v, axis):
    n = lax.axis_size(axis)
    return lax.all_to_all(jnp.broadcast_to(v[None], (n,) + v.shape), axis, 0, 0, tiled=True)


def gather(anomalies):
    near = lax.all_gather(to_all(anomalies[:FIRST_ROWS], "y"), "z", axis=0, tiled=False)
    own = to_all(anomalies[FIRST_ROWS:], "z")
    below, above = shift(own, "y", 1), shift(own, "y", -1)
    half = own.shape[0] // 2
    return near, own, below, above, shift(below[:half], "y", 1), shift(above[half:], "y", -1)


def local(anomalies, innovations, obs_var, basins, taper_mask):
    blk, members = anomalies.shape
    peers = lax.axis_size("y") * lax.axis_size("z")
    me_x, me_c = lax.axis_index("x"), lax.axis_index("c")
    nx, ny, nc, nz = (lax.axis_size(a) for a in ("x", "y", "c", "z"))
    nblocks = taper_mask.shape[0]

    near = taper_mask != 0
    place = jnp.arange(nblocks, dtype=jnp.int32)
    leader = jnp.min(jnp.where(near, place[None, :], nblocks), axis=1)
    leads = (leader == place)[None, :] & (place[None, :] < leader[:, None])
    gid = jnp.sum(leads.astype(jnp.int32), axis=1)
    gid = gid.reshape(nx, ny, nc, nz)
    gid = lax.dynamic_slice(gid, (me_x, 0, me_c, 0), (1, ny, 1, nz)).reshape(peers)
    gid = jnp.minimum(gid, GROUPS - 1)
    pos = jnp.stack([me_x, me_c, lax.axis_index("y")]).astype(jnp.int32)

    pieces = gather(anomalies)
    lanes = ((0, 0), (0, LANES - blk))
    each = members // peers
    field = jnp.pad(innovations.T, lanes).reshape(peers, each, LANES)
    extra = jnp.pad(jnp.stack([obs_var, basins.astype(jnp.float32)]), ((0, 6), (0, LANES - blk)))
    pay = jnp.concatenate([field, jnp.broadcast_to(extra[None], (peers, 8, LANES))], 1)
    pay = lax.all_to_all(pay, PEERS, 0, 0, tiled=True)

    smem = pl.BlockSpec(memory_space=pltpu.SMEM)
    vmem = pl.BlockSpec(memory_space=pltpu.VMEM)
    f32 = functools.partial(jax.ShapeDtypeStruct, dtype=jnp.float32)
    half = BASINS // 2 * each
    pairs = (peers + GROUPS) // 2
    shard = f32((GROUPS, half + each, members))
    state = f32((pairs, each, 2 * LANES))
    sums = (GROUPS, 2, half, members)
    params = pltpu.CompilerParams(vmem_limit_bytes=48 * 2**20)

    tab, anoms, gauges, keep, send = pl.pallas_call(
        first_kernel,
        out_shape=(
            jax.ShapeDtypeStruct((pairs + peers,), jnp.int32),
            jax.ShapeDtypeStruct((pairs, 4 * LANES, members), jnp.bfloat16),
            f32((2 * pairs, 2 * each, LANES)),
            shard,
            shard,
        ),
        in_specs=[smem, smem] + [vmem] * 7,
        out_specs=(smem, vmem, vmem, vmem, vmem),
        scratch_shapes=[pltpu.SMEM((GROUPS,), jnp.int32), pltpu.VMEM(sums, jnp.float32)],
        compiler_params=params,
        name="project",
    )(pos, gid, pay, *pieces)
    common = (pos, tab, anoms, gauges)
    carried = ()
    for step in range(ITERS):
        first, last = step == 0, step + 1 == ITERS
        own, other = total_over_gauges(keep, send)
        args = (*common, own, other, *carried)
        if last:
            shapes = f32((peers, 2 * each, LANES))
            extra_scratch = [pltpu.VMEM((2 * pairs, 2 * each, LANES), jnp.float32)]
        else:
            shapes = (state, state, f32(sums), f32((each, LANES)), shard, shard)
            shapes = shapes if first else shapes + (state,)
            extra_scratch = []
        out = pl.pallas_call(
            functools.partial(step_kernel, members, first, last),
            out_shape=shapes,
            in_specs=[smem, smem] + [vmem] * (len(args) - 2),
            out_specs=vmem if last else (vmem,) * len(shapes),
            scratch_shapes=[
                pltpu.VMEM((GROUPS, BASINS * each, members), jnp.bfloat16),
                pltpu.VMEM((GROUPS, BASINS * each, members), jnp.bfloat16),
                pltpu.VMEM(sums, jnp.float32),
            ] + extra_scratch,
            compiler_params=params,
            name="finish" if last else "step",
        )(*args)
        if not last:
            x, r, dir_sum, scal, keep, send = out[:6]
            carried = (x, r, gauges if first else out[6], dir_sum, scal)
    back = lax.all_to_all(out, PEERS, 0, 0, tiled=True)
    solution_field = back[:, :each, :blk].reshape(members, blk).T
    residual = back[:, each:, :blk].reshape(members, blk).T
    return solution_field, residual


def solution(mesh):
    fine = Mesh(mesh.devices.reshape(8, 4, 4, 2), ("z", "x", "y", "c"))
    split_all = ("x", "y", "c", "z")
    placed = (P(split_all, None), P(split_all, None), P(split_all), P(split_all), P())
    return jax.shard_map(
        local,
        mesh=fine,
        in_specs=placed,
        out_specs=(P(split_all, None), P(split_all, None)),
        check_vma=False,
    )
```

```python
import functools

import jax
import jax.numpy as jnp
from jax import lax
from jax.experimental import pallas as pl
from jax.experimental.pallas import tpu as pltpu
from jax.sharding import Mesh
from jax.sharding import PartitionSpec as P

ITERS = 3
BASINS = 16
GROUPS = 4
far_weight = 0.3

LANES = 128
PEERS = ("y", "z")
FIRST_ROWS = 64
UNROLL = 6
NT = (((1,), (1,)), ((), ()))


def split(v):
    high = v.astype(jnp.bfloat16)
    return high, (v - high.astype(jnp.float32)).astype(jnp.bfloat16)


def pair(ref, p, rows=slice(None)):
    return jnp.concatenate([ref[2 * p, rows], ref[2 * p + 1, rows]], 1)


def same_basin(gauge_ref, p):
    basin = pair(gauge_ref, p, slice(9, 10))[None]
    ids = lax.broadcasted_iota(jnp.int32, (BASINS, 8, 2 * LANES), 0).astype(jnp.float32)
    return ids == basin


def project(pos_ref, tab_ref, anom_ref, gauge_ref, field, sums, acc, outs):
    pairs = anom_ref.shape[0]
    acc[...] = jnp.zeros_like(acc)

    def body(p, carry):
        spread = jnp.where(same_basin(gauge_ref, p), field(p)[None], 0.0)
        high, low = split(spread.reshape(BASINS * 8, 2 * LANES))
        total = jnp.dot(
            jnp.concatenate([high, high], 1), anom_ref[p], preferred_element_type=jnp.float32
        ) + jnp.dot(low, anom_ref[p, : 2 * LANES], preferred_element_type=jnp.float32)
        g = tab_ref[p]
        acc[g] = acc[g] + total.reshape(acc.shape[1:])
        return carry

    lax.fori_loop(0, pairs, body, 0, unroll=UNROLL)
    half = acc.shape[2]
    lane = lax.broadcasted_iota(jnp.int32, (8, acc.shape[3]), 1)
    row = jnp.zeros((8, acc.shape[3]), jnp.float32)
    for place, value in enumerate(sums):
        row = jnp.where(lane == place, jnp.sum(value, axis=1, keepdims=True), row)
    me_c = pos_ref[0]
    for side in range(2):
        core = me_c if side == 0 else 1 - me_c
        for g in range(GROUPS):
            out = outs[2 * side + g // 2]
            out[(g % 2) * half : (g % 2 + 1) * half] = acc[g, core]
        outs[2 * side][2 * half :] = row


def first_kernel(
    pos_ref, gid_ref, pay_ref, own_0, below_0, above_0, far_0, own_1, below_1, above_1, far_1,
    tab_ref, anom_ref, gauge_ref, keep_0, keep_1, send_0, send_1, count, acc,
):
    blocks = pay_ref.shape[0]
    slots = gauge_ref.shape[0]
    pairs = slots // 2
    nz = own_0.shape[0]
    ny = blocks // nz

    for g in range(GROUPS):
        count[g] = 0

    def tally(b, carry):
        g = gid_ref[b]
        count[g] = count[g] + 1
        return carry

    lax.fori_loop(0, blocks, tally, 0, unroll=4)
    start = jnp.int32(0)
    spare = jnp.int32(0)
    for p in range(pairs):
        tab_ref[p] = 0
    empty = []
    for g in range(GROUPS):
        n = count[g]
        count[g] = 2 * start

        def mark(p, carry, g=g):
            tab_ref[p] = g
            return carry

        end = start + lax.div(n + 1, 2)
        lax.fori_loop(start, end, mark, 0)
        odd = lax.rem(n, 2)
        empty.append((odd == 1, 2 * end - 1))
        start = end

    def assign(b, carry):
        g = gid_ref[b]
        s = count[g]
        count[g] = s + 1
        tab_ref[pairs + b] = s
        gauge_ref[s] = pay_ref[b]
        return carry

    lax.fori_loop(0, blocks, assign, 0, unroll=4)

    def put(s, value):
        high, low = split(value)
        p, h = lax.div(s, 2), lax.rem(s, 2)
        anom_ref[p, pl.ds(pl.multiple_of(h * LANES, LANES), LANES)] = high
        anom_ref[p, pl.ds(pl.multiple_of((2 + h) * LANES, LANES), LANES)] = low

    blank = jnp.zeros((LANES, anom_ref.shape[2]), jnp.float32)

    def clear(s):
        put(s, blank)
        gauge_ref[s] = jnp.zeros(gauge_ref.shape[1:], jnp.float32)

    for odd, s in empty:
        pl.when(odd)(functools.partial(clear, s))

    def clear_slot(s, carry):
        clear(s)
        return carry

    lax.fori_loop(2 * start, slots, clear_slot, 0)

    me_y = pos_ref[1]
    rest = jnp.zeros((LANES - own_0.shape[1] - own_1.shape[1], own_0.shape[2]), jnp.float32)
    for k, top, tail in (
        (0, own_0, own_1), (ny - 1, below_0, below_1), (1, above_0, above_1), (2, far_0, far_1),
    ):
        y = lax.rem(me_y + k, ny)
        for z in range(nz):
            put(tab_ref[pairs + y * nz + z], jnp.concatenate([top[z], tail[z], rest], 0))

    zero = jnp.zeros((8, 2 * LANES), jnp.float32)
    one, two = zero, zero
    for p in range(pairs):
        r, obs = pair(gauge_ref, p, slice(0, 8)), pair(gauge_ref, p, slice(8, 9))
        one, two = one + r * r, two + r * r * obs
    project(
        pos_ref, tab_ref, anom_ref, gauge_ref, lambda p: pair(gauge_ref, p, slice(0, 8)),
        (one, two), acc, (keep_0, keep_1, send_0, send_1),
    )


def step_kernel(members, first, last, *refs):
    refs = list(refs)
    pos_ref, tab_ref, anom_ref, gauge_ref, own_0, own_1, other_0, other_1 = refs[:8]
    del refs[:8]
    if not first:
        x_in, r_in, d_in, dir_in, scal_in = refs[:5]
        del refs[:5]
    if last:
        out_ref = refs.pop(0)
        e_high, e_low, dir_sum, result = refs
    else:
        x_out, r_out, dir_out, scal_out, keep_0, keep_1, send_0, send_1 = refs[:8]
        d_out = None if first else refs[8]
        e_high, e_low, acc = refs[-3:]
        dir_sum = dir_out
    pairs = anom_ref.shape[0]
    wide = anom_ref.shape[2]
    rows = BASINS * 8
    half = rows // 2
    me_c = pos_ref[0]

    row = own_0[2 * half :]
    rr, r_obs_r, r_obs_d = row[:, 0:1], row[:, 1:2], row[:, 2:3]
    if first:
        d_obs_d = r_obs_r
    else:
        beta = rr / scal_in[:, 0:1]
        d_obs_d = r_obs_r + 2.0 * beta * r_obs_d + beta * beta * scal_in[:, 1:2]

    def advance(new, old):
        if first:
            return new
        mixed = new.reshape(-1, 8, wide) + beta[None] * old().reshape(-1, 8, wide)
        return mixed.reshape(half, wide)

    for g in range(GROUPS):
        own, other = (own_0, other_0) if g < 2 else (own_1, other_1)
        part = slice(g % 2 * half, (g % 2 + 1) * half)
        dir_sum[g, me_c] = advance(own[part], lambda: dir_in[g, me_c])
        dir_sum[g, 1 - me_c] = advance(other[part], lambda: dir_in[g, 1 - me_c])
    curve = jnp.zeros((8, wide), jnp.float32)
    for g in range(GROUPS):
        d_g = dir_sum[g].reshape(BASINS, 8, wide)
        every = jnp.sum(d_g, axis=0)
        e_g = ((1.0 - far_weight) / (members - 1)) * d_g + (far_weight / (members - 1)) * every[None]
        curve = curve + jnp.sum(d_g * e_g, axis=0)
        high, low = split(e_g.reshape(rows, wide))
        e_high[g] = high
        e_low[g] = low
    alpha = rr / (jnp.sum(curve, axis=1, keepdims=True) + d_obs_d)

    def body(p, carry):
        g = tab_ref[p]
        both = lax.dot_general(
            jnp.concatenate([e_high[g], e_low[g]], 0), anom_ref[p, : 2 * LANES], NT,
            preferred_element_type=jnp.float32,
        )
        third = lax.dot_general(
            e_high[g], anom_ref[p, 2 * LANES :], NT, preferred_element_type=jnp.float32
        )
        every = (both[:rows] + both[rows:] + third).reshape(BASINS, 8, 2 * LANES)
        image = jnp.sum(jnp.where(same_basin(gauge_ref, p), every, 0.0), axis=0)
        obs = pair(gauge_ref, p, slice(8, 9))
        if first:
            r = pair(gauge_ref, p, slice(0, 8))
            d = r
        else:
            r = r_in[p]
            d = r + beta * (pair(d_in, p, slice(0, 8)) if d_in.shape[0] == 2 * pairs else d_in[p])
        image = image + obs * d
        x = alpha * d
        if not first:
            x = x_in[p] + x
        r = r - alpha * image
        if last:
            for h in range(2):
                result[2 * p + h, 0:8] = x[:, h * LANES : (h + 1) * LANES]
                result[2 * p + h, 8:16] = r[:, h * LANES : (h + 1) * LANES]
            return carry
        x_out[p] = x
        r_out[p] = r
        if d_out is not None:
            d_out[p] = d
        return carry[0] + r * r, carry[1] + r * r * obs, carry[2] + r * d * obs

    if last:
        lax.fori_loop(0, pairs, body, 0, unroll=UNROLL)
        for b in range(out_ref.shape[0]):
            out_ref[b] = result[tab_ref[pairs + b]]
        return
    zero = jnp.zeros((8, 2 * LANES), jnp.float32)
    sums = lax.fori_loop(0, pairs, body, (zero, zero, zero), unroll=UNROLL)
    lane = lax.broadcasted_iota(jnp.int32, (8, LANES), 1)
    scal_out[...] = jnp.where(lane == 0, rr, d_obs_d)
    project(
        pos_ref, tab_ref, anom_ref, gauge_ref, lambda p: r_out[p], sums, acc,
        (keep_0, keep_1, send_0, send_1),
    )


def shift(v, axis, k):
    n = lax.axis_size(axis)
    return lax.ppermute(v, axis, [(i, (i + k) % n) for i in range(n)])


def swap(v):
    return lax.ppermute(v, "c", [(0, 1), (1, 0)])


EVEN = ((0, 1), (1, 0), (2, 3), (3, 2))
ODD = ((1, 2), (2, 1), (3, 0), (0, 3))


def meet(v, partners):
    return v + lax.ppermute(v, "x", partners)


def total_over_gauges(keep_0, keep_1, send_0, send_1):
    sum_0, sum_1 = keep_0 + swap(send_0), keep_1 + swap(send_1)
    sum_0, sum_1 = meet(sum_0, EVEN), meet(sum_1, ODD)
    sum_0, sum_1 = meet(sum_0, ODD), meet(sum_1, EVEN)
    return sum_0, sum_1, swap(sum_0), swap(sum_1)


def to_all(v, axis):
    n = lax.axis_size(axis)
    return lax.all_to_all(jnp.broadcast_to(v[None], (n,) + v.shape), axis, 0, 0, tiled=True)


def gather(anomalies):
    own_0 = to_all(anomalies[:FIRST_ROWS], "z")
    later, own_0 = lax.optimization_barrier((anomalies[FIRST_ROWS:], own_0))
    below_0, above_0 = shift(own_0, "y", 1), shift(own_0, "y", -1)
    own_1 = to_all(later, "z")
    far_0 = shift(below_0, "y", 1)
    below_1, above_1 = shift(own_1, "y", 1), shift(own_1, "y", -1)
    far_1 = shift(above_1, "y", -1)
    return own_0, below_0, above_0, far_0, own_1, below_1, above_1, far_1


def local(anomalies, innovations, obs_var, basins, taper_mask):
    blk, members = anomalies.shape
    peers = lax.axis_size("y") * lax.axis_size("z")
    me_x, me_c = lax.axis_index("x"), lax.axis_index("c")
    nx, ny, nc, nz = (lax.axis_size(a) for a in ("x", "y", "c", "z"))
    nblocks = taper_mask.shape[0]

    near = taper_mask != 0
    place = jnp.arange(nblocks, dtype=jnp.int32)
    leader = jnp.min(jnp.where(near, place[None, :], nblocks), axis=1)
    leads = (leader == place)[None, :] & (place[None, :] < leader[:, None])
    gid = jnp.sum(leads.astype(jnp.int32), axis=1)
    gid = gid.reshape(nx, ny, nc, nz)
    gid = lax.dynamic_slice(gid, (me_x, 0, me_c, 0), (1, ny, 1, nz)).reshape(peers)
    gid = jnp.minimum(gid, GROUPS - 1)
    pos = jnp.stack([me_c, lax.axis_index("y")]).astype(jnp.int32)

    pieces = gather(anomalies)
    lanes = ((0, 0), (0, LANES - blk))
    each = members // peers
    field = jnp.pad(innovations.T, lanes).reshape(peers, each, LANES)
    extra = jnp.pad(jnp.stack([obs_var, basins.astype(jnp.float32)]), ((0, 6), (0, LANES - blk)))
    pay = jnp.concatenate([field, jnp.broadcast_to(extra[None], (peers, 8, LANES))], 1)
    pay = lax.all_to_all(pay, PEERS, 0, 0, tiled=True)

    smem = pl.BlockSpec(memory_space=pltpu.SMEM)
    vmem = pl.BlockSpec(memory_space=pltpu.VMEM)
    f32 = functools.partial(jax.ShapeDtypeStruct, dtype=jnp.float32)
    half = BASINS // 2 * each
    pairs = (peers + GROUPS) // 2
    shards = [f32((2 * half + each, members)), f32((2 * half, members))] * 2
    state = f32((pairs, each, 2 * LANES))
    sums = (GROUPS, 2, half, members)
    params = pltpu.CompilerParams(vmem_limit_bytes=24 * 2**20)

    tab, anoms, gauges, *parts = pl.pallas_call(
        first_kernel,
        out_shape=(
            jax.ShapeDtypeStruct((pairs + peers,), jnp.int32),
            jax.ShapeDtypeStruct((pairs, 4 * LANES, members), jnp.bfloat16),
            f32((2 * pairs, 2 * each, LANES)),
            *shards,
        ),
        in_specs=[smem, smem] + [vmem] * 9,
        out_specs=(smem,) + (vmem,) * 6,
        scratch_shapes=[pltpu.SMEM((GROUPS,), jnp.int32), pltpu.VMEM(sums, jnp.float32)],
        compiler_params=params,
        name="project",
    )(pos, gid, pay, *pieces)
    common = (pos, tab, anoms, gauges)
    carried = ()
    for step in range(ITERS):
        first, last = step == 0, step + 1 == ITERS
        args = (*common, *total_over_gauges(*parts), *carried)
        if last:
            shapes = f32((peers, 2 * each, LANES))
            extra_scratch = [pltpu.VMEM((2 * pairs, 2 * each, LANES), jnp.float32)]
        else:
            shapes = (state, state, f32(sums), f32((each, LANES)), *shards)
            shapes = shapes if first else shapes + (state,)
            extra_scratch = []
        out = pl.pallas_call(
            functools.partial(step_kernel, members, first, last),
            out_shape=shapes,
            in_specs=[smem, smem] + [vmem] * (len(args) - 2),
            out_specs=vmem if last else (vmem,) * len(shapes),
            scratch_shapes=[
                pltpu.VMEM((GROUPS, BASINS * each, members), jnp.bfloat16),
                pltpu.VMEM((GROUPS, BASINS * each, members), jnp.bfloat16),
                pltpu.VMEM(sums, jnp.float32),
            ] + extra_scratch,
            compiler_params=params,
            name="finish" if last else "step",
        )(*args)
        if not last:
            x, r, dir_sum, scal, *parts = out[:8]
            carried = (x, r, gauges if first else out[8], dir_sum, scal)
    back = lax.all_to_all(out, PEERS, 0, 0, tiled=True)
    solution_field = back[:, :each, :blk].reshape(members, blk).T
    residual = back[:, each:, :blk].reshape(members, blk).T
    return solution_field, residual


def solution(mesh):
    fine = Mesh(mesh.devices.reshape(8, 4, 4, 2), ("z", "x", "y", "c"))
    split_all = ("x", "y", "c", "z")
    placed = (P(split_all, None), P(split_all, None), P(split_all), P(split_all), P())
    return jax.shard_map(
        local,
        mesh=fine,
        in_specs=placed,
        out_specs=(P(split_all, None), P(split_all, None)),
        check_vma=False,
    )
```

```python
import functools

import jax
import jax.numpy as jnp
from jax import lax
from jax.experimental import pallas as pl
from jax.experimental.pallas import tpu as pltpu
from jax.sharding import Mesh
from jax.sharding import PartitionSpec as P

ITERS = 3
BASINS = 16
GROUPS = 4
far_weight = 0.3

LANES = 128
PEERS = ("y", "z")
UNROLL = 6
NT = (((1,), (1,)), ((), ()))


def split(v):
    high = v.astype(jnp.bfloat16)
    return high, (v - high.astype(jnp.float32)).astype(jnp.bfloat16)


def pair(ref, p, rows=slice(None)):
    return jnp.concatenate([ref[2 * p, rows], ref[2 * p + 1, rows]], 1)


def same_basin(gauge_ref, p):
    basin = pair(gauge_ref, p, slice(9, 10))[None]
    ids = lax.broadcasted_iota(jnp.int32, (BASINS, 8, 2 * LANES), 0).astype(jnp.float32)
    return ids == basin


def project(pos_ref, tab_ref, anom_ref, gauge_ref, field, sums, acc, outs):
    pairs = anom_ref.shape[0]
    acc[...] = jnp.zeros_like(acc)

    def body(p, carry):
        spread = jnp.where(same_basin(gauge_ref, p), field(p)[None], 0.0)
        high, low = split(spread.reshape(BASINS * 8, 2 * LANES))
        total = jnp.dot(
            jnp.concatenate([high, high], 1), anom_ref[p], preferred_element_type=jnp.float32
        ) + jnp.dot(low, anom_ref[p, : 2 * LANES], preferred_element_type=jnp.float32)
        g = tab_ref[p]
        acc[g] = acc[g] + total.reshape(acc.shape[1:])
        return carry

    lax.fori_loop(0, pairs, body, 0, unroll=UNROLL)
    half = acc.shape[2]
    lane = lax.broadcasted_iota(jnp.int32, (8, acc.shape[3]), 1)
    row = jnp.zeros((8, acc.shape[3]), jnp.float32)
    for place, value in enumerate(sums):
        row = jnp.where(lane == place, jnp.sum(value, axis=1, keepdims=True), row)
    me_c = pos_ref[0]
    for side in range(2):
        core = me_c if side == 0 else 1 - me_c
        for g in range(GROUPS):
            out = outs[2 * side + g // 2]
            out[(g % 2) * half : (g % 2 + 1) * half] = acc[g, core]
        outs[2 * side][2 * half :] = row


def first_kernel(
    pos_ref, gid_ref, pay_ref, own, below_1, above_1, below_2, above_2, below_3, above_3,
    far_low, far_high, tab_ref, anom_ref, gauge_ref, keep_0, keep_1, send_0, send_1, count, acc,
):
    blocks = pay_ref.shape[0]
    slots = gauge_ref.shape[0]
    pairs = slots // 2
    ny = own.shape[0]
    nz = blocks // ny

    for g in range(GROUPS):
        count[g] = 0

    def tally(b, carry):
        g = gid_ref[b]
        count[g] = count[g] + 1
        return carry

    lax.fori_loop(0, blocks, tally, 0, unroll=4)
    start = jnp.int32(0)
    spare = jnp.int32(0)
    for p in range(pairs):
        tab_ref[p] = 0
    empty = []
    for g in range(GROUPS):
        n = count[g]
        count[g] = 2 * start

        def mark(p, carry, g=g):
            tab_ref[p] = g
            return carry

        end = start + lax.div(n + 1, 2)
        lax.fori_loop(start, end, mark, 0)
        odd = lax.rem(n, 2)
        empty.append((odd == 1, 2 * end - 1))
        start = end

    def assign(b, carry):
        g = gid_ref[b]
        s = count[g]
        count[g] = s + 1
        tab_ref[pairs + b] = s
        gauge_ref[s] = pay_ref[b]
        return carry

    lax.fori_loop(0, blocks, assign, 0, unroll=4)

    def put(s, value):
        high, low = split(value)
        p, h = lax.div(s, 2), lax.rem(s, 2)
        anom_ref[p, pl.ds(pl.multiple_of(h * LANES, LANES), LANES)] = high
        anom_ref[p, pl.ds(pl.multiple_of((2 + h) * LANES, LANES), LANES)] = low

    blank = jnp.zeros((LANES, anom_ref.shape[2]), jnp.float32)

    def clear(s):
        put(s, blank)
        gauge_ref[s] = jnp.zeros(gauge_ref.shape[1:], jnp.float32)

    for odd, s in empty:
        pl.when(odd)(functools.partial(clear, s))

    def clear_slot(s, carry):
        clear(s)
        return carry

    lax.fori_loop(2 * start, slots, clear_slot, 0)

    me_z = pos_ref[1]
    rest = jnp.zeros((LANES - own.shape[1], own.shape[2]), jnp.float32)
    near = (own, above_1, above_2, above_3, None, below_3, below_2, below_1)
    for k, ref in enumerate(near):
        z = lax.rem(me_z + k, nz)
        for y in range(ny):
            if ref is not None:
                value = ref[y]
            elif y < ny // 2:
                value = far_low[y]
            else:
                value = far_high[y - ny // 2]
            put(tab_ref[pairs + y * nz + z], jnp.concatenate([value, rest], 0))

    zero = jnp.zeros((8, 2 * LANES), jnp.float32)
    one, two = zero, zero
    for p in range(pairs):
        r, obs = pair(gauge_ref, p, slice(0, 8)), pair(gauge_ref, p, slice(8, 9))
        one, two = one + r * r, two + r * r * obs
    project(
        pos_ref, tab_ref, anom_ref, gauge_ref, lambda p: pair(gauge_ref, p, slice(0, 8)),
        (one, two), acc, (keep_0, keep_1, send_0, send_1),
    )


def step_kernel(members, first, last, *refs):
    refs = list(refs)
    pos_ref, tab_ref, anom_ref, gauge_ref, own_0, own_1, other_0, other_1 = refs[:8]
    del refs[:8]
    if not first:
        x_in, r_in, d_in, dir_in, scal_in = refs[:5]
        del refs[:5]
    if last:
        out_ref = refs.pop(0)
        e_high, e_low, dir_sum, result = refs
    else:
        x_out, r_out, dir_out, scal_out, keep_0, keep_1, send_0, send_1 = refs[:8]
        d_out = None if first else refs[8]
        e_high, e_low, acc = refs[-3:]
        dir_sum = dir_out
    pairs = anom_ref.shape[0]
    wide = anom_ref.shape[2]
    rows = BASINS * 8
    half = rows // 2
    me_c = pos_ref[0]

    row = own_0[2 * half :]
    rr, r_obs_r, r_obs_d = row[:, 0:1], row[:, 1:2], row[:, 2:3]
    if first:
        d_obs_d = r_obs_r
    else:
        beta = rr / scal_in[:, 0:1]
        d_obs_d = r_obs_r + 2.0 * beta * r_obs_d + beta * beta * scal_in[:, 1:2]

    def advance(new, old):
        if first:
            return new
        mixed = new.reshape(-1, 8, wide) + beta[None] * old().reshape(-1, 8, wide)
        return mixed.reshape(half, wide)

    for g in range(GROUPS):
        own, other = (own_0, other_0) if g < 2 else (own_1, other_1)
        part = slice(g % 2 * half, (g % 2 + 1) * half)
        dir_sum[g, me_c] = advance(own[part], lambda: dir_in[g, me_c])
        dir_sum[g, 1 - me_c] = advance(other[part], lambda: dir_in[g, 1 - me_c])
    curve = jnp.zeros((8, wide), jnp.float32)
    for g in range(GROUPS):
        d_g = dir_sum[g].reshape(BASINS, 8, wide)
        every = jnp.sum(d_g, axis=0)
        e_g = ((1.0 - far_weight) / (members - 1)) * d_g + (far_weight / (members - 1)) * every[None]
        curve = curve + jnp.sum(d_g * e_g, axis=0)
        high, low = split(e_g.reshape(rows, wide))
        e_high[g] = high
        e_low[g] = low
    alpha = rr / (jnp.sum(curve, axis=1, keepdims=True) + d_obs_d)

    def body(p, carry):
        g = tab_ref[p]
        both = lax.dot_general(
            jnp.concatenate([e_high[g], e_low[g]], 0), anom_ref[p, : 2 * LANES], NT,
            preferred_element_type=jnp.float32,
        )
        third = lax.dot_general(
            e_high[g], anom_ref[p, 2 * LANES :], NT, preferred_element_type=jnp.float32
        )
        every = (both[:rows] + both[rows:] + third).reshape(BASINS, 8, 2 * LANES)
        image = jnp.sum(jnp.where(same_basin(gauge_ref, p), every, 0.0), axis=0)
        obs = pair(gauge_ref, p, slice(8, 9))
        if first:
            r = pair(gauge_ref, p, slice(0, 8))
            d = r
        else:
            r = r_in[p]
            d = r + beta * (pair(d_in, p, slice(0, 8)) if d_in.shape[0] == 2 * pairs else d_in[p])
        image = image + obs * d
        x = alpha * d
        if not first:
            x = x_in[p] + x
        r = r - alpha * image
        if last:
            for h in range(2):
                result[2 * p + h, 0:8] = x[:, h * LANES : (h + 1) * LANES]
                result[2 * p + h, 8:16] = r[:, h * LANES : (h + 1) * LANES]
            return carry
        x_out[p] = x
        r_out[p] = r
        if d_out is not None:
            d_out[p] = d
        return carry[0] + r * r, carry[1] + r * r * obs, carry[2] + r * d * obs

    if last:
        lax.fori_loop(0, pairs, body, 0, unroll=UNROLL)
        for b in range(out_ref.shape[0]):
            out_ref[b] = result[tab_ref[pairs + b]]
        return
    zero = jnp.zeros((8, 2 * LANES), jnp.float32)
    sums = lax.fori_loop(0, pairs, body, (zero, zero, zero), unroll=UNROLL)
    lane = lax.broadcasted_iota(jnp.int32, (8, LANES), 1)
    scal_out[...] = jnp.where(lane == 0, rr, d_obs_d)
    project(
        pos_ref, tab_ref, anom_ref, gauge_ref, lambda p: r_out[p], sums, acc,
        (keep_0, keep_1, send_0, send_1),
    )


def shift(v, axis, k):
    n = lax.axis_size(axis)
    return lax.ppermute(v, axis, [(i, (i + k) % n) for i in range(n)])


def swap(v):
    return lax.ppermute(v, "c", [(0, 1), (1, 0)])


EVEN = ((0, 1), (1, 0), (2, 3), (3, 2))
ODD = ((1, 2), (2, 1), (3, 0), (0, 3))


def meet(v, partners):
    return v + lax.ppermute(v, "x", partners)


def total_over_gauges(keep_0, keep_1, send_0, send_1):
    sum_0, sum_1 = keep_0 + swap(send_0), keep_1 + swap(send_1)
    sum_0, sum_1 = meet(sum_0, EVEN), meet(sum_1, ODD)
    sum_0, sum_1 = meet(sum_0, ODD), meet(sum_1, EVEN)
    return sum_0, sum_1, swap(sum_0), swap(sum_1)


def to_all(v, axis):
    n = lax.axis_size(axis)
    return lax.all_to_all(jnp.broadcast_to(v[None], (n,) + v.shape), axis, 0, 0, tiled=True)


def gather(anomalies):
    own = to_all(anomalies, "y")
    below, above = own, own
    pieces = [own]
    for _ in range((lax.axis_size("z") - 1) // 2):
        below, above = shift(below, "z", 1), shift(above, "z", -1)
        pieces += [below, above]
    half = own.shape[0] // 2
    return (*pieces, shift(below[:half], "z", 1), shift(above[half:], "z", -1))


def local(anomalies, innovations, obs_var, basins, taper_mask):
    blk, members = anomalies.shape
    peers = lax.axis_size("y") * lax.axis_size("z")
    me_x, me_c = lax.axis_index("x"), lax.axis_index("c")
    nx, ny, nc, nz = (lax.axis_size(a) for a in ("x", "y", "c", "z"))
    nblocks = taper_mask.shape[0]

    near = taper_mask != 0
    place = jnp.arange(nblocks, dtype=jnp.int32)
    leader = jnp.min(jnp.where(near, place[None, :], nblocks), axis=1)
    leads = (leader == place)[None, :] & (place[None, :] < leader[:, None])
    gid = jnp.sum(leads.astype(jnp.int32), axis=1)
    gid = gid.reshape(nx, ny, nc, nz)
    gid = lax.dynamic_slice(gid, (me_x, 0, me_c, 0), (1, ny, 1, nz)).reshape(peers)
    gid = jnp.minimum(gid, GROUPS - 1)
    pos = jnp.stack([me_c, lax.axis_index("z")]).astype(jnp.int32)

    pieces = gather(anomalies)
    lanes = ((0, 0), (0, LANES - blk))
    each = members // peers
    field = jnp.pad(innovations.T, lanes).reshape(peers, each, LANES)
    extra = jnp.pad(jnp.stack([obs_var, basins.astype(jnp.float32)]), ((0, 6), (0, LANES - blk)))
    pay = jnp.concatenate([field, jnp.broadcast_to(extra[None], (peers, 8, LANES))], 1)
    pay = lax.all_to_all(pay, PEERS, 0, 0, tiled=True)

    smem = pl.BlockSpec(memory_space=pltpu.SMEM)
    vmem = pl.BlockSpec(memory_space=pltpu.VMEM)
    f32 = functools.partial(jax.ShapeDtypeStruct, dtype=jnp.float32)
    half = BASINS // 2 * each
    pairs = (peers + GROUPS) // 2
    shards = [f32((2 * half + each, members)), f32((2 * half, members))] * 2
    state = f32((pairs, each, 2 * LANES))
    sums = (GROUPS, 2, half, members)
    params = pltpu.CompilerParams(vmem_limit_bytes=24 * 2**20)

    tab, anoms, gauges, *parts = pl.pallas_call(
        first_kernel,
        out_shape=(
            jax.ShapeDtypeStruct((pairs + peers,), jnp.int32),
            jax.ShapeDtypeStruct((pairs, 4 * LANES, members), jnp.bfloat16),
            f32((2 * pairs, 2 * each, LANES)),
            *shards,
        ),
        in_specs=[smem, smem] + [vmem] * 10,
        out_specs=(smem,) + (vmem,) * 6,
        scratch_shapes=[pltpu.SMEM((GROUPS,), jnp.int32), pltpu.VMEM(sums, jnp.float32)],
        compiler_params=params,
        name="project",
    )(pos, gid, pay, *pieces)
    common = (pos, tab, anoms, gauges)
    carried = ()
    for step in range(ITERS):
        first, last = step == 0, step + 1 == ITERS
        args = (*common, *total_over_gauges(*parts), *carried)
        if last:
            shapes = f32((peers, 2 * each, LANES))
            extra_scratch = [pltpu.VMEM((2 * pairs, 2 * each, LANES), jnp.float32)]
        else:
            shapes = (state, state, f32(sums), f32((each, LANES)), *shards)
            shapes = shapes if first else shapes + (state,)
            extra_scratch = []
        out = pl.pallas_call(
            functools.partial(step_kernel, members, first, last),
            out_shape=shapes,
            in_specs=[smem, smem] + [vmem] * (len(args) - 2),
            out_specs=vmem if last else (vmem,) * len(shapes),
            scratch_shapes=[
                pltpu.VMEM((GROUPS, BASINS * each, members), jnp.bfloat16),
                pltpu.VMEM((GROUPS, BASINS * each, members), jnp.bfloat16),
                pltpu.VMEM(sums, jnp.float32),
            ] + extra_scratch,
            compiler_params=params,
            name="finish" if last else "step",
        )(*args)
        if not last:
            x, r, dir_sum, scal, *parts = out[:8]
            carried = (x, r, gauges if first else out[8], dir_sum, scal)
    back = lax.all_to_all(out, PEERS, 0, 0, tiled=True)
    solution_field = back[:, :each, :blk].reshape(members, blk).T
    residual = back[:, each:, :blk].reshape(members, blk).T
    return solution_field, residual


def solution(mesh):
    fine = Mesh(mesh.devices.reshape(8, 4, 4, 2), ("z", "x", "y", "c"))
    split_all = ("x", "y", "c", "z")
    placed = (P(split_all, None), P(split_all, None), P(split_all), P(split_all), P())
    return jax.shard_map(
        local,
        mesh=fine,
        in_specs=placed,
        out_specs=(P(split_all, None), P(split_all, None)),
        check_vma=False,
    )
```

```python
import functools

import jax
import jax.numpy as jnp
from jax import lax
from jax.experimental import pallas as pl
from jax.experimental.pallas import tpu as pltpu
from jax.sharding import Mesh
from jax.sharding import PartitionSpec as P

ITERS = 3
BASINS = 16
GROUPS = 4
far_weight = 0.3

LANES = 128
ROWS = 8
EACH = 4
PEERS = ("y", "c", "z")
EARLY = (0, -1, 1, -2, 2, -3, 3)


def split(v):
    high = v.astype(jnp.bfloat16)
    return high, (v - high.astype(jnp.float32)).astype(jnp.bfloat16)


def both_halves(v):
    return v + pltpu.roll(v, EACH, 0)


def block_id(pos_ref, shape, y, step, sibling):
    _, nc, nz = shape
    z = lax.rem(pos_ref[1] + (step + nz), nz)
    c = 1 - pos_ref[0] if sibling else pos_ref[0]
    return (y * nc + c) * nz + z


def early_blocks(shape):
    return [(y, step, s) for step in EARLY for s in (False, True) for y in range(shape[0])]


def late_blocks(shape):
    ny, _, nz = shape
    return [
        (y0 + y, nz // 2, s) for y0 in (0, ny // 2) for s in (False, True) for y in range(ny // 2)
    ]


def pack_kernel(shape, *refs):
    pos_ref, gid_ref = refs[:2]
    tab_ref, anom_ref, turn_ref, count = refs[-4:]
    pieces = refs[2:-4]
    ny = shape[0]
    pairs = anom_ref.shape[0]
    early = early_blocks(shape)
    ids = [block_id(pos_ref, shape, *e) for e in early]
    for g in range(GROUPS):
        count[g] = 0
    for i in ids:
        g = gid_ref[i]
        count[g] = count[g] + 1
    for p in range(pairs):
        tab_ref[p] = 0
    start = jnp.int32(0)
    empty = []
    for g in range(GROUPS):
        n = count[g]
        count[g] = 2 * start

        def mark(p, carry, g=g):
            tab_ref[p] = g
            return carry

        end = start + lax.div(n + 1, 2)
        lax.fori_loop(start, end, mark, 0)
        empty.append((lax.rem(n, 2) == 1, 2 * end - 1))
        start = end

    def put(s, value):
        high, low = split(value)
        p, h = lax.div(s, 2), lax.rem(s, 2)
        first = pl.ds(pl.multiple_of(h * LANES, LANES), LANES)
        second = pl.ds(pl.multiple_of((2 + h) * LANES, LANES), LANES)
        anom_ref[p, first] = high
        anom_ref[p, second] = low
        high, low = split(value.T)
        turn_ref[p, :, first] = high
        turn_ref[p, :, second] = low

    blank = jnp.zeros((LANES, anom_ref.shape[2]), jnp.float32)
    for odd, s in empty:
        pl.when(odd)(functools.partial(put, s, blank))

    def clear(s, carry):
        put(s, blank)
        return carry

    lax.fori_loop(2 * start, 2 * pairs, clear, 0)
    rest = blank[pieces[0].shape[1] :]
    for k, i in enumerate(ids):
        g = gid_ref[i]
        s = count[g]
        count[g] = s + 1
        tab_ref[pairs + k] = s
        put(s, jnp.concatenate([pieces[k // ny][k % ny], rest], 0))
    for k, e in enumerate(late_blocks(shape)):
        tab_ref[pairs + len(ids) + k] = gid_ref[block_id(pos_ref, shape, *e)]


class Part:
    def __init__(self, tab_ref, anom_ref, turn_ref, gauge_ref, pairs, early):
        self.count, self.width = anom_ref.shape[0], anom_ref.shape[1] // 2
        self.tab_ref, self.anom_ref, self.turn_ref = tab_ref, anom_ref, turn_ref
        self.gauge_ref = gauge_ref
        self.paired = self.width == 2 * LANES
        self.first_group = 0 if self.paired else pairs + early
        self.first_slot = 0 if self.paired else 2 * pairs

    def group(self, p):
        return self.tab_ref[self.first_group + p]

    def gauges(self, p, rows):
        if self.paired:
            return jnp.concatenate([self.gauge_ref[2 * p, rows], self.gauge_ref[2 * p + 1, rows]], 1)
        return self.gauge_ref[self.first_slot + p, rows]

    def field(self, p):
        return self.gauges(p, slice(0, ROWS))

    def obs(self, p):
        return self.gauges(p, slice(ROWS, ROWS + 1))

    def same_basin(self, p):
        basin = self.gauges(p, slice(ROWS + 1, ROWS + 2))[None]
        dims = (BASINS * EACH // ROWS, ROWS, self.width)
        tile = lax.broadcasted_iota(jnp.int32, dims, 0)
        row = lax.broadcasted_iota(jnp.int32, dims, 1)
        ids = tile * (ROWS // EACH) + jnp.where(row < EACH, 0, 1)
        return ids.astype(jnp.float32) == basin


def project(parts, fields, sums, acc, outs):
    rows = BASINS * EACH
    acc[...] = jnp.zeros_like(acc)
    for part, field in zip(parts, fields):
        width = part.width
        for p in range(part.count):
            near = part.same_basin(p)
            v = field(p)
            v_high = v.astype(jnp.bfloat16).astype(jnp.float32)
            high, low = (
                jnp.where(near, u[None], 0.0).reshape(rows, width).astype(jnp.bfloat16)
                for u in (v_high, v - v_high)
            )
            both = jnp.dot(
                jnp.concatenate([high, low], 0), part.anom_ref[p, :width],
                preferred_element_type=jnp.float32,
            )
            third = jnp.dot(high, part.anom_ref[p, width:], preferred_element_type=jnp.float32)
            g = part.group(p)
            acc[g] = acc[g] + (both[:rows] + both[rows:] + third)
    lane = lax.broadcasted_iota(jnp.int32, (ROWS, acc.shape[2]), 1)
    row = jnp.zeros((ROWS, acc.shape[2]), jnp.float32)
    for place, value in enumerate(sums):
        row = jnp.where(lane == place, value, row)
    for g in range(GROUPS):
        outs[g // 2][g % 2 * rows : (g % 2 + 1) * rows] = acc[g]
    outs[0][2 * rows :] = row


def lane_sum(v):
    return jnp.sum(v, axis=1, keepdims=True)


def total(values):
    return functools.reduce(lambda a, b: a + b, values)


def first_kernel(shape, *refs):
    pos_ref, tab_ref, pay_ref, anom_ref, turn_ref = refs[:5]
    gauge_ref, late_ref, late_turn, out_0, out_1, acc = refs[-6:]
    pieces = refs[5:-6]
    pairs = anom_ref.shape[0]
    early, late = early_blocks(shape), late_blocks(shape)
    row = lax.broadcasted_iota(jnp.int32, (ROWS, LANES), 0)

    def place(s, e):
        tile = pay_ref[block_id(pos_ref, shape, *e)]
        turned = pltpu.roll(tile, EACH, 0)
        gauge_ref[s, :ROWS] = jnp.where(row < EACH, tile, turned)
        gauge_ref[s, ROWS:] = turned

    gauge_ref[...] = jnp.zeros_like(gauge_ref)
    for k, e in enumerate(early):
        place(tab_ref[pairs + k], e)
    for k, e in enumerate(late):
        place(2 * pairs + k, e)
    rest = jnp.zeros((LANES - pieces[0].shape[1], pieces[0].shape[2]), jnp.float32)
    half = pieces[0].shape[0]
    for k in range(len(late)):
        value = jnp.concatenate([pieces[k // half][k % half], rest], 0)
        late_ref[k, :LANES], late_ref[k, LANES:] = split(value)
        late_turn[k, :, :LANES], late_turn[k, :, LANES:] = split(value.T)
    parts = [
        Part(tab_ref, a, t, gauge_ref, pairs, len(early))
        for a, t in ((anom_ref, turn_ref), (late_ref, late_turn))
    ]
    one, two = [], []
    for part in parts:
        squares = [part.field(p) * part.field(p) for p in range(part.count)]
        one.append(lane_sum(total(squares)))
        two.append(lane_sum(total([s * part.obs(p) for p, s in enumerate(squares)])))
    project(parts, [part.field for part in parts], (total(one), total(two)), acc, (out_0, out_1))


def step_kernel(shape, members, first, last, *refs):
    refs = list(refs)

    def take(n):
        taken = refs[:n]
        del refs[:n]
        return taken

    pos_ref, tab_ref, gauge_ref, anom_ref, turn_ref, late_ref, late_turn, sum_0, sum_1 = take(9)
    if not first:
        x_in, r_in, dir_in, scal_in = take(2), take(2), *take(2)
        d_in = take(0 if last is None else 2)
    if last:
        (out_ref,) = take(1)
        e_high, e_low, dir_sum, result = refs
    else:
        x_out, r_out, dir_out, scal_out, outs = take(2), take(2), *take(2), take(2)
        d_out = [] if first else take(2)
        e_high, e_low, acc = refs
        dir_sum = dir_out
    pairs = anom_ref.shape[0]
    wide = anom_ref.shape[2]
    rows = BASINS * EACH
    early, late = early_blocks(shape), late_blocks(shape)
    parts = [
        Part(tab_ref, a, t, gauge_ref, pairs, len(early))
        for a, t in ((anom_ref, turn_ref), (late_ref, late_turn))
    ]

    row = sum_0[2 * rows :]
    rr, r_obs_r, r_obs_d = row[:, 0:1], row[:, 1:2], row[:, 2:3]
    if first:
        d_obs_d = r_obs_r
    else:
        beta = rr / scal_in[:, 0:1]
        d_obs_d = r_obs_r + 2.0 * beta * r_obs_d + beta * beta * scal_in[:, 1:2]
    curve = jnp.zeros((ROWS, wide), jnp.float32)
    for g in range(GROUPS):
        d_g = (sum_0, sum_1)[g // 2][g % 2 * rows : (g % 2 + 1) * rows].reshape(-1, ROWS, wide)
        if not first:
            d_g = d_g + beta[None] * dir_in[g].reshape(-1, ROWS, wide)
        dir_sum[g] = d_g.reshape(rows, wide)
        every = both_halves(jnp.sum(d_g, axis=0))
        e_g = ((1.0 - far_weight) / (members - 1)) * d_g + (far_weight / (members - 1)) * every[None]
        curve = curve + jnp.sum(d_g * e_g, axis=0)
        e_high[g], e_low[g] = split(e_g.reshape(rows, wide))
    alpha = rr / (lane_sum(both_halves(curve)) + d_obs_d)

    one, two, three = [], [], []
    for k, part in enumerate(parts):
        width = part.width
        squares, weighted, crossed = [], [], []
        for p in range(part.count):
            g = part.group(p)
            both = jnp.dot(
                jnp.concatenate([e_high[g], e_low[g]], 0), part.turn_ref[p, :, :width],
                preferred_element_type=jnp.float32,
            )
            third = jnp.dot(
                e_high[g], part.turn_ref[p, :, width:], preferred_element_type=jnp.float32
            )
            every = (both[:rows] + both[rows:] + third).reshape(-1, ROWS, width)
            image = both_halves(jnp.sum(jnp.where(part.same_basin(p), every, 0.0), axis=0))
            obs = part.obs(p)
            if first:
                r = part.field(p)
                d = r
            else:
                r = r_in[k][p]
                d = r + beta * (d_in[k][p] if d_in else part.field(p))
            image = image + obs * d
            x = alpha * d
            if not first:
                x = x_in[k][p] + x
            r = r - alpha * image
            if last:
                for h in range(width // LANES):
                    lanes = slice(h * LANES, (h + 1) * LANES)
                    top = lax.broadcasted_iota(jnp.int32, (ROWS, LANES), 0) < EACH
                    s = part.first_slot + p * (width // LANES) + h
                    result[s] = jnp.where(top, x[:, lanes], r[:, lanes])
                continue
            x_out[k][p] = x
            r_out[k][p] = r
            if d_out:
                d_out[k][p] = d
            squares.append(r * r)
            weighted.append(r * r * obs)
            crossed.append(r * d * obs)
        if not last:
            one.append(lane_sum(total(squares)))
            two.append(lane_sum(total(weighted)))
            three.append(lane_sum(total(crossed)))
    if last:
        for k, e in enumerate(early):
            out_ref[block_id(pos_ref, shape, *e)] = result[tab_ref[pairs + k]]
        for k, e in enumerate(late):
            out_ref[block_id(pos_ref, shape, *e)] = result[2 * pairs + k]
        return
    lane = lax.broadcasted_iota(jnp.int32, (ROWS, LANES), 1)
    scal_out[...] = jnp.where(lane == 0, rr, d_obs_d)
    fields = [functools.partial(lambda ref, p: ref[p], ref) for ref in r_out]
    project(parts, fields, (total(one), total(two), total(three)), acc, outs)


def shift(v, axis, k):
    n = lax.axis_size(axis)
    return lax.ppermute(v, axis, [(i, (i + k) % n) for i in range(n)])


def swap(v):
    return lax.ppermute(v, "c", [(0, 1), (1, 0)])


EVEN = ((0, 1), (1, 0), (2, 3), (3, 2))
ODD = ((1, 2), (2, 1), (3, 0), (0, 3))


def meet(v, partners):
    return v + lax.ppermute(v, "x", partners)


def total_over_gauges(sum_0, sum_1):
    sum_0, sum_1 = meet(sum_0, EVEN), meet(sum_1, ODD)
    return meet(sum_0, ODD), meet(sum_1, EVEN)


def to_all(v, axis):
    n = lax.axis_size(axis)
    return lax.all_to_all(jnp.broadcast_to(v[None], (n,) + v.shape), axis, 0, 0, tiled=True)


def gather(anomalies):
    own = to_all(anomalies, "y")
    below, above = own, own
    early = [own, swap(own)]
    for _ in range((lax.axis_size("z") - 1) // 2):
        below, above = shift(below, "z", 1), shift(above, "z", -1)
        early += [below, swap(below), above, swap(above)]
    half = own.shape[0] // 2
    far_low, far_high = shift(below[:half], "z", 1), shift(above[half:], "z", -1)
    return early, [far_low, swap(far_low), far_high, swap(far_high)]


def local(anomalies, innovations, obs_var, basins, taper_mask):
    blk, members = anomalies.shape
    shape = tuple(lax.axis_size(a) for a in PEERS)
    peers = shape[0] * shape[1] * shape[2]
    nblocks = taper_mask.shape[0]

    near = taper_mask != 0
    place = jnp.arange(nblocks, dtype=jnp.int32)
    leader = jnp.min(jnp.where(near, place[None, :], nblocks), axis=1)
    leads = (leader == place)[None, :] & (place[None, :] < leader[:, None])
    gid = jnp.sum(leads.astype(jnp.int32), axis=1)
    gid = lax.dynamic_slice(gid, (lax.axis_index("x") * peers,), (peers,))
    gid = jnp.minimum(gid, GROUPS - 1)
    pos = jnp.stack([lax.axis_index("c"), lax.axis_index("z")]).astype(jnp.int32)

    early, late = gather(anomalies)
    field = innovations.T.reshape(peers, EACH, blk)
    extra = jnp.stack([obs_var, basins.astype(jnp.float32)])
    extra = jnp.pad(extra, ((0, ROWS - EACH - 2), (0, 0)))
    pay = jnp.concatenate([field, jnp.broadcast_to(extra[None], (peers, ROWS - EACH, blk))], 1)
    pay = jnp.pad(pay, ((0, 0), (0, 0), (0, LANES - blk)))
    pay = lax.all_to_all(pay, PEERS, 0, 0, tiled=True)

    smem = pl.BlockSpec(memory_space=pltpu.SMEM)
    vmem = pl.BlockSpec(memory_space=pltpu.VMEM)
    f32 = functools.partial(jax.ShapeDtypeStruct, dtype=jnp.float32)
    b16 = functools.partial(jax.ShapeDtypeStruct, dtype=jnp.bfloat16)
    rows = BASINS * EACH
    n_late = shape[0] * shape[1]
    n_early = peers - n_late
    pairs = (n_early + GROUPS) // 2
    shards = [f32((2 * rows + ROWS, members)), f32((2 * rows, members))]
    state = [f32((pairs, ROWS, 2 * LANES)), f32((n_late, ROWS, LANES))]
    sums = (GROUPS, rows, members)

    def params(mib):
        return pltpu.CompilerParams(vmem_limit_bytes=mib * 2**20)

    tab, anoms, turned = pl.pallas_call(
        functools.partial(pack_kernel, shape),
        out_shape=(
            jax.ShapeDtypeStruct((pairs + peers,), jnp.int32),
            b16((pairs, 4 * LANES, members)),
            b16((pairs, members, 4 * LANES)),
        ),
        in_specs=[smem, smem] + [vmem] * len(early),
        out_specs=(smem, vmem, vmem),
        scratch_shapes=[pltpu.SMEM((GROUPS,), jnp.int32)],
        compiler_params=params(28),
        cost_estimate=pl.CostEstimate(
            flops=n_early * blk * members * 8, bytes_accessed=n_early * blk * members * 12,
            transcendentals=0,
        ),
        name="pack",
    )(pos, gid, *early)
    gauges, late_anoms, late_turned, *parts = pl.pallas_call(
        functools.partial(first_kernel, shape),
        out_shape=(
            f32((2 * pairs + n_late, 2 * ROWS, LANES)),
            b16((n_late, 2 * LANES, members)),
            b16((n_late, members, 2 * LANES)),
            *shards,
        ),
        in_specs=[smem, smem] + [vmem] * (3 + len(late)),
        out_specs=(vmem,) * 5,
        scratch_shapes=[pltpu.VMEM(sums, jnp.float32)],
        compiler_params=params(28),
        name="project",
    )(pos, tab, pay, anoms, turned, *late)
    common = (pos, tab, gauges, anoms, turned, late_anoms, late_turned)
    carried = ()
    for step in range(ITERS):
        first, last = step == 0, step + 1 == ITERS
        args = (*common, *total_over_gauges(*parts), *carried)
        if last:
            shapes = [f32((peers, ROWS, LANES))]
            more = [pltpu.VMEM((2 * pairs + n_late, ROWS, LANES), jnp.float32)]
        else:
            shapes = [*state, *state, f32(sums), f32((ROWS, LANES)), *shards]
            shapes += [] if first else state
            more = []
        has_d = step > 1
        out = pl.pallas_call(
            functools.partial(step_kernel, shape, members, first, last if has_d or first else None),
            out_shape=shapes,
            in_specs=[smem, smem] + [vmem] * (len(args) - 2),
            out_specs=[vmem] * len(shapes),
            scratch_shapes=[
                pltpu.VMEM(sums, jnp.bfloat16),
                pltpu.VMEM(sums, jnp.bfloat16),
                pltpu.VMEM(sums, jnp.float32),
            ] + more,
            compiler_params=params(28),
            name="finish" if last else "step",
        )(*args)
        if not last:
            parts = out[6:8]
            carried = (*out[:6], *out[8:])
    back = lax.all_to_all(out[0], PEERS, 0, 0, tiled=True)
    solution_field = back[:, :EACH, :blk].reshape(members, blk).T
    residual = back[:, EACH:, :blk].reshape(members, blk).T
    return solution_field, residual


def solution(mesh):
    fine = Mesh(mesh.devices.reshape(8, 4, 4, 2), ("z", "x", "y", "c"))
    split_all = ("x", "y", "c", "z")
    placed = (P(split_all, None), P(split_all, None), P(split_all), P(split_all), P())
    return jax.shard_map(
        local,
        mesh=fine,
        in_specs=placed,
        out_specs=(P(split_all, None), P(split_all, None)),
        check_vma=False,
    )
```

```python
import functools

import jax
import jax.numpy as jnp
from jax import lax
from jax.experimental import pallas as pl
from jax.experimental.pallas import tpu as pltpu
from jax.sharding import Mesh
from jax.sharding import PartitionSpec as P

ITERS = 3
BASINS = 16
GROUPS = 4
far_weight = 0.3

LANES = 128
ROWS = 8
PEERS = ("y", "z")
EARLY = (0, -1, 1, -2, 2, -3, 3)


def split(v):
    high = v.astype(jnp.bfloat16)
    return high, (v - high.astype(jnp.float32)).astype(jnp.bfloat16)


def block_id(pos_ref, shape, y, step):
    nz = shape[1]
    return y * nz + lax.rem(pos_ref[1] + (step + nz), nz)


def early_blocks(shape):
    return [(y, step) for step in EARLY for y in range(shape[0])]


def late_blocks(shape):
    ny, nz = shape
    return [(y, nz // 2) for y in range(ny)]


def pack_kernel(shape, *refs):
    pos_ref, gid_ref = refs[:2]
    tab_ref, anom_ref, turn_ref, count = refs[-4:]
    pieces = refs[2:-4]
    ny = shape[0]
    pairs = anom_ref.shape[0]
    early = early_blocks(shape)
    ids = [block_id(pos_ref, shape, *e) for e in early]
    for g in range(GROUPS):
        count[g] = 0
    for i in ids:
        g = gid_ref[i]
        count[g] = count[g] + 1
    for p in range(pairs):
        tab_ref[p] = 0
    start = jnp.int32(0)
    empty = []
    for g in range(GROUPS):
        n = count[g]
        count[g] = 2 * start

        def mark(p, carry, g=g):
            tab_ref[p] = g
            return carry

        end = start + lax.div(n + 1, 2)
        lax.fori_loop(start, end, mark, 0)
        empty.append((lax.rem(n, 2) == 1, 2 * end - 1))
        start = end

    def put(s, value):
        high, low = split(value)
        p, h = lax.div(s, 2), lax.rem(s, 2)
        first = pl.ds(pl.multiple_of(h * LANES, LANES), LANES)
        second = pl.ds(pl.multiple_of((2 + h) * LANES, LANES), LANES)
        anom_ref[p, first] = high
        anom_ref[p, second] = low
        high, low = split(value.T)
        turn_ref[p, :, first] = high
        turn_ref[p, :, second] = low

    blank = jnp.zeros((LANES, anom_ref.shape[2]), jnp.float32)
    for odd, s in empty:
        pl.when(odd)(functools.partial(put, s, blank))

    def clear(s, carry):
        put(s, blank)
        return carry

    lax.fori_loop(2 * start, 2 * pairs, clear, 0)
    rest = blank[pieces[0].shape[1] :]
    for k, i in enumerate(ids):
        g = gid_ref[i]
        s = count[g]
        count[g] = s + 1
        tab_ref[pairs + k] = s
        put(s, jnp.concatenate([pieces[k // ny][k % ny], rest], 0))
    for k, e in enumerate(late_blocks(shape)):
        tab_ref[pairs + len(ids) + k] = gid_ref[block_id(pos_ref, shape, *e)]


class Part:
    def __init__(self, tab_ref, anom_ref, turn_ref, gauge_ref, pairs, early):
        self.count, self.width = anom_ref.shape[0], anom_ref.shape[1] // 2
        self.tab_ref, self.anom_ref, self.turn_ref = tab_ref, anom_ref, turn_ref
        self.gauge_ref = gauge_ref
        self.paired = self.width == 2 * LANES
        self.first_group = 0 if self.paired else pairs + early
        self.first_slot = 0 if self.paired else 2 * pairs

    def group(self, p):
        return self.tab_ref[self.first_group + p]

    def gauges(self, p, rows):
        if self.paired:
            return jnp.concatenate([self.gauge_ref[2 * p, rows], self.gauge_ref[2 * p + 1, rows]], 1)
        return self.gauge_ref[self.first_slot + p, rows]

    def field(self, p):
        return self.gauges(p, slice(0, ROWS))

    def obs(self, p):
        return self.gauges(p, slice(ROWS, ROWS + 1))

    def same_basin(self, p):
        basin = self.gauges(p, slice(ROWS + 1, ROWS + 2))[None]
        ids = lax.broadcasted_iota(jnp.int32, (BASINS, ROWS, self.width), 0)
        return ids.astype(jnp.float32) == basin


def project(pos_ref, parts, fields, sums, acc, outs):
    rows = BASINS * ROWS
    acc[...] = jnp.zeros_like(acc)
    for part, field in zip(parts, fields):
        width = part.width
        for p in range(part.count):
            near = part.same_basin(p)
            v = field(p)
            v_high = v.astype(jnp.bfloat16).astype(jnp.float32)
            high, low = (
                jnp.where(near, u[None], 0.0).reshape(rows, width).astype(jnp.bfloat16)
                for u in (v_high, v - v_high)
            )
            both = jnp.dot(
                jnp.concatenate([high, low], 0), part.anom_ref[p, :width],
                preferred_element_type=jnp.float32,
            )
            third = jnp.dot(high, part.anom_ref[p, width:], preferred_element_type=jnp.float32)
            g = part.group(p)
            acc[g] = acc[g] + (both[:rows] + both[rows:] + third).reshape(acc.shape[1:])
    lane = lax.broadcasted_iota(jnp.int32, (ROWS, acc.shape[3]), 1)
    row = jnp.zeros((ROWS, acc.shape[3]), jnp.float32)
    for place, value in enumerate(sums):
        row = jnp.where(lane == place, value, row)
    me_c, half = pos_ref[0], rows // 2
    for side in range(2):
        core = me_c if side == 0 else 1 - me_c
        for g in range(GROUPS):
            out = outs[2 * side + g // 2]
            out[g % 2 * half : (g % 2 + 1) * half] = acc[g, core]
        outs[2 * side][2 * half :] = row


def lane_sum(v):
    return jnp.sum(v, axis=1, keepdims=True)


def total(values):
    return functools.reduce(lambda a, b: a + b, values)


def first_kernel(shape, *refs):
    pos_ref, tab_ref, pay_ref, anom_ref, turn_ref = refs[:5]
    gauge_ref, late_ref, late_turn, *outs, acc = refs[-8:]
    pieces = refs[5:-8]
    pairs = anom_ref.shape[0]
    early, late = early_blocks(shape), late_blocks(shape)

    def place(s, e):
        gauge_ref[s] = pay_ref[block_id(pos_ref, shape, *e)]

    gauge_ref[...] = jnp.zeros_like(gauge_ref)
    for k, e in enumerate(early):
        place(tab_ref[pairs + k], e)
    for k, e in enumerate(late):
        place(2 * pairs + k, e)
    rest = jnp.zeros((LANES - pieces[0].shape[1], pieces[0].shape[2]), jnp.float32)
    half = pieces[0].shape[0]
    for k in range(len(late)):
        value = jnp.concatenate([pieces[k // half][k % half], rest], 0)
        late_ref[k, :LANES], late_ref[k, LANES:] = split(value)
        late_turn[k, :, :LANES], late_turn[k, :, LANES:] = split(value.T)
    parts = [
        Part(tab_ref, a, t, gauge_ref, pairs, len(early))
        for a, t in ((anom_ref, turn_ref), (late_ref, late_turn))
    ]
    one, two = [], []
    for part in parts:
        squares = [part.field(p) * part.field(p) for p in range(part.count)]
        one.append(lane_sum(total(squares)))
        two.append(lane_sum(total([s * part.obs(p) for p, s in enumerate(squares)])))
    fields = [part.field for part in parts]
    project(pos_ref, parts, fields, (total(one), total(two)), acc, outs)


def step_kernel(shape, members, first, last, *refs):
    refs = list(refs)

    def take(n):
        taken = refs[:n]
        del refs[:n]
        return taken

    pos_ref, tab_ref, gauge_ref, anom_ref, turn_ref, late_ref, late_turn = take(7)
    own, other = take(2), take(2)
    if not first:
        x_in, r_in, dir_in, scal_in = take(2), take(2), *take(2)
        d_in = take(0 if last is None else 2)
    if last:
        (out_ref,) = take(1)
        e_high, e_low, dir_sum, result = refs
    else:
        x_out, r_out, dir_out, scal_out, outs = take(2), take(2), *take(2), take(4)
        d_out = [] if first else take(2)
        e_high, e_low, acc = refs
        dir_sum = dir_out
    pairs = anom_ref.shape[0]
    wide = anom_ref.shape[2]
    rows = BASINS * ROWS
    early, late = early_blocks(shape), late_blocks(shape)
    parts = [
        Part(tab_ref, a, t, gauge_ref, pairs, len(early))
        for a, t in ((anom_ref, turn_ref), (late_ref, late_turn))
    ]

    me_c, half = pos_ref[0], rows // 2
    row = own[0][2 * half :]
    rr, r_obs_r, r_obs_d = row[:, 0:1], row[:, 1:2], row[:, 2:3]
    if first:
        d_obs_d = r_obs_r
    else:
        beta = rr / scal_in[:, 0:1]
        d_obs_d = r_obs_r + 2.0 * beta * r_obs_d + beta * beta * scal_in[:, 1:2]
    curve = jnp.zeros((ROWS, wide), jnp.float32)
    for g in range(GROUPS):
        halves = []
        for side, core in ((own, me_c), (other, 1 - me_c)):
            d_h = side[g // 2][g % 2 * half : (g % 2 + 1) * half].reshape(-1, ROWS, wide)
            if not first:
                d_h = d_h + beta[None] * dir_in[g, core].reshape(-1, ROWS, wide)
            dir_sum[g, core] = d_h.reshape(half, wide)
            halves.append((core, d_h))
        every = sum(jnp.sum(d_h, axis=0) for _, d_h in halves)
        for core, d_h in halves:
            e_h = (1.0 - far_weight) / (members - 1) * d_h + far_weight / (members - 1) * every[None]
            curve = curve + jnp.sum(d_h * e_h, axis=0)
            e_high[g, core], e_low[g, core] = split(e_h.reshape(half, wide))
    alpha = rr / (lane_sum(curve) + d_obs_d)

    one, two, three = [], [], []
    for k, part in enumerate(parts):
        width = part.width
        squares, weighted, crossed = [], [], []
        for p in range(part.count):
            g = part.group(p)
            e_g = e_high[g].reshape(rows, wide)
            both = jnp.dot(
                jnp.concatenate([e_g.reshape(rows, wide), e_low[g].reshape(rows, wide)], 0),
                part.turn_ref[p, :, :width],
                preferred_element_type=jnp.float32,
            )
            third = jnp.dot(
                e_g, part.turn_ref[p, :, width:], preferred_element_type=jnp.float32
            )
            every = (both[:rows] + both[rows:] + third).reshape(-1, ROWS, width)
            image = jnp.sum(jnp.where(part.same_basin(p), every, 0.0), axis=0)
            obs = part.obs(p)
            if first:
                r = part.field(p)
                d = r
            else:
                r = r_in[k][p]
                d = r + beta * (d_in[k][p] if d_in else part.field(p))
            image = image + obs * d
            x = alpha * d
            if not first:
                x = x_in[k][p] + x
            r = r - alpha * image
            if last:
                for h in range(width // LANES):
                    lanes = slice(h * LANES, (h + 1) * LANES)
                    s = part.first_slot + p * (width // LANES) + h
                    result[s, :ROWS] = x[:, lanes]
                    result[s, ROWS:] = r[:, lanes]
                continue
            x_out[k][p] = x
            r_out[k][p] = r
            if d_out:
                d_out[k][p] = d
            squares.append(r * r)
            weighted.append(r * r * obs)
            crossed.append(r * d * obs)
        if not last:
            one.append(lane_sum(total(squares)))
            two.append(lane_sum(total(weighted)))
            three.append(lane_sum(total(crossed)))
    if last:
        for k, e in enumerate(early):
            out_ref[block_id(pos_ref, shape, *e)] = result[tab_ref[pairs + k]]
        for k, e in enumerate(late):
            out_ref[block_id(pos_ref, shape, *e)] = result[2 * pairs + k]
        return
    lane = lax.broadcasted_iota(jnp.int32, (ROWS, LANES), 1)
    scal_out[...] = jnp.where(lane == 0, rr, d_obs_d)
    fields = [functools.partial(lambda ref, p: ref[p], ref) for ref in r_out]
    project(pos_ref, parts, fields, (total(one), total(two), total(three)), acc, outs)


def shift(v, axis, k):
    n = lax.axis_size(axis)
    return lax.ppermute(v, axis, [(i, (i + k) % n) for i in range(n)])


def swap(v):
    return lax.ppermute(v, "c", [(0, 1), (1, 0)])


EVEN = ((0, 1), (1, 0), (2, 3), (3, 2))
ODD = ((1, 2), (2, 1), (3, 0), (0, 3))


def meet(v, partners):
    return v + lax.ppermute(v, "x", partners)


def total_over_gauges(keep_0, keep_1, send_0, send_1):
    sum_0, sum_1 = keep_0 + swap(send_0), keep_1 + swap(send_1)
    sum_0, sum_1 = meet(sum_0, EVEN), meet(sum_1, ODD)
    sum_0, sum_1 = meet(sum_0, ODD), meet(sum_1, EVEN)
    return sum_0, sum_1, swap(sum_0), swap(sum_1)


def to_all(v, axis):
    n = lax.axis_size(axis)
    return lax.all_to_all(jnp.broadcast_to(v[None], (n,) + v.shape), axis, 0, 0, tiled=True)


def gather(anomalies):
    own = to_all(anomalies, "y")
    below, above = own, own
    early = [own]
    for _ in range((lax.axis_size("z") - 1) // 2):
        below, above = shift(below, "z", 1), shift(above, "z", -1)
        early += [below, above]
    half = own.shape[0] // 2
    return early, [shift(below[:half], "z", 1), shift(above[half:], "z", -1)]


def local(anomalies, innovations, obs_var, basins, taper_mask):
    blk, members = anomalies.shape
    shape = tuple(lax.axis_size(a) for a in PEERS)
    peers = shape[0] * shape[1]
    nx, nc = lax.axis_size("x"), lax.axis_size("c")
    me_x, me_c = lax.axis_index("x"), lax.axis_index("c")
    nblocks = taper_mask.shape[0]

    near = taper_mask != 0
    place = jnp.arange(nblocks, dtype=jnp.int32)
    leader = jnp.min(jnp.where(near, place[None, :], nblocks), axis=1)
    leads = (leader == place)[None, :] & (place[None, :] < leader[:, None])
    gid = jnp.sum(leads.astype(jnp.int32), axis=1)
    gid = gid.reshape(nx, shape[0], nc, shape[1])
    gid = lax.dynamic_slice(gid, (me_x, 0, me_c, 0), (1, shape[0], 1, shape[1])).reshape(peers)
    gid = jnp.minimum(gid, GROUPS - 1)
    pos = jnp.stack([me_c, lax.axis_index("z")]).astype(jnp.int32)

    early, late = gather(anomalies)
    lanes = ((0, 0), (0, LANES - blk))
    field = jnp.pad(innovations.T, lanes).reshape(peers, ROWS, LANES)
    extra = jnp.stack([obs_var, basins.astype(jnp.float32)])
    extra = jnp.pad(extra, ((0, ROWS - 2), (0, LANES - blk)))
    pay = jnp.concatenate([field, jnp.broadcast_to(extra[None], (peers, ROWS, LANES))], 1)
    pay = lax.all_to_all(pay, PEERS, 0, 0, tiled=True)

    smem = pl.BlockSpec(memory_space=pltpu.SMEM)
    vmem = pl.BlockSpec(memory_space=pltpu.VMEM)
    f32 = functools.partial(jax.ShapeDtypeStruct, dtype=jnp.float32)
    b16 = functools.partial(jax.ShapeDtypeStruct, dtype=jnp.bfloat16)
    rows = BASINS * ROWS
    n_late = shape[0]
    n_early = peers - n_late
    pairs = (n_early + GROUPS) // 2
    shards = [f32((rows + ROWS, members)), f32((rows, members))] * 2
    state = [f32((pairs, ROWS, 2 * LANES)), f32((n_late, ROWS, LANES))]
    sums = (GROUPS, 2, rows // 2, members)

    def params(mib):
        return pltpu.CompilerParams(vmem_limit_bytes=mib * 2**20)

    tab, anoms, turned = pl.pallas_call(
        functools.partial(pack_kernel, shape),
        out_shape=(
            jax.ShapeDtypeStruct((pairs + peers,), jnp.int32),
            b16((pairs, 4 * LANES, members)),
            b16((pairs, members, 4 * LANES)),
        ),
        in_specs=[smem, smem] + [vmem] * len(early),
        out_specs=(smem, vmem, vmem),
        scratch_shapes=[pltpu.SMEM((GROUPS,), jnp.int32)],
        compiler_params=params(20),
        cost_estimate=pl.CostEstimate(
            flops=n_early * blk * members * 8, bytes_accessed=n_early * blk * members * 12,
            transcendentals=0,
        ),
        name="pack",
    )(pos, gid, *early)
    gauges, late_anoms, late_turned, *parts = pl.pallas_call(
        functools.partial(first_kernel, shape),
        out_shape=(
            f32((2 * pairs + n_late, 2 * ROWS, LANES)),
            b16((n_late, 2 * LANES, members)),
            b16((n_late, members, 2 * LANES)),
            *shards,
        ),
        in_specs=[smem, smem] + [vmem] * (3 + len(late)),
        out_specs=(vmem,) * 7,
        scratch_shapes=[pltpu.VMEM(sums, jnp.float32)],
        compiler_params=params(20),
        name="project",
    )(pos, tab, pay, anoms, turned, *late)
    common = (pos, tab, gauges, anoms, turned, late_anoms, late_turned)
    carried = ()
    for step in range(ITERS):
        first, last = step == 0, step + 1 == ITERS
        args = (*common, *total_over_gauges(*parts), *carried)
        if last:
            shapes = [f32((peers, 2 * ROWS, LANES))]
            more = [pltpu.VMEM((2 * pairs + n_late, 2 * ROWS, LANES), jnp.float32)]
        else:
            shapes = [*state, *state, f32(sums), f32((ROWS, LANES)), *shards]
            shapes += [] if first else state
            more = []
        has_d = step > 1
        out = pl.pallas_call(
            functools.partial(step_kernel, shape, members, first, last if has_d or first else None),
            out_shape=shapes,
            in_specs=[smem, smem] + [vmem] * (len(args) - 2),
            out_specs=[vmem] * len(shapes),
            scratch_shapes=[
                pltpu.VMEM(sums, jnp.bfloat16),
                pltpu.VMEM(sums, jnp.bfloat16),
                pltpu.VMEM(sums, jnp.float32),
            ] + more,
            compiler_params=params(20),
            name="finish" if last else "step",
        )(*args)
        if not last:
            parts = out[6:10]
            carried = (*out[:6], *out[10:])
    back = lax.all_to_all(out[0], PEERS, 0, 0, tiled=True)
    solution_field = back[:, :ROWS, :blk].reshape(members, blk).T
    residual = back[:, ROWS:, :blk].reshape(members, blk).T
    return solution_field, residual


def solution(mesh):
    fine = Mesh(mesh.devices.reshape(8, 4, 4, 2), ("z", "x", "y", "c"))
    split_all = ("x", "y", "c", "z")
    placed = (P(split_all, None), P(split_all, None), P(split_all), P(split_all), P())
    return jax.shard_map(
        local,
        mesh=fine,
        in_specs=placed,
        out_specs=(P(split_all, None), P(split_all, None)),
        check_vma=False,
    )
```

```python
import functools

import jax
import jax.numpy as jnp
from jax import lax
from jax.experimental import pallas as pl
from jax.experimental.pallas import tpu as pltpu
from jax.sharding import Mesh
from jax.sharding import PartitionSpec as P

ITERS = 3
BASINS = 16
GROUPS = 4
far_weight = 0.3

LANES = 128
ROWS = 8
PEERS = ("y", "z")
EARLY = (0, -1, 1, -2, 2, -3, 3)


def split(v):
    high = v.astype(jnp.bfloat16)
    return high, (v - high.astype(jnp.float32)).astype(jnp.bfloat16)


def block_id(pos_ref, shape, y, step):
    nz = shape[1]
    return y * nz + lax.rem(pos_ref[1] + (step + nz), nz)


def early_blocks(shape):
    return [(y, step) for step in EARLY for y in range(shape[0])]


def late_blocks(shape):
    ny, nz = shape
    return [(y, nz // 2) for y in range(ny)]


def pack_kernel(shape, *refs):
    pos_ref, gid_ref, pay_ref = refs[:3]
    tab_ref, gauge_ref, anom_ref, turn_ref, count = refs[-5:]
    pieces = refs[3:-5]
    ny = shape[0]
    pairs = anom_ref.shape[0]
    early = early_blocks(shape)
    ids = [block_id(pos_ref, shape, *e) for e in early]
    for g in range(GROUPS):
        count[g] = 0
    for i in ids:
        g = gid_ref[i]
        count[g] = count[g] + 1
    for p in range(pairs):
        tab_ref[p] = 0
    start = jnp.int32(0)
    empty = []
    for g in range(GROUPS):
        n = count[g]
        count[g] = 2 * start

        def mark(p, carry, g=g):
            tab_ref[p] = g
            return carry

        end = start + lax.div(n + 1, 2)
        lax.fori_loop(start, end, mark, 0)
        empty.append((lax.rem(n, 2) == 1, 2 * end - 1))
        start = end

    def put(s, value):
        high, low = split(value)
        p, h = lax.div(s, 2), lax.rem(s, 2)
        first = pl.ds(pl.multiple_of(h * LANES, LANES), LANES)
        second = pl.ds(pl.multiple_of((2 + h) * LANES, LANES), LANES)
        anom_ref[p, first] = high
        anom_ref[p, second] = low
        high, low = split(value.T)
        turn_ref[p, :, first] = high
        turn_ref[p, :, second] = low

    blank = jnp.zeros((LANES, anom_ref.shape[2]), jnp.float32)
    for odd, s in empty:
        pl.when(odd)(functools.partial(put, s, blank))

    def clear(s, carry):
        put(s, blank)
        return carry

    lax.fori_loop(2 * start, 2 * pairs, clear, 0)
    gauge_ref[...] = jnp.zeros_like(gauge_ref)
    rest = blank[pieces[0].shape[1] :]
    for k, i in enumerate(ids):
        g = gid_ref[i]
        s = count[g]
        count[g] = s + 1
        tab_ref[pairs + k] = s
        gauge_ref[s] = pay_ref[i]
        put(s, jnp.concatenate([pieces[k // ny][k % ny], rest], 0))
    for k, e in enumerate(late_blocks(shape)):
        i = block_id(pos_ref, shape, *e)
        tab_ref[pairs + len(ids) + k] = gid_ref[i]
        gauge_ref[2 * pairs + k] = pay_ref[i]


class Part:
    def __init__(self, tab_ref, anom_ref, turn_ref, gauge_ref, pairs, early):
        self.count, self.width = anom_ref.shape[0], anom_ref.shape[1] // 2
        self.tab_ref, self.anom_ref, self.turn_ref = tab_ref, anom_ref, turn_ref
        self.gauge_ref = gauge_ref
        self.paired = self.width == 2 * LANES
        self.first_group = 0 if self.paired else pairs + early
        self.first_slot = 0 if self.paired else 2 * pairs

    def group(self, p):
        return self.tab_ref[self.first_group + p]

    def gauges(self, p, rows):
        if self.paired:
            return jnp.concatenate([self.gauge_ref[2 * p, rows], self.gauge_ref[2 * p + 1, rows]], 1)
        return self.gauge_ref[self.first_slot + p, rows]

    def field(self, p):
        return self.gauges(p, slice(0, ROWS))

    def obs(self, p):
        return self.gauges(p, slice(ROWS, ROWS + 1))

    def same_basin(self, p):
        basin = self.gauges(p, slice(ROWS + 1, ROWS + 2))[None]
        ids = lax.broadcasted_iota(jnp.int32, (BASINS, ROWS, self.width), 0)
        return ids.astype(jnp.float32) == basin


def project(pos_ref, parts, fields, sums, acc, outs):
    rows = BASINS * ROWS
    acc[...] = jnp.zeros_like(acc)
    for part, field in zip(parts, fields):
        width = part.width
        for p in range(part.count):
            near = part.same_basin(p)
            v = field(p)
            v_high = v.astype(jnp.bfloat16).astype(jnp.float32)
            high, low = (
                jnp.where(near, u[None], 0.0).reshape(rows, width).astype(jnp.bfloat16)
                for u in (v_high, v - v_high)
            )
            both = jnp.dot(
                jnp.concatenate([high, low], 0), part.anom_ref[p, :width],
                preferred_element_type=jnp.float32,
            )
            third = jnp.dot(high, part.anom_ref[p, width:], preferred_element_type=jnp.float32)
            g = part.group(p)
            acc[g] = acc[g] + (both[:rows] + both[rows:] + third).reshape(acc.shape[1:])
    lane = lax.broadcasted_iota(jnp.int32, (ROWS, acc.shape[3]), 1)
    row = jnp.zeros((ROWS, acc.shape[3]), jnp.float32)
    for place, value in enumerate(sums):
        row = jnp.where(lane == place, value, row)
    me_c, half = pos_ref[0], rows // 2
    for side in range(2):
        core = me_c if side == 0 else 1 - me_c
        for g in range(GROUPS):
            out = outs[2 * side + g // 2]
            out[g % 2 * half : (g % 2 + 1) * half] = acc[g, core]
        outs[2 * side][2 * half :] = row


def lane_sum(v):
    return jnp.sum(v, axis=1, keepdims=True)


def total(values):
    return functools.reduce(lambda a, b: a + b, values)


def first_kernel(shape, *refs):
    pos_ref, tab_ref, gauge_ref, anom_ref, turn_ref = refs[:5]
    late_ref, late_turn, *outs, acc = refs[-7:]
    pieces = refs[5:-7]
    pairs = anom_ref.shape[0]
    early, late = early_blocks(shape), late_blocks(shape)
    rest = jnp.zeros((LANES - pieces[0].shape[1], pieces[0].shape[2]), jnp.float32)
    half = pieces[0].shape[0]
    for k in range(len(late)):
        value = jnp.concatenate([pieces[k // half][k % half], rest], 0)
        late_ref[k, :LANES], late_ref[k, LANES:] = split(value)
        late_turn[k, :, :LANES], late_turn[k, :, LANES:] = split(value.T)
    parts = [
        Part(tab_ref, a, t, gauge_ref, pairs, len(early))
        for a, t in ((anom_ref, turn_ref), (late_ref, late_turn))
    ]
    one, two = [], []
    for part in parts:
        squares = [part.field(p) * part.field(p) for p in range(part.count)]
        one.append(lane_sum(total(squares)))
        two.append(lane_sum(total([s * part.obs(p) for p, s in enumerate(squares)])))
    fields = [part.field for part in parts]
    project(pos_ref, parts, fields, (total(one), total(two)), acc, outs)


def step_kernel(shape, members, first, last, *refs):
    refs = list(refs)

    def take(n):
        taken = refs[:n]
        del refs[:n]
        return taken

    pos_ref, tab_ref, gauge_ref, anom_ref, turn_ref, late_ref, late_turn = take(7)
    own, other = take(2), take(2)
    if not first:
        x_in, r_in, dir_in, scal_in = take(2), take(2), *take(2)
        d_in = take(0 if last is None else 2)
    if last:
        (out_ref,) = take(1)
        e_high, e_low, dir_sum, result = refs
    else:
        x_out, r_out, dir_out, scal_out, outs = take(2), take(2), *take(2), take(4)
        d_out = [] if first else take(2)
        e_high, e_low, acc = refs
        dir_sum = dir_out
    pairs = anom_ref.shape[0]
    wide = anom_ref.shape[2]
    rows = BASINS * ROWS
    early, late = early_blocks(shape), late_blocks(shape)
    parts = [
        Part(tab_ref, a, t, gauge_ref, pairs, len(early))
        for a, t in ((anom_ref, turn_ref), (late_ref, late_turn))
    ]

    me_c, half = pos_ref[0], rows // 2
    row = own[0][2 * half :]
    rr, r_obs_r, r_obs_d = row[:, 0:1], row[:, 1:2], row[:, 2:3]
    if first:
        d_obs_d = r_obs_r
    else:
        beta = rr / scal_in[:, 0:1]
        d_obs_d = r_obs_r + 2.0 * beta * r_obs_d + beta * beta * scal_in[:, 1:2]
    curve = jnp.zeros((ROWS, wide), jnp.float32)
    for g in range(GROUPS):
        halves = []
        for side, core in ((own, me_c), (other, 1 - me_c)):
            d_h = side[g // 2][g % 2 * half : (g % 2 + 1) * half].reshape(-1, ROWS, wide)
            if not first:
                d_h = d_h + beta[None] * dir_in[g, core].reshape(-1, ROWS, wide)
            dir_sum[g, core] = d_h.reshape(half, wide)
            halves.append((core, d_h))
        every = sum(jnp.sum(d_h, axis=0) for _, d_h in halves)
        for core, d_h in halves:
            e_h = (1.0 - far_weight) / (members - 1) * d_h + far_weight / (members - 1) * every[None]
            curve = curve + jnp.sum(d_h * e_h, axis=0)
            e_high[g, core], e_low[g, core] = split(e_h.reshape(half, wide))
    alpha = rr / (lane_sum(curve) + d_obs_d)

    one, two, three = [], [], []
    for k, part in enumerate(parts):
        width = part.width
        squares, weighted, crossed = [], [], []
        for p in range(part.count):
            g = part.group(p)
            e_g = e_high[g].reshape(rows, wide)
            both = jnp.dot(
                jnp.concatenate([e_g.reshape(rows, wide), e_low[g].reshape(rows, wide)], 0),
                part.turn_ref[p, :, :width],
                preferred_element_type=jnp.float32,
            )
            third = jnp.dot(
                e_g, part.turn_ref[p, :, width:], preferred_element_type=jnp.float32
            )
            every = (both[:rows] + both[rows:] + third).reshape(-1, ROWS, width)
            image = jnp.sum(jnp.where(part.same_basin(p), every, 0.0), axis=0)
            obs = part.obs(p)
            if first:
                r = part.field(p)
                d = r
            else:
                r = r_in[k][p]
                d = r + beta * (d_in[k][p] if d_in else part.field(p))
            image = image + obs * d
            x = alpha * d
            if not first:
                x = x_in[k][p] + x
            r = r - alpha * image
            if last:
                for h in range(width // LANES):
                    lanes = slice(h * LANES, (h + 1) * LANES)
                    s = part.first_slot + p * (width // LANES) + h
                    result[s, :ROWS] = x[:, lanes]
                    result[s, ROWS:] = r[:, lanes]
                continue
            x_out[k][p] = x
            r_out[k][p] = r
            if d_out:
                d_out[k][p] = d
            squares.append(r * r)
            weighted.append(r * r * obs)
            crossed.append(r * d * obs)
        if not last:
            one.append(lane_sum(total(squares)))
            two.append(lane_sum(total(weighted)))
            three.append(lane_sum(total(crossed)))
    if last:
        for k, e in enumerate(early):
            out_ref[block_id(pos_ref, shape, *e)] = result[tab_ref[pairs + k]]
        for k, e in enumerate(late):
            out_ref[block_id(pos_ref, shape, *e)] = result[2 * pairs + k]
        return
    lane = lax.broadcasted_iota(jnp.int32, (ROWS, LANES), 1)
    scal_out[...] = jnp.where(lane == 0, rr, d_obs_d)
    fields = [functools.partial(lambda ref, p: ref[p], ref) for ref in r_out]
    project(pos_ref, parts, fields, (total(one), total(two), total(three)), acc, outs)


def shift(v, axis, k):
    n = lax.axis_size(axis)
    return lax.ppermute(v, axis, [(i, (i + k) % n) for i in range(n)])


def swap(v):
    return lax.ppermute(v, "c", [(0, 1), (1, 0)])


EVEN = ((0, 1), (1, 0), (2, 3), (3, 2))
ODD = ((1, 2), (2, 1), (3, 0), (0, 3))


def meet(v, partners):
    return v + lax.ppermute(v, "x", partners)


def total_over_gauges(keep_0, keep_1, send_0, send_1):
    sum_0, sum_1 = keep_0 + swap(send_0), keep_1 + swap(send_1)
    sum_0, sum_1 = meet(sum_0, EVEN), meet(sum_1, ODD)
    sum_0, sum_1 = meet(sum_0, ODD), meet(sum_1, EVEN)
    return sum_0, sum_1, swap(sum_0), swap(sum_1)


def to_all(v, axis):
    n = lax.axis_size(axis)
    return lax.all_to_all(jnp.broadcast_to(v[None], (n,) + v.shape), axis, 0, 0, tiled=True)


def gather(anomalies):
    own = to_all(anomalies, "y")
    below, above = own, own
    early = [own]
    for _ in range((lax.axis_size("z") - 1) // 2):
        below, above = shift(below, "z", 1), shift(above, "z", -1)
        early += [below, above]
    half = own.shape[0] // 2
    return early, [shift(below[:half], "z", 1), shift(above[half:], "z", -1)]


def local(anomalies, innovations, obs_var, basins, taper_mask):
    blk, members = anomalies.shape
    shape = tuple(lax.axis_size(a) for a in PEERS)
    peers = shape[0] * shape[1]
    nx, nc = lax.axis_size("x"), lax.axis_size("c")
    me_x, me_c = lax.axis_index("x"), lax.axis_index("c")
    nblocks = taper_mask.shape[0]

    near = taper_mask != 0
    place = jnp.arange(nblocks, dtype=jnp.int32)
    leader = jnp.min(jnp.where(near, place[None, :], nblocks), axis=1)
    leads = (leader == place)[None, :] & (place[None, :] < leader[:, None])
    gid = jnp.sum(leads.astype(jnp.int32), axis=1)
    gid = gid.reshape(nx, shape[0], nc, shape[1])
    gid = lax.dynamic_slice(gid, (me_x, 0, me_c, 0), (1, shape[0], 1, shape[1])).reshape(peers)
    gid = jnp.minimum(gid, GROUPS - 1)
    pos = jnp.stack([me_c, lax.axis_index("z")]).astype(jnp.int32)

    early, late = gather(anomalies)
    lanes = ((0, 0), (0, LANES - blk))
    field = jnp.pad(innovations.T, lanes).reshape(peers, ROWS, LANES)
    extra = jnp.stack([obs_var, basins.astype(jnp.float32)])
    extra = jnp.pad(extra, ((0, ROWS - 2), (0, LANES - blk)))
    pay = jnp.concatenate([field, jnp.broadcast_to(extra[None], (peers, ROWS, LANES))], 1)
    pay = lax.all_to_all(pay, PEERS, 0, 0, tiled=True)

    smem = pl.BlockSpec(memory_space=pltpu.SMEM)
    vmem = pl.BlockSpec(memory_space=pltpu.VMEM)
    f32 = functools.partial(jax.ShapeDtypeStruct, dtype=jnp.float32)
    b16 = functools.partial(jax.ShapeDtypeStruct, dtype=jnp.bfloat16)
    rows = BASINS * ROWS
    n_late = shape[0]
    n_early = peers - n_late
    pairs = (n_early + GROUPS) // 2
    shards = [f32((rows + ROWS, members)), f32((rows, members))] * 2
    state = [f32((pairs, ROWS, 2 * LANES)), f32((n_late, ROWS, LANES))]
    sums = (GROUPS, 2, rows // 2, members)

    def params(mib):
        return pltpu.CompilerParams(vmem_limit_bytes=mib * 2**20)

    tab, gauges, anoms, turned = pl.pallas_call(
        functools.partial(pack_kernel, shape),
        out_shape=(
            jax.ShapeDtypeStruct((pairs + peers,), jnp.int32),
            f32((2 * pairs + n_late, 2 * ROWS, LANES)),
            b16((pairs, 4 * LANES, members)),
            b16((pairs, members, 4 * LANES)),
        ),
        in_specs=[smem, smem] + [vmem] * (1 + len(early)),
        out_specs=(smem, vmem, vmem, vmem),
        scratch_shapes=[pltpu.SMEM((GROUPS,), jnp.int32)],
        compiler_params=params(20),
        cost_estimate=pl.CostEstimate(
            flops=n_early * blk * members * 8, bytes_accessed=n_early * blk * members * 12,
            transcendentals=0,
        ),
        name="pack",
    )(pos, gid, pay, *early)
    late_anoms, late_turned, *parts = pl.pallas_call(
        functools.partial(first_kernel, shape),
        out_shape=(
            b16((n_late, 2 * LANES, members)),
            b16((n_late, members, 2 * LANES)),
            *shards,
        ),
        in_specs=[smem, smem] + [vmem] * (3 + len(late)),
        out_specs=(vmem,) * 6,
        scratch_shapes=[pltpu.VMEM(sums, jnp.float32)],
        compiler_params=params(20),
        name="project",
    )(pos, tab, gauges, anoms, turned, *late)
    common = (pos, tab, gauges, anoms, turned, late_anoms, late_turned)
    carried = ()
    for step in range(ITERS):
        first, last = step == 0, step + 1 == ITERS
        args = (*common, *total_over_gauges(*parts), *carried)
        if last:
            shapes = [f32((peers, 2 * ROWS, LANES))]
            more = [pltpu.VMEM((2 * pairs + n_late, 2 * ROWS, LANES), jnp.float32)]
        else:
            shapes = [*state, *state, f32(sums), f32((ROWS, LANES)), *shards]
            shapes += [] if first else state
            more = []
        has_d = step > 1
        out = pl.pallas_call(
            functools.partial(step_kernel, shape, members, first, last if has_d or first else None),
            out_shape=shapes,
            in_specs=[smem, smem] + [vmem] * (len(args) - 2),
            out_specs=[vmem] * len(shapes),
            scratch_shapes=[
                pltpu.VMEM(sums, jnp.bfloat16),
                pltpu.VMEM(sums, jnp.bfloat16),
                pltpu.VMEM(sums, jnp.float32),
            ] + more,
            compiler_params=params(20),
            name="finish" if last else "step",
        )(*args)
        if not last:
            parts = out[6:10]
            carried = (*out[:6], *out[10:])
    back = lax.all_to_all(out[0], PEERS, 0, 0, tiled=True)
    solution_field = back[:, :ROWS, :blk].reshape(members, blk).T
    residual = back[:, ROWS:, :blk].reshape(members, blk).T
    return solution_field, residual


def solution(mesh):
    fine = Mesh(mesh.devices.reshape(8, 4, 4, 2), ("z", "x", "y", "c"))
    split_all = ("x", "y", "c", "z")
    placed = (P(split_all, None), P(split_all, None), P(split_all), P(split_all), P())
    return jax.shard_map(
        local,
        mesh=fine,
        in_specs=placed,
        out_specs=(P(split_all, None), P(split_all, None)),
        check_vma=False,
    )
```

```python
import functools

import jax
import jax.numpy as jnp
from jax import lax
from jax.experimental import pallas as pl
from jax.experimental.pallas import tpu as pltpu
from jax.sharding import Mesh
from jax.sharding import PartitionSpec as P

ITERS = 3
BASINS = 16
GROUPS = 4
far_weight = 0.3

LANES = 128
ROWS = 8
PEERS = ("y", "z")
EARLY = (0, -1, 1, -2, 2, -3, 3)


def split(v):
    high = v.astype(jnp.bfloat16)
    return high, (v - high.astype(jnp.float32)).astype(jnp.bfloat16)


def block_id(pos_ref, shape, y, step):
    nz = shape[1]
    return y * nz + lax.rem(pos_ref[1] + (step + nz), nz)


def early_blocks(shape):
    return [(y, step) for step in EARLY for y in range(shape[0])]


def late_blocks(shape):
    ny, nz = shape
    return [(y, nz // 2) for y in range(ny)]


def pack_kernel(shape, *refs):
    pos_ref, gid_ref, pay_ref = refs[:3]
    tab_ref, gauge_ref, anom_ref, turn_ref, count = refs[-5:]
    pieces = refs[3:-5]
    ny = shape[0]
    pairs = anom_ref.shape[0]
    early = early_blocks(shape)
    ids = [block_id(pos_ref, shape, *e) for e in early]
    for g in range(GROUPS):
        count[g] = 0
    for i in ids:
        g = gid_ref[i]
        count[g] = count[g] + 1
    for p in range(pairs):
        tab_ref[p] = 0
    start = jnp.int32(0)
    empty = []
    for g in range(GROUPS):
        n = count[g]
        count[g] = 2 * start

        def mark(p, carry, g=g):
            tab_ref[p] = g
            return carry

        end = start + lax.div(n + 1, 2)
        lax.fori_loop(start, end, mark, 0)
        empty.append((lax.rem(n, 2) == 1, 2 * end - 1))
        start = end

    def put(s, value):
        high, low = split(value)
        p, h = lax.div(s, 2), lax.rem(s, 2)
        first = pl.ds(pl.multiple_of(h * LANES, LANES), LANES)
        second = pl.ds(pl.multiple_of((2 + h) * LANES, LANES), LANES)
        anom_ref[p, first] = high
        anom_ref[p, second] = low
        high, low = split(value.T)
        turn_ref[p, :, first] = high
        turn_ref[p, :, second] = low

    blank = jnp.zeros((LANES, anom_ref.shape[2]), jnp.float32)
    for odd, s in empty:
        pl.when(odd)(functools.partial(put, s, blank))

    def clear(s, carry):
        put(s, blank)
        return carry

    lax.fori_loop(2 * start, 2 * pairs, clear, 0)
    gauge_ref[...] = jnp.zeros_like(gauge_ref)
    rest = blank[pieces[0].shape[1] :]
    for k, i in enumerate(ids):
        g = gid_ref[i]
        s = count[g]
        count[g] = s + 1
        tab_ref[pairs + k] = s
        gauge_ref[s] = pay_ref[i]
        put(s, jnp.concatenate([pieces[k // ny][k % ny], rest], 0))
    for k, e in enumerate(late_blocks(shape)):
        i = block_id(pos_ref, shape, *e)
        tab_ref[pairs + len(ids) + k] = gid_ref[i]
        gauge_ref[2 * pairs + k] = pay_ref[i]


class Part:
    def __init__(self, tab_ref, anom_ref, turn_ref, gauge_ref, pairs, early):
        self.count, self.width = anom_ref.shape[0], anom_ref.shape[1] // 2
        self.tab_ref, self.anom_ref, self.turn_ref = tab_ref, anom_ref, turn_ref
        self.gauge_ref = gauge_ref
        self.paired = self.width == 2 * LANES
        self.first_group = 0 if self.paired else pairs + early
        self.first_slot = 0 if self.paired else 2 * pairs

    def group(self, p):
        return self.tab_ref[self.first_group + p]

    def gauges(self, p, rows):
        if self.paired:
            return jnp.concatenate([self.gauge_ref[2 * p, rows], self.gauge_ref[2 * p + 1, rows]], 1)
        return self.gauge_ref[self.first_slot + p, rows]

    def field(self, p):
        return self.gauges(p, slice(0, ROWS))

    def obs(self, p):
        return self.gauges(p, slice(ROWS, ROWS + 1))

    def same_basin(self, p):
        basin = self.gauges(p, slice(ROWS + 1, ROWS + 2))[None]
        ids = lax.broadcasted_iota(jnp.int32, (BASINS, ROWS, self.width), 0)
        return ids.astype(jnp.float32) == basin


def project(pos_ref, parts, fields, sums, acc, outs):
    rows = BASINS * ROWS
    acc[...] = jnp.zeros_like(acc)
    for part, field in zip(parts, fields):
        width = part.width
        for p in range(part.count):
            near = part.same_basin(p)
            v = field(p)
            v_high = v.astype(jnp.bfloat16).astype(jnp.float32)
            high, low = (
                jnp.where(near, u[None], 0.0).reshape(rows, width).astype(jnp.bfloat16)
                for u in (v_high, v - v_high)
            )
            both = jnp.dot(
                jnp.concatenate([high, low], 0), part.anom_ref[p, :width],
                preferred_element_type=jnp.float32,
            )
            third = jnp.dot(high, part.anom_ref[p, width:], preferred_element_type=jnp.float32)
            g = part.group(p)
            acc[g] = acc[g] + (both[:rows] + both[rows:] + third).reshape(acc.shape[1:])
    lane = lax.broadcasted_iota(jnp.int32, (ROWS, acc.shape[3]), 1)
    row = jnp.zeros((ROWS, acc.shape[3]), jnp.float32)
    for place, value in enumerate(sums):
        row = jnp.where(lane == place, value, row)
    me_c, half = pos_ref[0], rows // 2
    for out, core in zip(outs, (me_c, 1 - me_c)):
        for g in range(GROUPS):
            out[g * half : (g + 1) * half] = acc[g, core]
        out[GROUPS * half :] = row


def lane_sum(v):
    return jnp.sum(v, axis=1, keepdims=True)


def total(values):
    return functools.reduce(lambda a, b: a + b, values)


def first_kernel(shape, *refs):
    pos_ref, tab_ref, gauge_ref, anom_ref, turn_ref = refs[:5]
    late_ref, late_turn, *outs, acc = refs[-5:]
    pieces = refs[5:-5]
    pairs = anom_ref.shape[0]
    early, late = early_blocks(shape), late_blocks(shape)
    rest = jnp.zeros((LANES - pieces[0].shape[1], pieces[0].shape[2]), jnp.float32)
    half = pieces[0].shape[0]
    for k in range(len(late)):
        value = jnp.concatenate([pieces[k // half][k % half], rest], 0)
        late_ref[k, :LANES], late_ref[k, LANES:] = split(value)
        late_turn[k, :, :LANES], late_turn[k, :, LANES:] = split(value.T)
    parts = [
        Part(tab_ref, a, t, gauge_ref, pairs, len(early))
        for a, t in ((anom_ref, turn_ref), (late_ref, late_turn))
    ]
    one, two = [], []
    for part in parts:
        squares = [part.field(p) * part.field(p) for p in range(part.count)]
        one.append(lane_sum(total(squares)))
        two.append(lane_sum(total([s * part.obs(p) for p, s in enumerate(squares)])))
    fields = [part.field for part in parts]
    project(pos_ref, parts, fields, (total(one), total(two)), acc, outs)


def step_kernel(shape, members, first, last, *refs):
    refs = list(refs)

    def take(n):
        taken = refs[:n]
        del refs[:n]
        return taken

    pos_ref, tab_ref, gauge_ref, anom_ref, turn_ref, late_ref, late_turn = take(7)
    own, other = take(2)
    if not first:
        x_in, r_in, dir_in, scal_in = take(2), take(2), *take(2)
        d_in = take(0 if last is None else 2)
    if last:
        (out_ref,) = take(1)
        e_high, e_low, dir_sum, result = refs
    else:
        x_out, r_out, dir_out, scal_out, outs = take(2), take(2), *take(2), take(2)
        d_out = [] if first else take(2)
        e_high, e_low, acc = refs
        dir_sum = dir_out
    pairs = anom_ref.shape[0]
    wide = anom_ref.shape[2]
    rows = BASINS * ROWS
    early, late = early_blocks(shape), late_blocks(shape)
    parts = [
        Part(tab_ref, a, t, gauge_ref, pairs, len(early))
        for a, t in ((anom_ref, turn_ref), (late_ref, late_turn))
    ]

    me_c, half = pos_ref[0], rows // 2
    row = own[GROUPS * half :]
    rr, r_obs_r, r_obs_d = row[:, 0:1], row[:, 1:2], row[:, 2:3]
    if first:
        d_obs_d = r_obs_r
    else:
        beta = rr / scal_in[:, 0:1]
        d_obs_d = r_obs_r + 2.0 * beta * r_obs_d + beta * beta * scal_in[:, 1:2]
    curve = jnp.zeros((ROWS, wide), jnp.float32)
    for g in range(GROUPS):
        halves = []
        for side, core in ((own, me_c), (other, 1 - me_c)):
            d_h = side[g * half : (g + 1) * half].reshape(-1, ROWS, wide)
            if not first:
                d_h = d_h + beta[None] * dir_in[g, core].reshape(-1, ROWS, wide)
            dir_sum[g, core] = d_h.reshape(half, wide)
            halves.append((core, d_h))
        every = sum(jnp.sum(d_h, axis=0) for _, d_h in halves)
        for core, d_h in halves:
            e_h = (1.0 - far_weight) / (members - 1) * d_h + far_weight / (members - 1) * every[None]
            curve = curve + jnp.sum(d_h * e_h, axis=0)
            e_high[g, core], e_low[g, core] = split(e_h.reshape(half, wide))
    alpha = rr / (lane_sum(curve) + d_obs_d)

    one, two, three = [], [], []
    for k, part in enumerate(parts):
        width = part.width
        squares, weighted, crossed = [], [], []
        for p in range(part.count):
            g = part.group(p)
            e_g = e_high[g].reshape(rows, wide)
            both = jnp.dot(
                jnp.concatenate([e_g.reshape(rows, wide), e_low[g].reshape(rows, wide)], 0),
                part.turn_ref[p, :, :width],
                preferred_element_type=jnp.float32,
            )
            third = jnp.dot(
                e_g, part.turn_ref[p, :, width:], preferred_element_type=jnp.float32
            )
            every = (both[:rows] + both[rows:] + third).reshape(-1, ROWS, width)
            image = jnp.sum(jnp.where(part.same_basin(p), every, 0.0), axis=0)
            obs = part.obs(p)
            if first:
                r = part.field(p)
                d = r
            else:
                r = r_in[k][p]
                d = r + beta * (d_in[k][p] if d_in else part.field(p))
            image = image + obs * d
            x = alpha * d
            if not first:
                x = x_in[k][p] + x
            r = r - alpha * image
            if last:
                for h in range(width // LANES):
                    lanes = slice(h * LANES, (h + 1) * LANES)
                    s = part.first_slot + p * (width // LANES) + h
                    result[s, :ROWS] = x[:, lanes]
                    result[s, ROWS:] = r[:, lanes]
                continue
            x_out[k][p] = x
            r_out[k][p] = r
            if d_out:
                d_out[k][p] = d
            squares.append(r * r)
            weighted.append(r * r * obs)
            crossed.append(r * d * obs)
        if not last:
            one.append(lane_sum(total(squares)))
            two.append(lane_sum(total(weighted)))
            three.append(lane_sum(total(crossed)))
    if last:
        for k, e in enumerate(early):
            out_ref[block_id(pos_ref, shape, *e)] = result[tab_ref[pairs + k]]
        for k, e in enumerate(late):
            out_ref[block_id(pos_ref, shape, *e)] = result[2 * pairs + k]
        return
    lane = lax.broadcasted_iota(jnp.int32, (ROWS, LANES), 1)
    scal_out[...] = jnp.where(lane == 0, rr, d_obs_d)
    fields = [functools.partial(lambda ref, p: ref[p], ref) for ref in r_out]
    project(pos_ref, parts, fields, (total(one), total(two), total(three)), acc, outs)


def shift(v, axis, k):
    n = lax.axis_size(axis)
    return lax.ppermute(v, axis, [(i, (i + k) % n) for i in range(n)])


def swap(v):
    return lax.ppermute(v, "c", [(0, 1), (1, 0)])


def meet(v, step):
    nx, nc = lax.axis_size("x"), lax.axis_size("c")

    def partner(x, c):
        forward = (x + c + step) % 2 == 0
        return (x + (1 if forward else -1)) % nx * nc + c

    pairs = [(x * nc + c, partner(x, c)) for x in range(nx) for c in range(nc)]
    return v + lax.ppermute(v, ("x", "c"), pairs)


def total_over_gauges(keep, send):
    mine = meet(meet(keep + swap(send), 0), 1)
    return mine, swap(mine)


def to_all(v, axis):
    n = lax.axis_size(axis)
    return lax.all_to_all(jnp.broadcast_to(v[None], (n,) + v.shape), axis, 0, 0, tiled=True)


def gather(anomalies, pay):
    own = to_all(anomalies, "y")
    pay = lax.all_to_all(pay, PEERS, 0, 0, tiled=True)
    below, above = own, own
    early = [own]
    for step in range((lax.axis_size("z") - 1) // 2):
        if step == 2:
            below, above, pay = lax.optimization_barrier((below, above, pay))
        below, above = shift(below, "z", 1), shift(above, "z", -1)
        early += [below, above]
    half = own.shape[0] // 2
    return early, [shift(below[:half], "z", 1), shift(above[half:], "z", -1)], pay


def local(anomalies, innovations, obs_var, basins, taper_mask):
    blk, members = anomalies.shape
    shape = tuple(lax.axis_size(a) for a in PEERS)
    peers = shape[0] * shape[1]
    nx, nc = lax.axis_size("x"), lax.axis_size("c")
    me_x, me_c = lax.axis_index("x"), lax.axis_index("c")
    nblocks = taper_mask.shape[0]

    near = taper_mask != 0
    place = jnp.arange(nblocks, dtype=jnp.int32)
    leader = jnp.min(jnp.where(near, place[None, :], nblocks), axis=1)
    leads = (leader == place)[None, :] & (place[None, :] < leader[:, None])
    gid = jnp.sum(leads.astype(jnp.int32), axis=1)
    gid = gid.reshape(nx, shape[0], nc, shape[1])
    gid = lax.dynamic_slice(gid, (me_x, 0, me_c, 0), (1, shape[0], 1, shape[1])).reshape(peers)
    gid = jnp.minimum(gid, GROUPS - 1)
    pos = jnp.stack([me_c, lax.axis_index("z")]).astype(jnp.int32)

    lanes = ((0, 0), (0, LANES - blk))
    field = jnp.pad(innovations.T, lanes).reshape(peers, ROWS, LANES)
    extra = jnp.stack([obs_var, basins.astype(jnp.float32)])
    extra = jnp.pad(extra, ((0, ROWS - 2), (0, LANES - blk)))
    pay = jnp.concatenate([field, jnp.broadcast_to(extra[None], (peers, ROWS, LANES))], 1)
    early, late, pay = gather(anomalies, pay)

    smem = pl.BlockSpec(memory_space=pltpu.SMEM)
    vmem = pl.BlockSpec(memory_space=pltpu.VMEM)
    f32 = functools.partial(jax.ShapeDtypeStruct, dtype=jnp.float32)
    b16 = functools.partial(jax.ShapeDtypeStruct, dtype=jnp.bfloat16)
    rows = BASINS * ROWS
    n_late = shape[0]
    n_early = peers - n_late
    pairs = (n_early + GROUPS) // 2
    shards = [f32((2 * rows + ROWS, members))] * 2
    state = [f32((pairs, ROWS, 2 * LANES)), f32((n_late, ROWS, LANES))]
    sums = (GROUPS, 2, rows // 2, members)

    def params(mib):
        return pltpu.CompilerParams(vmem_limit_bytes=mib * 2**20)

    tab, gauges, anoms, turned = pl.pallas_call(
        functools.partial(pack_kernel, shape),
        out_shape=(
            jax.ShapeDtypeStruct((pairs + peers,), jnp.int32),
            f32((2 * pairs + n_late, 2 * ROWS, LANES)),
            b16((pairs, 4 * LANES, members)),
            b16((pairs, members, 4 * LANES)),
        ),
        in_specs=[smem, smem] + [vmem] * (1 + len(early)),
        out_specs=(smem, vmem, vmem, vmem),
        scratch_shapes=[pltpu.SMEM((GROUPS,), jnp.int32)],
        compiler_params=params(20),
        cost_estimate=pl.CostEstimate(
            flops=n_early * blk * members * 8, bytes_accessed=n_early * blk * members * 12,
            transcendentals=0,
        ),
        name="pack",
    )(pos, gid, pay, *early)
    late_anoms, late_turned, *parts = pl.pallas_call(
        functools.partial(first_kernel, shape),
        out_shape=(
            b16((n_late, 2 * LANES, members)),
            b16((n_late, members, 2 * LANES)),
            *shards,
        ),
        in_specs=[smem, smem] + [vmem] * (3 + len(late)),
        out_specs=(vmem,) * 4,
        scratch_shapes=[pltpu.VMEM(sums, jnp.float32)],
        compiler_params=params(20),
        name="project",
    )(pos, tab, gauges, anoms, turned, *late)
    common = (pos, tab, gauges, anoms, turned, late_anoms, late_turned)
    carried = ()
    for step in range(ITERS):
        first, last = step == 0, step + 1 == ITERS
        args = (*common, *total_over_gauges(*parts), *carried)
        if last:
            shapes = [f32((peers, 2 * ROWS, LANES))]
            more = [pltpu.VMEM((2 * pairs + n_late, 2 * ROWS, LANES), jnp.float32)]
        else:
            shapes = [*state, *state, f32(sums), f32((ROWS, LANES)), *shards]
            shapes += [] if first else state
            more = []
        has_d = step > 1
        out = pl.pallas_call(
            functools.partial(step_kernel, shape, members, first, last if has_d or first else None),
            out_shape=shapes,
            in_specs=[smem, smem] + [vmem] * (len(args) - 2),
            out_specs=[vmem] * len(shapes),
            scratch_shapes=[
                pltpu.VMEM(sums, jnp.bfloat16),
                pltpu.VMEM(sums, jnp.bfloat16),
                pltpu.VMEM(sums, jnp.float32),
            ] + more,
            compiler_params=params(20),
            name="finish" if last else "step",
        )(*args)
        if not last:
            parts = out[6:8]
            carried = (*out[:6], *out[8:])
    back = lax.all_to_all(out[0], PEERS, 0, 0, tiled=True)
    solution_field = back[:, :ROWS, :blk].reshape(members, blk).T
    residual = back[:, ROWS:, :blk].reshape(members, blk).T
    return solution_field, residual


def solution(mesh):
    fine = Mesh(mesh.devices.reshape(8, 4, 4, 2), ("z", "x", "y", "c"))
    split_all = ("x", "y", "c", "z")
    placed = (P(split_all, None), P(split_all, None), P(split_all), P(split_all), P())
    return jax.shard_map(
        local,
        mesh=fine,
        in_specs=placed,
        out_specs=(P(split_all, None), P(split_all, None)),
        check_vma=False,
    )
```

```python
import functools

import jax
import jax.numpy as jnp
from jax import lax
from jax.experimental import pallas as pl
from jax.experimental.pallas import tpu as pltpu
from jax.sharding import Mesh
from jax.sharding import PartitionSpec as P

ITERS = 3
BASINS = 16
GROUPS = 4
far_weight = 0.3

LANES = 128
ROWS = 8
PEERS = ("y", "z")
EARLY = (0, -1, 1, -2, 2, -3, 3)


def split(v):
    high = v.astype(jnp.bfloat16)
    return high, (v - high.astype(jnp.float32)).astype(jnp.bfloat16)


def block_id(pos_ref, shape, y, step):
    nz = shape[1]
    return y * nz + lax.rem(pos_ref[1] + (step + nz), nz)


def early_blocks(shape):
    return [(y, step) for step in EARLY for y in range(shape[0])]


def late_blocks(shape):
    ny, nz = shape
    return [(y, nz // 2) for y in range(ny)]


def pack_kernel(shape, *refs):
    pos_ref, gid_ref, pay_ref = refs[:3]
    tab_ref, gauge_ref, anom_ref, count = refs[-4:]
    pieces = refs[3:-4]
    ny = shape[0]
    pairs = anom_ref.shape[0]
    early = early_blocks(shape)
    ids = [block_id(pos_ref, shape, *e) for e in early]
    for g in range(GROUPS):
        count[g] = 0
    for i in ids:
        g = gid_ref[i]
        count[g] = count[g] + 1
    for p in range(pairs):
        tab_ref[p] = 0
    start = jnp.int32(0)
    empty = []
    for g in range(GROUPS):
        n = count[g]
        count[g] = 2 * start

        def mark(p, carry, g=g):
            tab_ref[p] = g
            return carry

        end = start + lax.div(n + 1, 2)
        lax.fori_loop(start, end, mark, 0)
        empty.append((lax.rem(n, 2) == 1, 2 * end - 1))
        start = end

    def put(s, value):
        high, low = split(value)
        p, h = lax.div(s, 2), lax.rem(s, 2)
        anom_ref[p, pl.ds(pl.multiple_of(h * LANES, LANES), LANES)] = high
        anom_ref[p, pl.ds(pl.multiple_of((2 + h) * LANES, LANES), LANES)] = low

    blank = jnp.zeros((LANES, anom_ref.shape[2]), jnp.float32)
    for odd, s in empty:
        pl.when(odd)(functools.partial(put, s, blank))

    def clear(s, carry):
        put(s, blank)
        return carry

    lax.fori_loop(2 * start, 2 * pairs, clear, 0)
    gauge_ref[...] = jnp.zeros_like(gauge_ref)
    rest = blank[pieces[0].shape[1] :]
    for k, i in enumerate(ids):
        g = gid_ref[i]
        s = count[g]
        count[g] = s + 1
        tab_ref[pairs + k] = s
        gauge_ref[s] = pay_ref[i]
        put(s, jnp.concatenate([pieces[k // ny][k % ny], rest], 0))
    for k, e in enumerate(late_blocks(shape)):
        i = block_id(pos_ref, shape, *e)
        tab_ref[pairs + len(ids) + k] = gid_ref[i]
        gauge_ref[2 * pairs + k] = pay_ref[i]


def turn_kernel(anom_ref, late_ref, turn_ref, late_turn):
    for ref, out in ((anom_ref, turn_ref), (late_ref, late_turn)):
        width = ref.shape[1] // 2
        for p in range(ref.shape[0]):
            for h in range(2):
                part = slice(h * width, (h + 1) * width)
                out[p, :, part] = ref[p, part].T


def out_kernel(back_ref, x_ref, r_ref):
    for out, rows in ((x_ref, slice(0, ROWS)), (r_ref, slice(ROWS, 2 * ROWS))):
        for k in range(0, back_ref.shape[0], LANES // ROWS):
            tile = back_ref[k : k + LANES // ROWS, rows].reshape(LANES, LANES).T
            out[:, k * ROWS : k * ROWS + LANES] = tile[: out.shape[0]]


class Part:
    def __init__(self, tab_ref, anom_ref, turn_ref, gauge_ref, pairs, early):
        self.count, self.width = anom_ref.shape[0], anom_ref.shape[1] // 2
        self.tab_ref, self.anom_ref, self.turn_ref = tab_ref, anom_ref, turn_ref
        self.gauge_ref = gauge_ref
        self.paired = self.width == 2 * LANES
        self.first_group = 0 if self.paired else pairs + early
        self.first_slot = 0 if self.paired else 2 * pairs

    def group(self, p):
        return self.tab_ref[self.first_group + p]

    def gauges(self, p, rows):
        if self.paired:
            return jnp.concatenate([self.gauge_ref[2 * p, rows], self.gauge_ref[2 * p + 1, rows]], 1)
        return self.gauge_ref[self.first_slot + p, rows]

    def field(self, p):
        return self.gauges(p, slice(0, ROWS))

    def obs(self, p):
        return self.gauges(p, slice(ROWS, ROWS + 1))

    def same_basin(self, p):
        basin = self.gauges(p, slice(ROWS + 1, ROWS + 2))[None]
        ids = lax.broadcasted_iota(jnp.int32, (BASINS, ROWS, self.width), 0)
        return ids.astype(jnp.float32) == basin


def project(pos_ref, parts, fields, sums, acc, outs):
    rows = BASINS * ROWS
    acc[...] = jnp.zeros_like(acc)
    for part, field in zip(parts, fields):
        width = part.width
        for p in range(part.count):
            near = part.same_basin(p)
            v = field(p)
            v_high = v.astype(jnp.bfloat16).astype(jnp.float32)
            high, low = (
                jnp.where(near, u[None], 0.0).reshape(rows, width).astype(jnp.bfloat16)
                for u in (v_high, v - v_high)
            )
            both = jnp.dot(
                jnp.concatenate([high, low], 0), part.anom_ref[p, :width],
                preferred_element_type=jnp.float32,
            )
            third = jnp.dot(high, part.anom_ref[p, width:], preferred_element_type=jnp.float32)
            g = part.group(p)
            acc[g] = acc[g] + (both[:rows] + both[rows:] + third).reshape(acc.shape[1:])
    lane = lax.broadcasted_iota(jnp.int32, (ROWS, acc.shape[3]), 1)
    row = jnp.zeros((ROWS, acc.shape[3]), jnp.float32)
    for place, value in enumerate(sums):
        row = jnp.where(lane == place, value, row)
    me_c, half = pos_ref[0], rows // 2
    for side in range(2):
        core = me_c if side == 0 else 1 - me_c
        for g in range(GROUPS):
            out = outs[2 * side + g // 2]
            out[g % 2 * half : (g % 2 + 1) * half] = acc[g, core]
        outs[2 * side][2 * half :] = row


def lane_sum(v):
    return jnp.sum(v, axis=1, keepdims=True)


def total(values):
    return functools.reduce(lambda a, b: a + b, values)


def first_kernel(shape, *refs):
    pos_ref, tab_ref, gauge_ref, anom_ref = refs[:4]
    late_ref, *outs, acc = refs[-6:]
    pieces = refs[4:-6]
    pairs = anom_ref.shape[0]
    early, late = early_blocks(shape), late_blocks(shape)
    rest = jnp.zeros((LANES - pieces[0].shape[1], pieces[0].shape[2]), jnp.float32)
    half = pieces[0].shape[0]
    for k in range(len(late)):
        value = jnp.concatenate([pieces[k // half][k % half], rest], 0)
        late_ref[k, :LANES], late_ref[k, LANES:] = split(value)
    parts = [
        Part(tab_ref, a, t, gauge_ref, pairs, len(early))
        for a, t in ((anom_ref, None), (late_ref, None))
    ]
    one, two = [], []
    for part in parts:
        squares = [part.field(p) * part.field(p) for p in range(part.count)]
        one.append(lane_sum(total(squares)))
        two.append(lane_sum(total([s * part.obs(p) for p, s in enumerate(squares)])))
    fields = [part.field for part in parts]
    project(pos_ref, parts, fields, (total(one), total(two)), acc, outs)


def step_kernel(shape, members, first, last, *refs):
    refs = list(refs)

    def take(n):
        taken = refs[:n]
        del refs[:n]
        return taken

    pos_ref, tab_ref, gauge_ref, anom_ref, turn_ref, late_ref, late_turn = take(7)
    own, other = take(2), take(2)
    if not first:
        x_in, r_in, dir_in, scal_in = take(2), take(2), *take(2)
        d_in = take(0 if last is None else 2)
    if last:
        (out_ref,) = take(1)
        e_high, e_low, dir_sum, result = refs
    else:
        x_out, r_out, dir_out, scal_out, outs = take(2), take(2), *take(2), take(4)
        d_out = [] if first else take(2)
        e_high, e_low, acc = refs
        dir_sum = dir_out
    pairs = anom_ref.shape[0]
    wide = anom_ref.shape[2]
    rows = BASINS * ROWS
    early, late = early_blocks(shape), late_blocks(shape)
    parts = [
        Part(tab_ref, a, t, gauge_ref, pairs, len(early))
        for a, t in ((anom_ref, turn_ref), (late_ref, late_turn))
    ]

    me_c, half = pos_ref[0], rows // 2
    row = own[0][2 * half :]
    rr, r_obs_r, r_obs_d = row[:, 0:1], row[:, 1:2], row[:, 2:3]
    if first:
        d_obs_d = r_obs_r
    else:
        beta = rr / scal_in[:, 0:1]
        d_obs_d = r_obs_r + 2.0 * beta * r_obs_d + beta * beta * scal_in[:, 1:2]
    curve = jnp.zeros((ROWS, wide), jnp.float32)
    for g in range(GROUPS):
        halves = []
        for side, core in ((own, me_c), (other, 1 - me_c)):
            d_h = side[g // 2][g % 2 * half : (g % 2 + 1) * half].reshape(-1, ROWS, wide)
            if not first:
                d_h = d_h + beta[None] * dir_in[g, core].reshape(-1, ROWS, wide)
            dir_sum[g, core] = d_h.reshape(half, wide)
            halves.append((core, d_h))
        every = sum(jnp.sum(d_h, axis=0) for _, d_h in halves)
        for core, d_h in halves:
            e_h = (1.0 - far_weight) / (members - 1) * d_h + far_weight / (members - 1) * every[None]
            curve = curve + jnp.sum(d_h * e_h, axis=0)
            e_high[g, core], e_low[g, core] = split(e_h.reshape(half, wide))
    alpha = rr / (lane_sum(curve) + d_obs_d)

    one, two, three = [], [], []
    for k, part in enumerate(parts):
        width = part.width
        squares, weighted, crossed = [], [], []
        for p in range(part.count):
            g = part.group(p)
            e_g = e_high[g].reshape(rows, wide)
            both = jnp.dot(
                jnp.concatenate([e_g.reshape(rows, wide), e_low[g].reshape(rows, wide)], 0),
                part.turn_ref[p, :, :width],
                preferred_element_type=jnp.float32,
            )
            third = jnp.dot(
                e_g, part.turn_ref[p, :, width:], preferred_element_type=jnp.float32
            )
            every = (both[:rows] + both[rows:] + third).reshape(-1, ROWS, width)
            image = jnp.sum(jnp.where(part.same_basin(p), every, 0.0), axis=0)
            obs = part.obs(p)
            if first:
                r = part.field(p)
                d = r
            else:
                r = r_in[k][p]
                d = r + beta * (d_in[k][p] if d_in else part.field(p))
            image = image + obs * d
            x = alpha * d
            if not first:
                x = x_in[k][p] + x
            r = r - alpha * image
            if last:
                for h in range(width // LANES):
                    lanes = slice(h * LANES, (h + 1) * LANES)
                    s = part.first_slot + p * (width // LANES) + h
                    result[s, :ROWS] = x[:, lanes]
                    result[s, ROWS:] = r[:, lanes]
                continue
            x_out[k][p] = x
            r_out[k][p] = r
            if d_out:
                d_out[k][p] = d
            squares.append(r * r)
            weighted.append(r * r * obs)
            crossed.append(r * d * obs)
        if not last:
            one.append(lane_sum(total(squares)))
            two.append(lane_sum(total(weighted)))
            three.append(lane_sum(total(crossed)))
    if last:
        for k, e in enumerate(early):
            out_ref[block_id(pos_ref, shape, *e)] = result[tab_ref[pairs + k]]
        for k, e in enumerate(late):
            out_ref[block_id(pos_ref, shape, *e)] = result[2 * pairs + k]
        return
    lane = lax.broadcasted_iota(jnp.int32, (ROWS, LANES), 1)
    scal_out[...] = jnp.where(lane == 0, rr, d_obs_d)
    fields = [functools.partial(lambda ref, p: ref[p], ref) for ref in r_out]
    project(pos_ref, parts, fields, (total(one), total(two), total(three)), acc, outs)


def shift(v, axis, k):
    n = lax.axis_size(axis)
    return lax.ppermute(v, axis, [(i, (i + k) % n) for i in range(n)])


def swap(v):
    return lax.ppermute(v, "c", [(0, 1), (1, 0)])


EVEN = ((0, 1), (1, 0), (2, 3), (3, 2))
ODD = ((1, 2), (2, 1), (3, 0), (0, 3))


def meet(v, partners):
    return v + lax.ppermute(v, "x", partners)


def total_over_gauges(keep_0, keep_1, send_0, send_1):
    sum_0, sum_1 = keep_0 + swap(send_0), keep_1 + swap(send_1)
    sum_0, sum_1 = meet(sum_0, EVEN), meet(sum_1, ODD)
    sum_0, sum_1 = meet(sum_0, ODD), meet(sum_1, EVEN)
    return sum_0, sum_1, swap(sum_0), swap(sum_1)


def to_all(v, axis):
    n = lax.axis_size(axis)
    return lax.all_to_all(jnp.broadcast_to(v[None], (n,) + v.shape), axis, 0, 0, tiled=True)


def gather(anomalies):
    own = to_all(anomalies, "y")
    below, above = own, own
    early = [own]
    for _ in range((lax.axis_size("z") - 1) // 2):
        below, above = shift(below, "z", 1), shift(above, "z", -1)
        early += [below, above]
    half = own.shape[0] // 2
    return early, [shift(below[:half], "z", 1), shift(above[half:], "z", -1)]


def local(anomalies, innovations, obs_var, basins, taper_mask):
    blk, members = anomalies.shape
    shape = tuple(lax.axis_size(a) for a in PEERS)
    peers = shape[0] * shape[1]
    nx, nc = lax.axis_size("x"), lax.axis_size("c")
    me_x, me_c = lax.axis_index("x"), lax.axis_index("c")
    nblocks = taper_mask.shape[0]

    near = taper_mask != 0
    place = jnp.arange(nblocks, dtype=jnp.int32)
    leader = jnp.min(jnp.where(near, place[None, :], nblocks), axis=1)
    leads = (leader == place)[None, :] & (place[None, :] < leader[:, None])
    gid = jnp.sum(leads.astype(jnp.int32), axis=1)
    gid = gid.reshape(nx, shape[0], nc, shape[1])
    gid = lax.dynamic_slice(gid, (me_x, 0, me_c, 0), (1, shape[0], 1, shape[1])).reshape(peers)
    gid = jnp.minimum(gid, GROUPS - 1)
    pos = jnp.stack([me_c, lax.axis_index("z")]).astype(jnp.int32)

    early, late = gather(anomalies)
    lanes = ((0, 0), (0, LANES - blk))
    field = jnp.pad(innovations.T, lanes).reshape(peers, ROWS, LANES)
    extra = jnp.stack([obs_var, basins.astype(jnp.float32)])
    extra = jnp.pad(extra, ((0, ROWS - 2), (0, LANES - blk)))
    pay = jnp.concatenate([field, jnp.broadcast_to(extra[None], (peers, ROWS, LANES))], 1)
    pay = lax.all_to_all(pay, PEERS, 0, 0, tiled=True)

    smem = pl.BlockSpec(memory_space=pltpu.SMEM)
    vmem = pl.BlockSpec(memory_space=pltpu.VMEM)
    f32 = functools.partial(jax.ShapeDtypeStruct, dtype=jnp.float32)
    b16 = functools.partial(jax.ShapeDtypeStruct, dtype=jnp.bfloat16)
    rows = BASINS * ROWS
    n_late = shape[0]
    n_early = peers - n_late
    pairs = (n_early + GROUPS) // 2
    shards = [f32((rows + ROWS, members)), f32((rows, members))] * 2
    state = [f32((pairs, ROWS, 2 * LANES)), f32((n_late, ROWS, LANES))]
    sums = (GROUPS, 2, rows // 2, members)

    def params(mib):
        return pltpu.CompilerParams(vmem_limit_bytes=mib * 2**20)

    tab, gauges, anoms = pl.pallas_call(
        functools.partial(pack_kernel, shape),
        out_shape=(
            jax.ShapeDtypeStruct((pairs + peers,), jnp.int32),
            f32((2 * pairs + n_late, 2 * ROWS, LANES)),
            b16((pairs, 4 * LANES, members)),
        ),
        in_specs=[smem, smem] + [vmem] * (1 + len(early)),
        out_specs=(smem, vmem, vmem),
        scratch_shapes=[pltpu.SMEM((GROUPS,), jnp.int32)],
        compiler_params=params(20),
        cost_estimate=pl.CostEstimate(
            flops=n_early * blk * members * 8, bytes_accessed=n_early * blk * members * 12,
            transcendentals=0,
        ),
        name="pack",
    )(pos, gid, pay, *early)
    late_anoms, *parts = pl.pallas_call(
        functools.partial(first_kernel, shape),
        out_shape=(
            b16((n_late, 2 * LANES, members)),
            *shards,
        ),
        in_specs=[smem, smem] + [vmem] * (2 + len(late)),
        out_specs=(vmem,) * 5,
        scratch_shapes=[pltpu.VMEM(sums, jnp.float32)],
        compiler_params=params(20),
        name="project",
    )(pos, tab, gauges, anoms, *late)
    turned, late_turned = pl.pallas_call(
        turn_kernel,
        out_shape=(b16((pairs, members, 4 * LANES)), b16((n_late, members, 2 * LANES))),
        in_specs=[vmem, vmem],
        out_specs=(vmem, vmem),
        compiler_params=params(20),
        cost_estimate=pl.CostEstimate(
            flops=peers * blk * members * 8, bytes_accessed=peers * blk * members * 8,
            transcendentals=0,
        ),
        name="turn",
    )(anoms, late_anoms)
    common = (pos, tab, gauges, anoms, turned, late_anoms, late_turned)
    carried = ()
    for step in range(ITERS):
        first, last = step == 0, step + 1 == ITERS
        args = (*common, *total_over_gauges(*parts), *carried)
        if last:
            shapes = [f32((peers, 2 * ROWS, LANES))]
            more = [pltpu.VMEM((2 * pairs + n_late, 2 * ROWS, LANES), jnp.float32)]
        else:
            shapes = [*state, *state, f32(sums), f32((ROWS, LANES)), *shards]
            shapes += [] if first else state
            more = []
        has_d = step > 1
        out = pl.pallas_call(
            functools.partial(step_kernel, shape, members, first, last if has_d or first else None),
            out_shape=shapes,
            in_specs=[smem, smem] + [vmem] * (len(args) - 2),
            out_specs=[vmem] * len(shapes),
            scratch_shapes=[
                pltpu.VMEM(sums, jnp.bfloat16),
                pltpu.VMEM(sums, jnp.bfloat16),
                pltpu.VMEM(sums, jnp.float32),
            ] + more,
            compiler_params=params(20),
            name="finish" if last else "step",
        )(*args)
        if not last:
            parts = out[6:10]
            carried = (*out[:6], *out[10:])
    back = lax.all_to_all(out[0], PEERS, 0, 0, tiled=True)
    solution_field, residual = pl.pallas_call(
        out_kernel,
        out_shape=(f32((blk, members)), f32((blk, members))),
        in_specs=[vmem],
        out_specs=(vmem, vmem),
        compiler_params=params(20),
        name="out",
    )(back)
    return solution_field, residual


def solution(mesh):
    fine = Mesh(mesh.devices.reshape(8, 4, 4, 2), ("z", "x", "y", "c"))
    split_all = ("x", "y", "c", "z")
    placed = (P(split_all, None), P(split_all, None), P(split_all), P(split_all), P())
    return jax.shard_map(
        local,
        mesh=fine,
        in_specs=placed,
        out_specs=(P(split_all, None), P(split_all, None)),
        check_vma=False,
    )
```

```python
import functools

import jax
import jax.numpy as jnp
from jax import lax
from jax.experimental import pallas as pl
from jax.experimental.pallas import tpu as pltpu
from jax.sharding import Mesh
from jax.sharding import PartitionSpec as P

ITERS = 3
BASINS = 16
GROUPS = 4
far_weight = 0.3

LANES = 128
ROWS = 8
PEERS = ("y", "z")
EARLY = (0, -1, 1, -2, 2, -3, 3)


def split(v):
    high = v.astype(jnp.bfloat16)
    return high, (v - high.astype(jnp.float32)).astype(jnp.bfloat16)


def block_id(pos_ref, shape, y, step):
    nz = shape[1]
    return y * nz + lax.rem(pos_ref[1] + (step + nz), nz)


def early_blocks(shape):
    return [(y, step) for step in EARLY for y in range(shape[0])]


def late_blocks(shape):
    ny, nz = shape
    return [(y, nz // 2) for y in range(ny)]


def pack_kernel(shape, *refs):
    pos_ref, gid_ref, pay_ref = refs[:3]
    tab_ref, gauge_ref, anom_ref, count = refs[-4:]
    pieces = refs[3:-4]
    ny = shape[0]
    pairs = anom_ref.shape[0]
    early = early_blocks(shape)
    ids = [block_id(pos_ref, shape, *e) for e in early]
    for g in range(GROUPS):
        count[g] = 0
    for i in ids:
        g = gid_ref[i]
        count[g] = count[g] + 1
    for p in range(pairs):
        tab_ref[p] = 0
    start = jnp.int32(0)
    empty = []
    for g in range(GROUPS):
        n = count[g]
        count[g] = 2 * start

        def mark(p, carry, g=g):
            tab_ref[p] = g
            return carry

        end = start + lax.div(n + 1, 2)
        lax.fori_loop(start, end, mark, 0)
        empty.append((lax.rem(n, 2) == 1, 2 * end - 1))
        start = end

    def put(s, value):
        high, low = split(value)
        p, h = lax.div(s, 2), lax.rem(s, 2)
        anom_ref[p, pl.ds(pl.multiple_of(h * LANES, LANES), LANES)] = high
        anom_ref[p, pl.ds(pl.multiple_of((2 + h) * LANES, LANES), LANES)] = low

    blank = jnp.zeros((LANES, anom_ref.shape[2]), jnp.float32)
    for odd, s in empty:
        pl.when(odd)(functools.partial(put, s, blank))

    def clear(s, carry):
        put(s, blank)
        return carry

    lax.fori_loop(2 * start, 2 * pairs, clear, 0)
    gauge_ref[...] = jnp.zeros_like(gauge_ref)
    rest = blank[pieces[0].shape[1] :]
    for k, i in enumerate(ids):
        g = gid_ref[i]
        s = count[g]
        count[g] = s + 1
        tab_ref[pairs + k] = s
        gauge_ref[s] = pay_ref[i]
        put(s, jnp.concatenate([pieces[k // ny][k % ny], rest], 0))
    for k, e in enumerate(late_blocks(shape)):
        i = block_id(pos_ref, shape, *e)
        tab_ref[pairs + len(ids) + k] = gid_ref[i]
        gauge_ref[2 * pairs + k] = pay_ref[i]


def turn_kernel(anom_ref, late_ref, turn_ref, late_turn):
    for ref, out in ((anom_ref, turn_ref), (late_ref, late_turn)):
        width = ref.shape[1] // 2
        for p in range(ref.shape[0]):
            for h in range(2):
                part = slice(h * width, (h + 1) * width)
                out[p, :, part] = ref[p, part].T


def out_kernel(back_ref, x_ref, r_ref):
    for out, rows in ((x_ref, slice(0, ROWS)), (r_ref, slice(ROWS, 2 * ROWS))):
        for k in range(0, back_ref.shape[0], LANES // ROWS):
            tile = back_ref[k : k + LANES // ROWS, rows].reshape(LANES, LANES).T
            out[:, k * ROWS : k * ROWS + LANES] = tile[: out.shape[0]]


class Part:
    def __init__(self, tab_ref, anom_ref, turn_ref, gauge_ref, pairs, early):
        self.count, self.width = anom_ref.shape[0], anom_ref.shape[1] // 2
        self.tab_ref, self.anom_ref, self.turn_ref = tab_ref, anom_ref, turn_ref
        self.gauge_ref = gauge_ref
        self.paired = self.width == 2 * LANES
        self.first_group = 0 if self.paired else pairs + early
        self.first_slot = 0 if self.paired else 2 * pairs

    def group(self, p):
        return self.tab_ref[self.first_group + p]

    def gauges(self, p, rows):
        if self.paired:
            return jnp.concatenate([self.gauge_ref[2 * p, rows], self.gauge_ref[2 * p + 1, rows]], 1)
        return self.gauge_ref[self.first_slot + p, rows]

    def field(self, p):
        return self.gauges(p, slice(0, ROWS))

    def obs(self, p):
        return self.gauges(p, slice(ROWS, ROWS + 1))

    def same_basin(self, p):
        basin = self.gauges(p, slice(ROWS + 1, ROWS + 2))[None]
        ids = lax.broadcasted_iota(jnp.int32, (BASINS, ROWS, self.width), 0)
        return ids.astype(jnp.float32) == basin


def project(pos_ref, parts, fields, sums, acc, outs):
    rows = BASINS * ROWS
    acc[...] = jnp.zeros_like(acc)
    for part, field in zip(parts, fields):
        width = part.width
        for p in range(part.count):
            near = part.same_basin(p)
            v = field(p)
            v_high = v.astype(jnp.bfloat16).astype(jnp.float32)
            high, low = (
                jnp.where(near, u[None], 0.0).reshape(rows, width).astype(jnp.bfloat16)
                for u in (v_high, v - v_high)
            )
            both = jnp.dot(
                jnp.concatenate([high, low], 0), part.anom_ref[p, :width],
                preferred_element_type=jnp.float32,
            )
            third = jnp.dot(high, part.anom_ref[p, width:], preferred_element_type=jnp.float32)
            g = part.group(p)
            acc[g] = acc[g] + (both[:rows] + both[rows:] + third).reshape(acc.shape[1:])
    lane = lax.broadcasted_iota(jnp.int32, (ROWS, acc.shape[3]), 1)
    row = jnp.zeros((ROWS, acc.shape[3]), jnp.float32)
    for place, value in enumerate(sums):
        row = jnp.where(lane == place, value, row)
    me_c, half = pos_ref[0], rows // 2
    for side in range(2):
        core = me_c if side == 0 else 1 - me_c
        for g in range(GROUPS):
            out = outs[2 * side + g // 2]
            out[g % 2 * half : (g % 2 + 1) * half] = acc[g, core]
        outs[2 * side][2 * half :] = row


def lane_sum(v):
    return jnp.sum(v, axis=1, keepdims=True)


def total(values):
    return functools.reduce(lambda a, b: a + b, values)


def first_kernel(shape, *refs):
    pos_ref, tab_ref, gauge_ref, anom_ref = refs[:4]
    late_ref, *outs, acc = refs[-6:]
    pieces = refs[4:-6]
    pairs = anom_ref.shape[0]
    early, late = early_blocks(shape), late_blocks(shape)
    rest = jnp.zeros((LANES - pieces[0].shape[1], pieces[0].shape[2]), jnp.float32)
    half = pieces[0].shape[0]
    for k in range(len(late)):
        value = jnp.concatenate([pieces[k // half][k % half], rest], 0)
        late_ref[k, :LANES], late_ref[k, LANES:] = split(value)
    parts = [
        Part(tab_ref, a, t, gauge_ref, pairs, len(early))
        for a, t in ((anom_ref, None), (late_ref, None))
    ]
    one, two = [], []
    for part in parts:
        squares = [part.field(p) * part.field(p) for p in range(part.count)]
        one.append(lane_sum(total(squares)))
        two.append(lane_sum(total([s * part.obs(p) for p, s in enumerate(squares)])))
    fields = [part.field for part in parts]
    project(pos_ref, parts, fields, (total(one), total(two)), acc, outs)


def step_kernel(shape, members, first, last, *refs):
    refs = list(refs)

    def take(n):
        taken = refs[:n]
        del refs[:n]
        return taken

    pos_ref, tab_ref, gauge_ref, anom_ref, turn_ref, late_ref, late_turn = take(7)
    own, other = take(2), take(2)
    if not first:
        x_in, r_in, dir_in, scal_in = take(2), take(2), *take(2)
        d_in = take(0 if last is None else 2)
    if last:
        (out_ref,) = take(1)
        e_high, e_low, dir_sum, result = refs
    else:
        x_out, r_out, dir_out, scal_out, outs = take(2), take(2), *take(2), take(4)
        d_out = [] if first else take(2)
        e_high, e_low, acc = refs
        dir_sum = dir_out
    pairs = anom_ref.shape[0]
    wide = anom_ref.shape[2]
    rows = BASINS * ROWS
    early, late = early_blocks(shape), late_blocks(shape)
    parts = [
        Part(tab_ref, a, t, gauge_ref, pairs, len(early))
        for a, t in ((anom_ref, turn_ref), (late_ref, late_turn))
    ]

    me_c, half = pos_ref[0], rows // 2
    row = own[0][2 * half :]
    rr, r_obs_r, r_obs_d = row[:, 0:1], row[:, 1:2], row[:, 2:3]
    if first:
        d_obs_d = r_obs_r
    else:
        beta = rr / scal_in[:, 0:1]
        d_obs_d = r_obs_r + 2.0 * beta * r_obs_d + beta * beta * scal_in[:, 1:2]
    curve = jnp.zeros((ROWS, wide), jnp.float32)
    for g in range(GROUPS):
        halves = []
        for side, core in ((own, me_c), (other, 1 - me_c)):
            d_h = side[g // 2][g % 2 * half : (g % 2 + 1) * half].reshape(-1, ROWS, wide)
            if not first:
                d_h = d_h + beta[None] * dir_in[g, core].reshape(-1, ROWS, wide)
            dir_sum[g, core] = d_h.reshape(half, wide)
            halves.append((core, d_h))
        every = sum(jnp.sum(d_h, axis=0) for _, d_h in halves)
        for core, d_h in halves:
            e_h = (1.0 - far_weight) / (members - 1) * d_h + far_weight / (members - 1) * every[None]
            curve = curve + jnp.sum(d_h * e_h, axis=0)
            e_high[g, core], e_low[g, core] = split(e_h.reshape(half, wide))
    alpha = rr / (lane_sum(curve) + d_obs_d)

    one, two, three = [], [], []
    for k, part in enumerate(parts):
        width = part.width
        squares, weighted, crossed = [], [], []
        for p in range(part.count):
            g = part.group(p)
            e_g = e_high[g].reshape(rows, wide)
            both = jnp.dot(
                jnp.concatenate([e_g.reshape(rows, wide), e_low[g].reshape(rows, wide)], 0),
                part.turn_ref[p, :, :width],
                preferred_element_type=jnp.float32,
            )
            third = jnp.dot(
                e_g, part.turn_ref[p, :, width:], preferred_element_type=jnp.float32
            )
            every = (both[:rows] + both[rows:] + third).reshape(-1, ROWS, width)
            image = jnp.sum(jnp.where(part.same_basin(p), every, 0.0), axis=0)
            obs = part.obs(p)
            if first:
                r = part.field(p)
                d = r
            else:
                r = r_in[k][p]
                d = r + beta * (d_in[k][p] if d_in else part.field(p))
            image = image + obs * d
            x = alpha * d
            if not first:
                x = x_in[k][p] + x
            r = r - alpha * image
            if last:
                for h in range(width // LANES):
                    lanes = slice(h * LANES, (h + 1) * LANES)
                    s = part.first_slot + p * (width // LANES) + h
                    result[s, :ROWS] = x[:, lanes]
                    result[s, ROWS:] = r[:, lanes]
                continue
            x_out[k][p] = x
            r_out[k][p] = r
            if d_out:
                d_out[k][p] = d
            squares.append(r * r)
            weighted.append(r * r * obs)
            crossed.append(r * d * obs)
        if not last:
            one.append(lane_sum(total(squares)))
            two.append(lane_sum(total(weighted)))
            three.append(lane_sum(total(crossed)))
    if last:
        for k, e in enumerate(early):
            out_ref[block_id(pos_ref, shape, *e)] = result[tab_ref[pairs + k]]
        for k, e in enumerate(late):
            out_ref[block_id(pos_ref, shape, *e)] = result[2 * pairs + k]
        return
    lane = lax.broadcasted_iota(jnp.int32, (ROWS, LANES), 1)
    scal_out[...] = jnp.where(lane == 0, rr, d_obs_d)
    fields = [functools.partial(lambda ref, p: ref[p], ref) for ref in r_out]
    project(pos_ref, parts, fields, (total(one), total(two), total(three)), acc, outs)


def shift(v, axis, k):
    n = lax.axis_size(axis)
    return lax.ppermute(v, axis, [(i, (i + k) % n) for i in range(n)])


def swap(v):
    return lax.ppermute(v, "c", [(0, 1), (1, 0)])


EVEN = ((0, 1), (1, 0), (2, 3), (3, 2))
ODD = ((1, 2), (2, 1), (3, 0), (0, 3))


def meet(v, partners):
    return v + lax.ppermute(v, "x", partners)


def total_over_gauges(keep_0, keep_1, send_0, send_1, beside):
    sum_0, sum_1 = keep_0 + swap(send_0), keep_1 + swap(send_1)
    sum_0, sum_1 = meet(sum_0, EVEN), meet(sum_1, ODD)
    if beside:
        sum_0, sum_1, *beside = lax.optimization_barrier((sum_0, sum_1, *beside))
    sum_0, sum_1 = meet(sum_0, ODD), meet(sum_1, EVEN)
    return (sum_0, sum_1, swap(sum_0), swap(sum_1)), beside


def to_all(v, axis):
    n = lax.axis_size(axis)
    return lax.all_to_all(jnp.broadcast_to(v[None], (n,) + v.shape), axis, 0, 0, tiled=True)


def gather(anomalies):
    own = to_all(anomalies, "y")
    below, above = own, own
    early = [own]
    for _ in range((lax.axis_size("z") - 1) // 2):
        below, above = shift(below, "z", 1), shift(above, "z", -1)
        early += [below, above]
    nz, nc = lax.axis_size("z"), lax.axis_size("c")
    ways = [
        (z * nc + c, (z + (1 if c == 0 else -1)) % nz * nc + c) for z in range(nz) for c in range(nc)
    ]
    far = jnp.where(lax.axis_index("c") == 0, below, above)
    return early, [lax.ppermute(far, ("z", "c"), ways)]


def local(anomalies, innovations, obs_var, basins, taper_mask):
    blk, members = anomalies.shape
    shape = tuple(lax.axis_size(a) for a in PEERS)
    peers = shape[0] * shape[1]
    nx, nc = lax.axis_size("x"), lax.axis_size("c")
    me_x, me_c = lax.axis_index("x"), lax.axis_index("c")
    nblocks = taper_mask.shape[0]

    near = taper_mask != 0
    place = jnp.arange(nblocks, dtype=jnp.int32)
    leader = jnp.min(jnp.where(near, place[None, :], nblocks), axis=1)
    leads = (leader == place)[None, :] & (place[None, :] < leader[:, None])
    gid = jnp.sum(leads.astype(jnp.int32), axis=1)
    gid = gid.reshape(nx, shape[0], nc, shape[1])
    gid = lax.dynamic_slice(gid, (me_x, 0, me_c, 0), (1, shape[0], 1, shape[1])).reshape(peers)
    gid = jnp.minimum(gid, GROUPS - 1)
    pos = jnp.stack([me_c, lax.axis_index("z")]).astype(jnp.int32)

    early, late = gather(anomalies)
    lanes = ((0, 0), (0, LANES - blk))
    field = jnp.pad(innovations.T, lanes).reshape(peers, ROWS, LANES)
    extra = jnp.stack([obs_var, basins.astype(jnp.float32)])
    extra = jnp.pad(extra, ((0, ROWS - 2), (0, LANES - blk)))
    pay = jnp.concatenate([field, jnp.broadcast_to(extra[None], (peers, ROWS, LANES))], 1)
    pay = lax.all_to_all(pay, PEERS, 0, 0, tiled=True)

    smem = pl.BlockSpec(memory_space=pltpu.SMEM)
    vmem = pl.BlockSpec(memory_space=pltpu.VMEM)
    f32 = functools.partial(jax.ShapeDtypeStruct, dtype=jnp.float32)
    b16 = functools.partial(jax.ShapeDtypeStruct, dtype=jnp.bfloat16)
    rows = BASINS * ROWS
    n_late = shape[0]
    n_early = peers - n_late
    pairs = (n_early + GROUPS) // 2
    shards = [f32((rows + ROWS, members)), f32((rows, members))] * 2
    state = [f32((pairs, ROWS, 2 * LANES)), f32((n_late, ROWS, LANES))]
    sums = (GROUPS, 2, rows // 2, members)

    def params(mib):
        return pltpu.CompilerParams(vmem_limit_bytes=mib * 2**20)

    tab, gauges, anoms = pl.pallas_call(
        functools.partial(pack_kernel, shape),
        out_shape=(
            jax.ShapeDtypeStruct((pairs + peers,), jnp.int32),
            f32((2 * pairs + n_late, 2 * ROWS, LANES)),
            b16((pairs, 4 * LANES, members)),
        ),
        in_specs=[smem, smem] + [vmem] * (1 + len(early)),
        out_specs=(smem, vmem, vmem),
        scratch_shapes=[pltpu.SMEM((GROUPS,), jnp.int32)],
        compiler_params=params(20),
        cost_estimate=pl.CostEstimate(
            flops=n_early * blk * members * 8, bytes_accessed=n_early * blk * members * 12,
            transcendentals=0,
        ),
        name="pack",
    )(pos, gid, pay, *early)
    late_anoms, *parts = pl.pallas_call(
        functools.partial(first_kernel, shape),
        out_shape=(
            b16((n_late, 2 * LANES, members)),
            *shards,
        ),
        in_specs=[smem, smem] + [vmem] * (2 + len(late)),
        out_specs=(vmem,) * 5,
        scratch_shapes=[pltpu.VMEM(sums, jnp.float32)],
        compiler_params=params(20),
        name="project",
    )(pos, tab, gauges, anoms, *late)
    turned, late_turned = pl.pallas_call(
        turn_kernel,
        out_shape=(b16((pairs, members, 4 * LANES)), b16((n_late, members, 2 * LANES))),
        in_specs=[vmem, vmem],
        out_specs=(vmem, vmem),
        compiler_params=params(20),
        cost_estimate=pl.CostEstimate(
            flops=peers * blk * members * 8, bytes_accessed=peers * blk * members * 8,
            transcendentals=0,
        ),
        name="turn",
    )(anoms, late_anoms)
    carried = ()
    for step in range(ITERS):
        first, last = step == 0, step + 1 == ITERS
        sides, beside = total_over_gauges(*parts, [turned, late_turned] if first else [])
        if first:
            turned, late_turned = beside
        common = (pos, tab, gauges, anoms, turned, late_anoms, late_turned)
        args = (*common, *sides, *carried)
        if last:
            shapes = [f32((peers, 2 * ROWS, LANES))]
            more = [pltpu.VMEM((2 * pairs + n_late, 2 * ROWS, LANES), jnp.float32)]
        else:
            shapes = [*state, *state, f32(sums), f32((ROWS, LANES)), *shards]
            shapes += [] if first else state
            more = []
        has_d = step > 1
        out = pl.pallas_call(
            functools.partial(step_kernel, shape, members, first, last if has_d or first else None),
            out_shape=shapes,
            in_specs=[smem, smem] + [vmem] * (len(args) - 2),
            out_specs=[vmem] * len(shapes),
            scratch_shapes=[
                pltpu.VMEM(sums, jnp.bfloat16),
                pltpu.VMEM(sums, jnp.bfloat16),
                pltpu.VMEM(sums, jnp.float32),
            ] + more,
            compiler_params=params(20),
            name="finish" if last else "step",
        )(*args)
        if not last:
            parts = out[6:10]
            carried = (*out[:6], *out[10:])
    back = lax.all_to_all(out[0], PEERS, 0, 0, tiled=True)
    solution_field, residual = pl.pallas_call(
        out_kernel,
        out_shape=(f32((blk, members)), f32((blk, members))),
        in_specs=[vmem],
        out_specs=(vmem, vmem),
        compiler_params=params(20),
        name="out",
    )(back)
    return solution_field, residual


def solution(mesh):
    fine = Mesh(mesh.devices.reshape(8, 4, 4, 2), ("z", "x", "y", "c"))
    split_all = ("x", "y", "c", "z")
    placed = (P(split_all, None), P(split_all, None), P(split_all), P(split_all), P())
    return jax.shard_map(
        local,
        mesh=fine,
        in_specs=placed,
        out_specs=(P(split_all, None), P(split_all, None)),
        check_vma=False,
    )
```

```python
import functools

import jax
import jax.numpy as jnp
from jax import lax
from jax.experimental import pallas as pl
from jax.experimental.pallas import tpu as pltpu
from jax.sharding import Mesh
from jax.sharding import PartitionSpec as P

ITERS = 3
BASINS = 16
GROUPS = 4
far_weight = 0.3

LANES = 128
ROWS = 8
PEERS = ("y", "z")
EARLY = (0, -1, 1, -2, 2, -3, 3)


def split(v):
    high = v.astype(jnp.bfloat16)
    return high, (v - high.astype(jnp.float32)).astype(jnp.bfloat16)


def block_id(pos_ref, shape, y, step):
    nz = shape[1]
    return y * nz + lax.rem(pos_ref[1] + (step + nz), nz)


def early_blocks(shape):
    return [(y, step) for step in EARLY for y in range(shape[0])]


def late_blocks(shape):
    ny, nz = shape
    return [(y, nz // 2) for y in range(ny)]


def pack_kernel(shape, *refs):
    pos_ref, gid_ref, pay_ref = refs[:3]
    tab_ref, gauge_ref, anom_ref, turn_ref, count = refs[-5:]
    pieces = refs[3:-5]
    ny = shape[0]
    pairs = anom_ref.shape[0]
    early = early_blocks(shape)
    ids = [block_id(pos_ref, shape, *e) for e in early]
    for g in range(GROUPS):
        count[g] = 0
    for i in ids:
        g = gid_ref[i]
        count[g] = count[g] + 1
    for p in range(pairs):
        tab_ref[p] = 0
    start = jnp.int32(0)
    empty = []
    for g in range(GROUPS):
        n = count[g]
        count[g] = 2 * start

        def mark(p, carry, g=g):
            tab_ref[p] = g
            return carry

        end = start + lax.div(n + 1, 2)
        lax.fori_loop(start, end, mark, 0)
        empty.append((lax.rem(n, 2) == 1, 2 * end - 1))
        start = end

    def put(s, value):
        high, low = split(value)
        p, h = lax.div(s, 2), lax.rem(s, 2)
        first = pl.ds(pl.multiple_of(h * LANES, LANES), LANES)
        second = pl.ds(pl.multiple_of((2 + h) * LANES, LANES), LANES)
        anom_ref[p, first] = high
        anom_ref[p, second] = low
        high, low = split(value.T)
        turn_ref[p, :, first] = high
        turn_ref[p, :, second] = low

    blank = jnp.zeros((LANES, anom_ref.shape[2]), jnp.float32)
    for odd, s in empty:
        pl.when(odd)(functools.partial(put, s, blank))

    def clear(s, carry):
        put(s, blank)
        return carry

    lax.fori_loop(2 * start, 2 * pairs, clear, 0)
    gauge_ref[...] = jnp.zeros_like(gauge_ref)
    rest = blank[pieces[0].shape[1] :]
    for k, i in enumerate(ids):
        g = gid_ref[i]
        s = count[g]
        count[g] = s + 1
        tab_ref[pairs + k] = s
        gauge_ref[s] = pay_ref[i]
        put(s, jnp.concatenate([pieces[k // ny][k % ny], rest], 0))
    for k, e in enumerate(late_blocks(shape)):
        i = block_id(pos_ref, shape, *e)
        tab_ref[pairs + len(ids) + k] = gid_ref[i]
        gauge_ref[2 * pairs + k] = pay_ref[i]


def out_kernel(back_ref, x_ref, r_ref):
    for out, rows in ((x_ref, slice(0, ROWS)), (r_ref, slice(ROWS, 2 * ROWS))):
        for k in range(0, back_ref.shape[0], LANES // ROWS):
            tile = back_ref[k : k + LANES // ROWS, rows].reshape(LANES, LANES).T
            out[:, k * ROWS : k * ROWS + LANES] = tile[: out.shape[0]]


class Part:
    def __init__(self, tab_ref, anom_ref, turn_ref, gauge_ref, pairs, early):
        self.count, self.width = anom_ref.shape[0], anom_ref.shape[1] // 2
        self.tab_ref, self.anom_ref, self.turn_ref = tab_ref, anom_ref, turn_ref
        self.gauge_ref = gauge_ref
        self.paired = self.width == 2 * LANES
        self.first_group = 0 if self.paired else pairs + early
        self.first_slot = 0 if self.paired else 2 * pairs

    def group(self, p):
        return self.tab_ref[self.first_group + p]

    def gauges(self, p, rows):
        if self.paired:
            return jnp.concatenate([self.gauge_ref[2 * p, rows], self.gauge_ref[2 * p + 1, rows]], 1)
        return self.gauge_ref[self.first_slot + p, rows]

    def field(self, p):
        return self.gauges(p, slice(0, ROWS))

    def obs(self, p):
        return self.gauges(p, slice(ROWS, ROWS + 1))

    def same_basin(self, p):
        basin = self.gauges(p, slice(ROWS + 1, ROWS + 2))[None]
        ids = lax.broadcasted_iota(jnp.int32, (BASINS, ROWS, self.width), 0)
        return ids.astype(jnp.float32) == basin


def project(pos_ref, parts, fields, sums, acc, outs):
    rows = BASINS * ROWS
    acc[...] = jnp.zeros_like(acc)
    for part, field in zip(parts, fields):
        width = part.width
        for p in range(part.count):
            near = part.same_basin(p)
            v = field(p)
            v_high = v.astype(jnp.bfloat16).astype(jnp.float32)
            high, low = (
                jnp.where(near, u[None], 0.0).reshape(rows, width).astype(jnp.bfloat16)
                for u in (v_high, v - v_high)
            )
            both = jnp.dot(
                jnp.concatenate([high, low], 0), part.anom_ref[p, :width],
                preferred_element_type=jnp.float32,
            )
            third = jnp.dot(high, part.anom_ref[p, width:], preferred_element_type=jnp.float32)
            g = part.group(p)
            acc[g] = acc[g] + (both[:rows] + both[rows:] + third).reshape(acc.shape[1:])
    lane = lax.broadcasted_iota(jnp.int32, (ROWS, acc.shape[3]), 1)
    row = jnp.zeros((ROWS, acc.shape[3]), jnp.float32)
    for place, value in enumerate(sums):
        row = jnp.where(lane == place, value, row)
    me_c, half = pos_ref[0], rows // 2
    for side in range(2):
        core = me_c if side == 0 else 1 - me_c
        for g in range(GROUPS):
            out = outs[2 * side + g // 2]
            out[g % 2 * half : (g % 2 + 1) * half] = acc[g, core]
        outs[2 * side][2 * half :] = row


def lane_sum(v):
    return jnp.sum(v, axis=1, keepdims=True)


def total(values):
    return functools.reduce(lambda a, b: a + b, values)


def first_kernel(shape, *refs):
    pos_ref, tab_ref, gauge_ref, anom_ref, turn_ref = refs[:5]
    late_ref, late_turn, *outs, acc = refs[-7:]
    pieces = refs[5:-7]
    pairs = anom_ref.shape[0]
    early, late = early_blocks(shape), late_blocks(shape)
    rest = jnp.zeros((LANES - pieces[0].shape[1], pieces[0].shape[2]), jnp.float32)
    half = pieces[0].shape[0]
    for k in range(len(late)):
        value = jnp.concatenate([pieces[k // half][k % half], rest], 0)
        late_ref[k, :LANES], late_ref[k, LANES:] = split(value)
        late_turn[k, :, :LANES], late_turn[k, :, LANES:] = split(value.T)
    parts = [
        Part(tab_ref, a, t, gauge_ref, pairs, len(early))
        for a, t in ((anom_ref, turn_ref), (late_ref, late_turn))
    ]
    one, two = [], []
    for part in parts:
        squares = [part.field(p) * part.field(p) for p in range(part.count)]
        one.append(lane_sum(total(squares)))
        two.append(lane_sum(total([s * part.obs(p) for p, s in enumerate(squares)])))
    fields = [part.field for part in parts]
    project(pos_ref, parts, fields, (total(one), total(two)), acc, outs)


def step_kernel(shape, members, first, last, *refs):
    refs = list(refs)

    def take(n):
        taken = refs[:n]
        del refs[:n]
        return taken

    pos_ref, tab_ref, gauge_ref, anom_ref, turn_ref, late_ref, late_turn = take(7)
    own, other = take(2), take(2)
    if not first:
        x_in, r_in, dir_in, scal_in = take(2), take(2), *take(2)
        d_in = take(0 if last is None else 2)
    if last:
        (out_ref,) = take(1)
        e_high, e_low, dir_sum, result = refs
    else:
        x_out, r_out, dir_out, scal_out, outs = take(2), take(2), *take(2), take(4)
        d_out = [] if first else take(2)
        e_high, e_low, acc = refs
        dir_sum = dir_out
    pairs = anom_ref.shape[0]
    wide = anom_ref.shape[2]
    rows = BASINS * ROWS
    early, late = early_blocks(shape), late_blocks(shape)
    parts = [
        Part(tab_ref, a, t, gauge_ref, pairs, len(early))
        for a, t in ((anom_ref, turn_ref), (late_ref, late_turn))
    ]

    me_c, half = pos_ref[0], rows // 2
    row = own[0][2 * half :]
    rr, r_obs_r, r_obs_d = row[:, 0:1], row[:, 1:2], row[:, 2:3]
    if first:
        d_obs_d = r_obs_r
    else:
        beta = rr / scal_in[:, 0:1]
        d_obs_d = r_obs_r + 2.0 * beta * r_obs_d + beta * beta * scal_in[:, 1:2]
    curve = jnp.zeros((ROWS, wide), jnp.float32)
    for g in range(GROUPS):
        halves = []
        for side, core in ((own, me_c), (other, 1 - me_c)):
            d_h = side[g // 2][g % 2 * half : (g % 2 + 1) * half].reshape(-1, ROWS, wide)
            if not first:
                d_h = d_h + beta[None] * dir_in[g, core].reshape(-1, ROWS, wide)
            dir_sum[g, core] = d_h.reshape(half, wide)
            halves.append((core, d_h))
        every = sum(jnp.sum(d_h, axis=0) for _, d_h in halves)
        for core, d_h in halves:
            e_h = (1.0 - far_weight) / (members - 1) * d_h + far_weight / (members - 1) * every[None]
            curve = curve + jnp.sum(d_h * e_h, axis=0)
            e_high[g, core], e_low[g, core] = split(e_h.reshape(half, wide))
    alpha = rr / (lane_sum(curve) + d_obs_d)

    one, two, three = [], [], []
    for k, part in enumerate(parts):
        width = part.width
        squares, weighted, crossed = [], [], []
        for p in range(part.count):
            g = part.group(p)
            e_g = e_high[g].reshape(rows, wide)
            both = jnp.dot(
                jnp.concatenate([e_g.reshape(rows, wide), e_low[g].reshape(rows, wide)], 0),
                part.turn_ref[p, :, :width],
                preferred_element_type=jnp.float32,
            )
            third = jnp.dot(
                e_g, part.turn_ref[p, :, width:], preferred_element_type=jnp.float32
            )
            every = (both[:rows] + both[rows:] + third).reshape(-1, ROWS, width)
            image = jnp.sum(jnp.where(part.same_basin(p), every, 0.0), axis=0)
            obs = part.obs(p)
            if first:
                r = part.field(p)
                d = r
            else:
                r = r_in[k][p]
                d = r + beta * (d_in[k][p] if d_in else part.field(p))
            image = image + obs * d
            x = alpha * d
            if not first:
                x = x_in[k][p] + x
            r = r - alpha * image
            if last:
                for h in range(width // LANES):
                    lanes = slice(h * LANES, (h + 1) * LANES)
                    s = part.first_slot + p * (width // LANES) + h
                    result[s, :ROWS] = x[:, lanes]
                    result[s, ROWS:] = r[:, lanes]
                continue
            x_out[k][p] = x
            r_out[k][p] = r
            if d_out:
                d_out[k][p] = d
            squares.append(r * r)
            weighted.append(r * r * obs)
            crossed.append(r * d * obs)
        if not last:
            one.append(lane_sum(total(squares)))
            two.append(lane_sum(total(weighted)))
            three.append(lane_sum(total(crossed)))
    if last:
        for k, e in enumerate(early):
            out_ref[block_id(pos_ref, shape, *e)] = result[tab_ref[pairs + k]]
        for k, e in enumerate(late):
            out_ref[block_id(pos_ref, shape, *e)] = result[2 * pairs + k]
        return
    lane = lax.broadcasted_iota(jnp.int32, (ROWS, LANES), 1)
    scal_out[...] = jnp.where(lane == 0, rr, d_obs_d)
    fields = [functools.partial(lambda ref, p: ref[p], ref) for ref in r_out]
    project(pos_ref, parts, fields, (total(one), total(two), total(three)), acc, outs)


def shift(v, axis, k):
    n = lax.axis_size(axis)
    return lax.ppermute(v, axis, [(i, (i + k) % n) for i in range(n)])


def swap(v):
    return lax.ppermute(v, "c", [(0, 1), (1, 0)])


EVEN = ((0, 1), (1, 0), (2, 3), (3, 2))
ODD = ((1, 2), (2, 1), (3, 0), (0, 3))


def meet(v, partners):
    return v + lax.ppermute(v, "x", partners)


def total_over_gauges(keep_0, keep_1, send_0, send_1):
    sum_0, sum_1 = keep_0 + swap(send_0), keep_1 + swap(send_1)
    sum_0, sum_1 = meet(sum_0, EVEN), meet(sum_1, ODD)
    sum_0, sum_1 = meet(sum_0, ODD), meet(sum_1, EVEN)
    return sum_0, sum_1, swap(sum_0), swap(sum_1)


def to_all(v, axis):
    n = lax.axis_size(axis)
    return lax.all_to_all(jnp.broadcast_to(v[None], (n,) + v.shape), axis, 0, 0, tiled=True)


def gather(anomalies):
    own = to_all(anomalies, "y")
    below, above = own, own
    early = [own]
    for _ in range((lax.axis_size("z") - 1) // 2):
        below, above = shift(below, "z", 1), shift(above, "z", -1)
        early += [below, above]
    nz, nc = lax.axis_size("z"), lax.axis_size("c")
    ways = [
        (z * nc + c, (z + (1 if c == 0 else -1)) % nz * nc + c) for z in range(nz) for c in range(nc)
    ]
    far = jnp.where(lax.axis_index("c") == 0, below, above)
    return early, [lax.ppermute(far, ("z", "c"), ways)]


def local(anomalies, innovations, obs_var, basins, taper_mask):
    blk, members = anomalies.shape
    shape = tuple(lax.axis_size(a) for a in PEERS)
    peers = shape[0] * shape[1]
    nx, nc = lax.axis_size("x"), lax.axis_size("c")
    me_x, me_c = lax.axis_index("x"), lax.axis_index("c")
    nblocks = taper_mask.shape[0]

    near = taper_mask != 0
    place = jnp.arange(nblocks, dtype=jnp.int32)
    leader = jnp.min(jnp.where(near, place[None, :], nblocks), axis=1)
    leads = (leader == place)[None, :] & (place[None, :] < leader[:, None])
    gid = jnp.sum(leads.astype(jnp.int32), axis=1)
    gid = gid.reshape(nx, shape[0], nc, shape[1])
    gid = lax.dynamic_slice(gid, (me_x, 0, me_c, 0), (1, shape[0], 1, shape[1])).reshape(peers)
    gid = jnp.minimum(gid, GROUPS - 1)
    pos = jnp.stack([me_c, lax.axis_index("z")]).astype(jnp.int32)

    early, late = gather(anomalies)
    lanes = ((0, 0), (0, LANES - blk))
    field = jnp.pad(innovations.T, lanes).reshape(peers, ROWS, LANES)
    extra = jnp.stack([obs_var, basins.astype(jnp.float32)])
    extra = jnp.pad(extra, ((0, ROWS - 2), (0, LANES - blk)))
    pay = jnp.concatenate([field, jnp.broadcast_to(extra[None], (peers, ROWS, LANES))], 1)
    pay = lax.all_to_all(pay, PEERS, 0, 0, tiled=True)

    smem = pl.BlockSpec(memory_space=pltpu.SMEM)
    vmem = pl.BlockSpec(memory_space=pltpu.VMEM)
    f32 = functools.partial(jax.ShapeDtypeStruct, dtype=jnp.float32)
    b16 = functools.partial(jax.ShapeDtypeStruct, dtype=jnp.bfloat16)
    rows = BASINS * ROWS
    n_late = shape[0]
    n_early = peers - n_late
    pairs = (n_early + GROUPS) // 2
    shards = [f32((rows + ROWS, members)), f32((rows, members))] * 2
    state = [f32((pairs, ROWS, 2 * LANES)), f32((n_late, ROWS, LANES))]
    sums = (GROUPS, 2, rows // 2, members)

    def params(mib):
        return pltpu.CompilerParams(vmem_limit_bytes=mib * 2**20)

    tab, gauges, anoms, turned = pl.pallas_call(
        functools.partial(pack_kernel, shape),
        out_shape=(
            jax.ShapeDtypeStruct((pairs + peers,), jnp.int32),
            f32((2 * pairs + n_late, 2 * ROWS, LANES)),
            b16((pairs, 4 * LANES, members)),
            b16((pairs, members, 4 * LANES)),
        ),
        in_specs=[smem, smem] + [vmem] * (1 + len(early)),
        out_specs=(smem, vmem, vmem, vmem),
        scratch_shapes=[pltpu.SMEM((GROUPS,), jnp.int32)],
        compiler_params=params(20),
        cost_estimate=pl.CostEstimate(
            flops=n_early * blk * members * 8, bytes_accessed=n_early * blk * members * 12,
            transcendentals=0,
        ),
        name="pack",
    )(pos, gid, pay, *early)
    late_anoms, late_turned, *parts = pl.pallas_call(
        functools.partial(first_kernel, shape),
        out_shape=(
            b16((n_late, 2 * LANES, members)),
            b16((n_late, members, 2 * LANES)),
            *shards,
        ),
        in_specs=[smem, smem] + [vmem] * (3 + len(late)),
        out_specs=(vmem,) * 6,
        scratch_shapes=[pltpu.VMEM(sums, jnp.float32)],
        compiler_params=params(20),
        name="project",
    )(pos, tab, gauges, anoms, turned, *late)
    common = (pos, tab, gauges, anoms, turned, late_anoms, late_turned)
    carried = ()
    for step in range(ITERS):
        first, last = step == 0, step + 1 == ITERS
        args = (*common, *total_over_gauges(*parts), *carried)
        if last:
            shapes = [f32((peers, 2 * ROWS, LANES))]
            more = [pltpu.VMEM((2 * pairs + n_late, 2 * ROWS, LANES), jnp.float32)]
        else:
            shapes = [*state, *state, f32(sums), f32((ROWS, LANES)), *shards]
            shapes += [] if first else state
            more = []
        has_d = step > 1
        out = pl.pallas_call(
            functools.partial(step_kernel, shape, members, first, last if has_d or first else None),
            out_shape=shapes,
            in_specs=[smem, smem] + [vmem] * (len(args) - 2),
            out_specs=[vmem] * len(shapes),
            scratch_shapes=[
                pltpu.VMEM(sums, jnp.bfloat16),
                pltpu.VMEM(sums, jnp.bfloat16),
                pltpu.VMEM(sums, jnp.float32),
            ] + more,
            compiler_params=params(20),
            name="finish" if last else "step",
        )(*args)
        if not last:
            parts = out[6:10]
            carried = (*out[:6], *out[10:])
    back = lax.all_to_all(out[0], PEERS, 0, 0, tiled=True)
    solution_field, residual = pl.pallas_call(
        out_kernel,
        out_shape=(f32((blk, members)), f32((blk, members))),
        in_specs=[vmem],
        out_specs=(vmem, vmem),
        compiler_params=params(20),
        name="out",
    )(back)
    return solution_field, residual


def solution(mesh):
    fine = Mesh(mesh.devices.reshape(8, 4, 4, 2), ("z", "x", "y", "c"))
    split_all = ("x", "y", "c", "z")
    placed = (P(split_all, None), P(split_all, None), P(split_all), P(split_all), P())
    return jax.shard_map(
        local,
        mesh=fine,
        in_specs=placed,
        out_specs=(P(split_all, None), P(split_all, None)),
        check_vma=False,
    )
```

```python
import functools

import jax
import jax.numpy as jnp
from jax import lax
from jax.experimental import pallas as pl
from jax.experimental.pallas import tpu as pltpu
from jax.sharding import Mesh
from jax.sharding import PartitionSpec as P

ITERS = 3
BASINS = 16
GROUPS = 4
far_weight = 0.3

LANES = 128
ROWS = 8
PEERS = ("y", "z")
EARLY = (0, -1, 1, -2, 2, -3, 3)


def split(v):
    high = v.astype(jnp.bfloat16)
    return high, (v - high.astype(jnp.float32)).astype(jnp.bfloat16)


def block_id(pos_ref, shape, y, step):
    nz = shape[1]
    return y * nz + lax.rem(pos_ref[1] + (step + nz), nz)


def early_blocks(shape):
    return [(y, step) for step in EARLY for y in range(shape[0])]


def late_blocks(shape):
    ny, nz = shape
    return [(y, nz // 2) for y in range(ny)]


def pack_kernel(shape, *refs):
    pos_ref, gid_ref, pay_ref = refs[:3]
    tab_ref, gauge_ref, anom_ref, turn_ref, count = refs[-5:]
    pieces = refs[3:-5]
    ny = shape[0]
    pairs = anom_ref.shape[0]
    early = early_blocks(shape)
    ids = [block_id(pos_ref, shape, *e) for e in early]
    for g in range(GROUPS):
        count[g] = 0
    for i in ids:
        g = gid_ref[i]
        count[g] = count[g] + 1
    for p in range(pairs):
        tab_ref[p] = 0
    start = jnp.int32(0)
    empty = []
    for g in range(GROUPS):
        n = count[g]
        count[g] = 2 * start

        def mark(p, carry, g=g):
            tab_ref[p] = g
            return carry

        end = start + lax.div(n + 1, 2)
        lax.fori_loop(start, end, mark, 0)
        empty.append((lax.rem(n, 2) == 1, 2 * end - 1))
        start = end

    def put(s, value):
        high, low = split(value)
        p, h = lax.div(s, 2), lax.rem(s, 2)
        first = pl.ds(pl.multiple_of(h * LANES, LANES), LANES)
        second = pl.ds(pl.multiple_of((2 + h) * LANES, LANES), LANES)
        anom_ref[p, first] = high
        anom_ref[p, second] = low
        high, low = split(value.T)
        turn_ref[p, :, first] = high
        turn_ref[p, :, second] = low

    blank = jnp.zeros((LANES, anom_ref.shape[2]), jnp.float32)
    for odd, s in empty:
        pl.when(odd)(functools.partial(put, s, blank))

    def clear(s, carry):
        put(s, blank)
        return carry

    lax.fori_loop(2 * start, 2 * pairs, clear, 0)
    gauge_ref[...] = jnp.zeros_like(gauge_ref)
    rest = blank[pieces[0].shape[1] :]
    for k, i in enumerate(ids):
        g = gid_ref[i]
        s = count[g]
        count[g] = s + 1
        tab_ref[pairs + k] = s
        gauge_ref[s] = pay_ref[i]
        put(s, jnp.concatenate([pieces[k // ny][k % ny], rest], 0))
    for k, e in enumerate(late_blocks(shape)):
        i = block_id(pos_ref, shape, *e)
        tab_ref[pairs + len(ids) + k] = gid_ref[i]
        gauge_ref[2 * pairs + k] = pay_ref[i]


def out_kernel(back_ref, x_ref, r_ref):
    for out, rows in ((x_ref, slice(0, ROWS)), (r_ref, slice(ROWS, 2 * ROWS))):
        for k in range(0, back_ref.shape[0], LANES // ROWS):
            tile = back_ref[k : k + LANES // ROWS, rows].reshape(LANES, LANES).T
            out[:, k * ROWS : k * ROWS + LANES] = tile[: out.shape[0]]


class Part:
    def __init__(self, tab_ref, anom_ref, turn_ref, gauge_ref, pairs, early):
        self.count, self.width = anom_ref.shape[0], anom_ref.shape[1] // 2
        self.tab_ref, self.anom_ref, self.turn_ref = tab_ref, anom_ref, turn_ref
        self.gauge_ref = gauge_ref
        self.paired = self.width == 2 * LANES
        self.first_group = 0 if self.paired else pairs + early
        self.first_slot = 0 if self.paired else 2 * pairs

    def group(self, p):
        return self.tab_ref[self.first_group + p]

    def gauges(self, p, rows):
        if self.paired:
            return jnp.concatenate([self.gauge_ref[2 * p, rows], self.gauge_ref[2 * p + 1, rows]], 1)
        return self.gauge_ref[self.first_slot + p, rows]

    def field(self, p):
        return self.gauges(p, slice(0, ROWS))

    def obs(self, p):
        return self.gauges(p, slice(ROWS, ROWS + 1))

    def same_basin(self, p):
        basin = self.gauges(p, slice(ROWS + 1, ROWS + 2))[None]
        ids = lax.broadcasted_iota(jnp.int32, (BASINS, ROWS, self.width), 0)
        return ids.astype(jnp.float32) == basin


def project(pos_ref, parts, fields, sums, acc, outs):
    rows = BASINS * ROWS
    acc[...] = jnp.zeros_like(acc)
    for part, field in zip(parts, fields):
        width = part.width
        for p in range(part.count):
            near = part.same_basin(p)
            v = field(p)
            v_high = v.astype(jnp.bfloat16).astype(jnp.float32)
            high, low = (
                jnp.where(near, u[None], 0.0).reshape(rows, width).astype(jnp.bfloat16)
                for u in (v_high, v - v_high)
            )
            both = jnp.dot(
                jnp.concatenate([high, low], 0), part.anom_ref[p, :width],
                preferred_element_type=jnp.float32,
            )
            third = jnp.dot(high, part.anom_ref[p, width:], preferred_element_type=jnp.float32)
            g = part.group(p)
            acc[g] = acc[g] + (both[:rows] + both[rows:] + third).reshape(acc.shape[1:])
    lane = lax.broadcasted_iota(jnp.int32, (ROWS, acc.shape[3]), 1)
    row = jnp.zeros((ROWS, acc.shape[3]), jnp.float32)
    for place, value in enumerate(sums):
        row = jnp.where(lane == place, value, row)
    me_c, half = pos_ref[0], rows // 2
    for side in range(2):
        core = me_c if side == 0 else 1 - me_c
        for g in range(GROUPS):
            out = outs[2 * side + g // 2]
            out[g % 2 * half : (g % 2 + 1) * half] = acc[g, core]
        outs[2 * side][2 * half :] = row


def lane_sum(v):
    return jnp.sum(v, axis=1, keepdims=True)


def total(values):
    return functools.reduce(lambda a, b: a + b, values)


def first_kernel(shape, *refs):
    pos_ref, tab_ref, gauge_ref, anom_ref, turn_ref = refs[:5]
    late_ref, late_turn, *outs, acc = refs[-7:]
    pieces = refs[5:-7]
    pairs = anom_ref.shape[0]
    early, late = early_blocks(shape), late_blocks(shape)
    rest = jnp.zeros((LANES - pieces[0].shape[1], pieces[0].shape[2]), jnp.float32)
    half = pieces[0].shape[0]
    for k in range(len(late)):
        value = jnp.concatenate([pieces[k // half][k % half], rest], 0)
        late_ref[k, :LANES], late_ref[k, LANES:] = split(value)
        late_turn[k, :, :LANES], late_turn[k, :, LANES:] = split(value.T)
    parts = [
        Part(tab_ref, a, t, gauge_ref, pairs, len(early))
        for a, t in ((anom_ref, turn_ref), (late_ref, late_turn))
    ]
    one, two = [], []
    for part in parts:
        squares = [part.field(p) * part.field(p) for p in range(part.count)]
        one.append(lane_sum(total(squares)))
        two.append(lane_sum(total([s * part.obs(p) for p, s in enumerate(squares)])))
    fields = [part.field for part in parts]
    project(pos_ref, parts, fields, (total(one), total(two)), acc, outs)


def step_kernel(shape, members, first, last, *refs):
    refs = list(refs)

    def take(n):
        taken = refs[:n]
        del refs[:n]
        return taken

    pos_ref, tab_ref, gauge_ref, anom_ref, turn_ref, late_ref, late_turn = take(7)
    own, other = take(2), take(2)
    if not first:
        x_in, r_in, dir_in, scal_in = take(2), take(2), *take(2)
        d_in = take(0 if last is None else 2)
    if last:
        (out_ref,) = take(1)
        e_high, e_low, dir_sum, result = refs
    else:
        x_out, r_out, dir_out, scal_out, outs = take(2), take(2), *take(2), take(4)
        d_out = [] if first else take(2)
        e_high, e_low, acc = refs
        dir_sum = dir_out
    pairs = anom_ref.shape[0]
    wide = anom_ref.shape[2]
    rows = BASINS * ROWS
    early, late = early_blocks(shape), late_blocks(shape)
    parts = [
        Part(tab_ref, a, t, gauge_ref, pairs, len(early))
        for a, t in ((anom_ref, turn_ref), (late_ref, late_turn))
    ]

    me_c, half = pos_ref[0], rows // 2
    row = own[0][2 * half :]
    rr, r_obs_r, r_obs_d = row[:, 0:1], row[:, 1:2], row[:, 2:3]
    if first:
        d_obs_d = r_obs_r
    else:
        beta = rr / scal_in[:, 0:1]
        d_obs_d = r_obs_r + 2.0 * beta * r_obs_d + beta * beta * scal_in[:, 1:2]
    curve = jnp.zeros((ROWS, wide), jnp.float32)
    for g in range(GROUPS):
        halves = []
        for side, core in ((own, me_c), (other, 1 - me_c)):
            d_h = side[g // 2][g % 2 * half : (g % 2 + 1) * half].reshape(-1, ROWS, wide)
            if not first:
                d_h = d_h + beta[None] * dir_in[g, core].reshape(-1, ROWS, wide)
            dir_sum[g, core] = d_h.reshape(half, wide)
            halves.append((core, d_h))
        every = sum(jnp.sum(d_h, axis=0) for _, d_h in halves)
        for core, d_h in halves:
            e_h = (1.0 - far_weight) / (members - 1) * d_h + far_weight / (members - 1) * every[None]
            curve = curve + jnp.sum(d_h * e_h, axis=0)
            e_high[g, core], e_low[g, core] = split(e_h.reshape(half, wide))
    alpha = rr / (lane_sum(curve) + d_obs_d)

    one, two, three = [], [], []
    for k, part in enumerate(parts):
        width = part.width
        squares, weighted, crossed = [], [], []
        for p in range(part.count):
            g = part.group(p)
            e_g = e_high[g].reshape(rows, wide)
            both = jnp.dot(
                jnp.concatenate([e_g.reshape(rows, wide), e_low[g].reshape(rows, wide)], 0),
                part.turn_ref[p, :, :width],
                preferred_element_type=jnp.float32,
            )
            third = jnp.dot(
                e_g, part.turn_ref[p, :, width:], preferred_element_type=jnp.float32
            )
            every = (both[:rows] + both[rows:] + third).reshape(-1, ROWS, width)
            image = jnp.sum(jnp.where(part.same_basin(p), every, 0.0), axis=0)
            obs = part.obs(p)
            if first:
                r = part.field(p)
                d = r
            else:
                r = r_in[k][p]
                d = r + beta * (d_in[k][p] if d_in else part.field(p))
            image = image + obs * d
            x = alpha * d
            if not first:
                x = x_in[k][p] + x
            r = r - alpha * image
            if last:
                for h in range(width // LANES):
                    lanes = slice(h * LANES, (h + 1) * LANES)
                    s = part.first_slot + p * (width // LANES) + h
                    result[s, :ROWS] = x[:, lanes]
                    result[s, ROWS:] = r[:, lanes]
                continue
            x_out[k][p] = x
            r_out[k][p] = r
            if d_out:
                d_out[k][p] = d
            squares.append(r * r)
            weighted.append(r * r * obs)
            crossed.append(r * d * obs)
        if not last:
            one.append(lane_sum(total(squares)))
            two.append(lane_sum(total(weighted)))
            three.append(lane_sum(total(crossed)))
    if last:
        for k, e in enumerate(early):
            out_ref[block_id(pos_ref, shape, *e)] = result[tab_ref[pairs + k]]
        for k, e in enumerate(late):
            out_ref[block_id(pos_ref, shape, *e)] = result[2 * pairs + k]
        return
    lane = lax.broadcasted_iota(jnp.int32, (ROWS, LANES), 1)
    scal_out[...] = jnp.where(lane == 0, rr, d_obs_d)
    fields = [functools.partial(lambda ref, p: ref[p], ref) for ref in r_out]
    project(pos_ref, parts, fields, (total(one), total(two), total(three)), acc, outs)


def shift(v, axis, k):
    n = lax.axis_size(axis)
    return lax.ppermute(v, axis, [(i, (i + k) % n) for i in range(n)])


def swap(v):
    return lax.ppermute(v, "c", [(0, 1), (1, 0)])


EVEN = ((0, 1), (1, 0), (2, 3), (3, 2))
ODD = ((1, 2), (2, 1), (3, 0), (0, 3))


def meet(v, partners):
    return v + lax.ppermute(v, "x", partners)


def total_over_gauges(keep_0, keep_1, send_0, send_1):
    sum_0, sum_1 = keep_0 + swap(send_0), keep_1 + swap(send_1)
    sum_0, sum_1 = meet(sum_0, EVEN), meet(sum_1, ODD)
    sum_0, sum_1 = meet(sum_0, ODD), meet(sum_1, EVEN)
    return sum_0, sum_1, swap(sum_0), swap(sum_1)


def to_all(v, axis):
    n = lax.axis_size(axis)
    return lax.all_to_all(jnp.broadcast_to(v[None], (n,) + v.shape), axis, 0, 0, tiled=True)


def gather(anomalies, pay):
    own = to_all(anomalies, "y")
    below, above = own, own
    early = [own]
    for step in range((lax.axis_size("z") - 1) // 2):
        if step == 2:
            below, above, pay = lax.optimization_barrier((below, above, pay))
        below, above = shift(below, "z", 1), shift(above, "z", -1)
        early += [below, above]
    nz, nc = lax.axis_size("z"), lax.axis_size("c")
    ways = [
        (z * nc + c, (z + (1 if c == 0 else -1)) % nz * nc + c) for z in range(nz) for c in range(nc)
    ]
    far = jnp.where(lax.axis_index("c") == 0, below, above)
    return early, [lax.ppermute(far, ("z", "c"), ways)], pay


def local(anomalies, innovations, obs_var, basins, taper_mask):
    blk, members = anomalies.shape
    shape = tuple(lax.axis_size(a) for a in PEERS)
    peers = shape[0] * shape[1]
    nx, nc = lax.axis_size("x"), lax.axis_size("c")
    me_x, me_c = lax.axis_index("x"), lax.axis_index("c")
    nblocks = taper_mask.shape[0]

    near = taper_mask != 0
    place = jnp.arange(nblocks, dtype=jnp.int32)
    leader = jnp.min(jnp.where(near, place[None, :], nblocks), axis=1)
    leads = (leader == place)[None, :] & (place[None, :] < leader[:, None])
    gid = jnp.sum(leads.astype(jnp.int32), axis=1)
    gid = gid.reshape(nx, shape[0], nc, shape[1])
    gid = lax.dynamic_slice(gid, (me_x, 0, me_c, 0), (1, shape[0], 1, shape[1])).reshape(peers)
    gid = jnp.minimum(gid, GROUPS - 1)
    pos = jnp.stack([me_c, lax.axis_index("z")]).astype(jnp.int32)

    lanes = ((0, 0), (0, LANES - blk))
    field = jnp.pad(innovations.T, lanes).reshape(peers, ROWS, LANES)
    extra = jnp.stack([obs_var, basins.astype(jnp.float32)])
    extra = jnp.pad(extra, ((0, ROWS - 2), (0, LANES - blk)))
    pay = jnp.concatenate([field, jnp.broadcast_to(extra[None], (peers, ROWS, LANES))], 1)
    early, late, pay = gather(anomalies, pay)
    pay = lax.all_to_all(pay, PEERS, 0, 0, tiled=True)

    smem = pl.BlockSpec(memory_space=pltpu.SMEM)
    vmem = pl.BlockSpec(memory_space=pltpu.VMEM)
    f32 = functools.partial(jax.ShapeDtypeStruct, dtype=jnp.float32)
    b16 = functools.partial(jax.ShapeDtypeStruct, dtype=jnp.bfloat16)
    rows = BASINS * ROWS
    n_late = shape[0]
    n_early = peers - n_late
    pairs = (n_early + GROUPS) // 2
    shards = [f32((rows + ROWS, members)), f32((rows, members))] * 2
    state = [f32((pairs, ROWS, 2 * LANES)), f32((n_late, ROWS, LANES))]
    sums = (GROUPS, 2, rows // 2, members)

    def params(mib):
        return pltpu.CompilerParams(vmem_limit_bytes=mib * 2**20)

    tab, gauges, anoms, turned = pl.pallas_call(
        functools.partial(pack_kernel, shape),
        out_shape=(
            jax.ShapeDtypeStruct((pairs + peers,), jnp.int32),
            f32((2 * pairs + n_late, 2 * ROWS, LANES)),
            b16((pairs, 4 * LANES, members)),
            b16((pairs, members, 4 * LANES)),
        ),
        in_specs=[smem, smem] + [vmem] * (1 + len(early)),
        out_specs=(smem, vmem, vmem, vmem),
        scratch_shapes=[pltpu.SMEM((GROUPS,), jnp.int32)],
        compiler_params=params(20),
        cost_estimate=pl.CostEstimate(
            flops=n_early * blk * members * 8, bytes_accessed=n_early * blk * members * 12,
            transcendentals=0,
        ),
        name="pack",
    )(pos, gid, pay, *early)
    late_anoms, late_turned, *parts = pl.pallas_call(
        functools.partial(first_kernel, shape),
        out_shape=(
            b16((n_late, 2 * LANES, members)),
            b16((n_late, members, 2 * LANES)),
            *shards,
        ),
        in_specs=[smem, smem] + [vmem] * (3 + len(late)),
        out_specs=(vmem,) * 6,
        scratch_shapes=[pltpu.VMEM(sums, jnp.float32)],
        compiler_params=params(20),
        name="project",
    )(pos, tab, gauges, anoms, turned, *late)
    common = (pos, tab, gauges, anoms, turned, late_anoms, late_turned)
    carried = ()
    for step in range(ITERS):
        first, last = step == 0, step + 1 == ITERS
        args = (*common, *total_over_gauges(*parts), *carried)
        if last:
            shapes = [f32((peers, 2 * ROWS, LANES))]
            more = [pltpu.VMEM((2 * pairs + n_late, 2 * ROWS, LANES), jnp.float32)]
        else:
            shapes = [*state, *state, f32(sums), f32((ROWS, LANES)), *shards]
            shapes += [] if first else state
            more = []
        has_d = step > 1
        out = pl.pallas_call(
            functools.partial(step_kernel, shape, members, first, last if has_d or first else None),
            out_shape=shapes,
            in_specs=[smem, smem] + [vmem] * (len(args) - 2),
            out_specs=[vmem] * len(shapes),
            scratch_shapes=[
                pltpu.VMEM(sums, jnp.bfloat16),
                pltpu.VMEM(sums, jnp.bfloat16),
                pltpu.VMEM(sums, jnp.float32),
            ] + more,
            compiler_params=params(20),
            name="finish" if last else "step",
        )(*args)
        if not last:
            parts = out[6:10]
            carried = (*out[:6], *out[10:])
    back = lax.all_to_all(out[0], PEERS, 0, 0, tiled=True)
    solution_field, residual = pl.pallas_call(
        out_kernel,
        out_shape=(f32((blk, members)), f32((blk, members))),
        in_specs=[vmem],
        out_specs=(vmem, vmem),
        compiler_params=params(20),
        name="out",
    )(back)
    return solution_field, residual


def solution(mesh):
    fine = Mesh(mesh.devices.reshape(8, 4, 4, 2), ("z", "x", "y", "c"))
    split_all = ("x", "y", "c", "z")
    placed = (P(split_all, None), P(split_all, None), P(split_all), P(split_all), P())
    return jax.shard_map(
        local,
        mesh=fine,
        in_specs=placed,
        out_specs=(P(split_all, None), P(split_all, None)),
        check_vma=False,
    )
```

```python
import functools

import jax
import jax.numpy as jnp
from jax import lax
from jax.experimental import pallas as pl
from jax.experimental.pallas import tpu as pltpu
from jax.sharding import Mesh
from jax.sharding import PartitionSpec as P

ITERS = 3
BASINS = 16
GROUPS = 4
far_weight = 0.3

LANES = 128
ROWS = 8
PEERS = ("y", "z")
EARLY = (0, -1, 1, -2, 2, -3, 3)


def split(v):
    high = v.astype(jnp.bfloat16)
    return high, (v - high.astype(jnp.float32)).astype(jnp.bfloat16)


def block_id(pos_ref, shape, y, step):
    nz = shape[1]
    return y * nz + lax.rem(pos_ref[1] + (step + nz), nz)


def early_blocks(shape):
    return [(y, step) for step in EARLY for y in range(shape[0])]


def late_blocks(shape):
    ny, nz = shape
    return [(y, nz // 2) for y in range(ny)]


def pack_kernel(shape, *refs):
    pos_ref, gid_ref, pay_ref = refs[:3]
    tab_ref, gauge_ref, anom_ref, turn_ref, count = refs[-5:]
    pieces = refs[3:-5]
    ny = shape[0]
    pairs = anom_ref.shape[0]
    early = early_blocks(shape)
    ids = [block_id(pos_ref, shape, *e) for e in early]
    for g in range(GROUPS):
        count[g] = 0
    for i in ids:
        g = gid_ref[i]
        count[g] = count[g] + 1
    for p in range(pairs):
        tab_ref[p] = 0
    start = jnp.int32(0)
    empty = []
    for g in range(GROUPS):
        n = count[g]
        count[g] = 2 * start

        def mark(p, carry, g=g):
            tab_ref[p] = g
            return carry

        end = start + lax.div(n + 1, 2)
        lax.fori_loop(start, end, mark, 0)
        empty.append((lax.rem(n, 2) == 1, 2 * end - 1))
        start = end

    def put(s, value):
        high, low = split(value)
        p, h = lax.div(s, 2), lax.rem(s, 2)
        first = pl.ds(pl.multiple_of(h * LANES, LANES), LANES)
        second = pl.ds(pl.multiple_of((2 + h) * LANES, LANES), LANES)
        anom_ref[p, first] = high
        anom_ref[p, second] = low
        high, low = split(value.T)
        turn_ref[p, :, first] = high
        turn_ref[p, :, second] = low

    blank = jnp.zeros((LANES, anom_ref.shape[2]), jnp.float32)
    for odd, s in empty:
        pl.when(odd)(functools.partial(put, s, blank))

    def clear(s, carry):
        put(s, blank)
        return carry

    lax.fori_loop(2 * start, 2 * pairs, clear, 0)
    gauge_ref[...] = jnp.zeros_like(gauge_ref)
    rest = blank[pieces[0].shape[1] :]
    for k, i in enumerate(ids):
        g = gid_ref[i]
        s = count[g]
        count[g] = s + 1
        tab_ref[pairs + k] = s
        gauge_ref[s, : ROWS + 2] = pay_ref[i]
        put(s, jnp.concatenate([pieces[k // ny][k % ny], rest], 0))
    for k, e in enumerate(late_blocks(shape)):
        i = block_id(pos_ref, shape, *e)
        tab_ref[pairs + len(ids) + k] = gid_ref[i]
        gauge_ref[2 * pairs + k, : ROWS + 2] = pay_ref[i]


def out_kernel(back_ref, x_ref, r_ref):
    for out, rows in ((x_ref, slice(0, ROWS)), (r_ref, slice(ROWS, 2 * ROWS))):
        for k in range(0, back_ref.shape[0], LANES // ROWS):
            tile = back_ref[k : k + LANES // ROWS, rows].reshape(LANES, LANES).T
            out[:, k * ROWS : k * ROWS + LANES] = tile[: out.shape[0]]


class Part:
    def __init__(self, tab_ref, anom_ref, turn_ref, gauge_ref, pairs, early):
        self.count, self.width = anom_ref.shape[0], anom_ref.shape[1] // 2
        self.tab_ref, self.anom_ref, self.turn_ref = tab_ref, anom_ref, turn_ref
        self.gauge_ref = gauge_ref
        self.paired = self.width == 2 * LANES
        self.first_group = 0 if self.paired else pairs + early
        self.first_slot = 0 if self.paired else 2 * pairs

    def group(self, p):
        return self.tab_ref[self.first_group + p]

    def gauges(self, p, rows):
        if self.paired:
            return jnp.concatenate([self.gauge_ref[2 * p, rows], self.gauge_ref[2 * p + 1, rows]], 1)
        return self.gauge_ref[self.first_slot + p, rows]

    def field(self, p):
        return self.gauges(p, slice(0, ROWS))

    def obs(self, p):
        return self.gauges(p, slice(ROWS, ROWS + 1))

    def same_basin(self, p):
        basin = self.gauges(p, slice(ROWS + 1, ROWS + 2))[None]
        ids = lax.broadcasted_iota(jnp.int32, (BASINS, ROWS, self.width), 0)
        return ids.astype(jnp.float32) == basin


def project(pos_ref, parts, fields, sums, acc, outs):
    rows = BASINS * ROWS
    acc[...] = jnp.zeros_like(acc)
    for part, field in zip(parts, fields):
        width = part.width
        for p in range(part.count):
            near = part.same_basin(p)
            v = field(p)
            v_high = v.astype(jnp.bfloat16).astype(jnp.float32)
            high, low = (
                jnp.where(near, u[None], 0.0).reshape(rows, width).astype(jnp.bfloat16)
                for u in (v_high, v - v_high)
            )
            both = jnp.dot(
                jnp.concatenate([high, low], 0), part.anom_ref[p, :width],
                preferred_element_type=jnp.float32,
            )
            third = jnp.dot(high, part.anom_ref[p, width:], preferred_element_type=jnp.float32)
            g = part.group(p)
            acc[g] = acc[g] + (both[:rows] + both[rows:] + third).reshape(acc.shape[1:])
    lane = lax.broadcasted_iota(jnp.int32, (ROWS, acc.shape[3]), 1)
    row = jnp.zeros((ROWS, acc.shape[3]), jnp.float32)
    for place, value in enumerate(sums):
        row = jnp.where(lane == place, value, row)
    me_c, half = pos_ref[0], rows // 2
    for side in range(2):
        core = me_c if side == 0 else 1 - me_c
        for g in range(GROUPS):
            out = outs[2 * side + g // 2]
            out[g % 2 * half : (g % 2 + 1) * half] = acc[g, core]
        outs[2 * side][2 * half :] = row


def lane_sum(v):
    return jnp.sum(v, axis=1, keepdims=True)


def total(values):
    return functools.reduce(lambda a, b: a + b, values)


def first_kernel(shape, *refs):
    pos_ref, tab_ref, gauge_ref, anom_ref, turn_ref = refs[:5]
    late_ref, late_turn, *outs, acc = refs[-7:]
    pieces = refs[5:-7]
    pairs = anom_ref.shape[0]
    early, late = early_blocks(shape), late_blocks(shape)
    rest = jnp.zeros((LANES - pieces[0].shape[1], pieces[0].shape[2]), jnp.float32)
    half = pieces[0].shape[0]
    for k in range(len(late)):
        value = jnp.concatenate([pieces[k // half][k % half], rest], 0)
        late_ref[k, :LANES], late_ref[k, LANES:] = split(value)
        late_turn[k, :, :LANES], late_turn[k, :, LANES:] = split(value.T)
    parts = [
        Part(tab_ref, a, t, gauge_ref, pairs, len(early))
        for a, t in ((anom_ref, turn_ref), (late_ref, late_turn))
    ]
    one, two = [], []
    for part in parts:
        squares = [part.field(p) * part.field(p) for p in range(part.count)]
        one.append(lane_sum(total(squares)))
        two.append(lane_sum(total([s * part.obs(p) for p, s in enumerate(squares)])))
    fields = [part.field for part in parts]
    project(pos_ref, parts, fields, (total(one), total(two)), acc, outs)


def step_kernel(shape, members, first, last, *refs):
    refs = list(refs)

    def take(n):
        taken = refs[:n]
        del refs[:n]
        return taken

    pos_ref, tab_ref, gauge_ref, anom_ref, turn_ref, late_ref, late_turn = take(7)
    own, other = take(2), take(2)
    if not first:
        x_in, r_in, dir_in, scal_in = take(2), take(2), *take(2)
        d_in = take(0 if last is None else 2)
    if last:
        (out_ref,) = take(1)
        e_high, e_low, dir_sum, result = refs
    else:
        x_out, r_out, dir_out, scal_out, outs = take(2), take(2), *take(2), take(4)
        d_out = [] if first else take(2)
        e_high, e_low, acc = refs
        dir_sum = dir_out
    pairs = anom_ref.shape[0]
    wide = anom_ref.shape[2]
    rows = BASINS * ROWS
    early, late = early_blocks(shape), late_blocks(shape)
    parts = [
        Part(tab_ref, a, t, gauge_ref, pairs, len(early))
        for a, t in ((anom_ref, turn_ref), (late_ref, late_turn))
    ]

    me_c, half = pos_ref[0], rows // 2
    row = own[0][2 * half :]
    rr, r_obs_r, r_obs_d = row[:, 0:1], row[:, 1:2], row[:, 2:3]
    if first:
        d_obs_d = r_obs_r
    else:
        beta = rr / scal_in[:, 0:1]
        d_obs_d = r_obs_r + 2.0 * beta * r_obs_d + beta * beta * scal_in[:, 1:2]
    curve = jnp.zeros((ROWS, wide), jnp.float32)
    for g in range(GROUPS):
        halves = []
        for side, core in ((own, me_c), (other, 1 - me_c)):
            d_h = side[g // 2][g % 2 * half : (g % 2 + 1) * half].reshape(-1, ROWS, wide)
            if not first:
                d_h = d_h + beta[None] * dir_in[g, core].reshape(-1, ROWS, wide)
            dir_sum[g, core] = d_h.reshape(half, wide)
            halves.append((core, d_h))
        every = sum(jnp.sum(d_h, axis=0) for _, d_h in halves)
        for core, d_h in halves:
            e_h = (1.0 - far_weight) / (members - 1) * d_h + far_weight / (members - 1) * every[None]
            curve = curve + jnp.sum(d_h * e_h, axis=0)
            e_high[g, core], e_low[g, core] = split(e_h.reshape(half, wide))
    alpha = rr / (lane_sum(curve) + d_obs_d)

    one, two, three = [], [], []
    for k, part in enumerate(parts):
        width = part.width
        squares, weighted, crossed = [], [], []
        for p in range(part.count):
            g = part.group(p)
            e_g = e_high[g].reshape(rows, wide)
            both = jnp.dot(
                jnp.concatenate([e_g.reshape(rows, wide), e_low[g].reshape(rows, wide)], 0),
                part.turn_ref[p, :, :width],
                preferred_element_type=jnp.float32,
            )
            third = jnp.dot(
                e_g, part.turn_ref[p, :, width:], preferred_element_type=jnp.float32
            )
            every = (both[:rows] + both[rows:] + third).reshape(-1, ROWS, width)
            image = jnp.sum(jnp.where(part.same_basin(p), every, 0.0), axis=0)
            obs = part.obs(p)
            if first:
                r = part.field(p)
                d = r
            else:
                r = r_in[k][p]
                d = r + beta * (d_in[k][p] if d_in else part.field(p))
            image = image + obs * d
            x = alpha * d
            if not first:
                x = x_in[k][p] + x
            r = r - alpha * image
            if last:
                for h in range(width // LANES):
                    lanes = slice(h * LANES, (h + 1) * LANES)
                    s = part.first_slot + p * (width // LANES) + h
                    result[s, :ROWS] = x[:, lanes]
                    result[s, ROWS:] = r[:, lanes]
                continue
            x_out[k][p] = x
            r_out[k][p] = r
            if d_out:
                d_out[k][p] = d
            squares.append(r * r)
            weighted.append(r * r * obs)
            crossed.append(r * d * obs)
        if not last:
            one.append(lane_sum(total(squares)))
            two.append(lane_sum(total(weighted)))
            three.append(lane_sum(total(crossed)))
    if last:
        for k, e in enumerate(early):
            out_ref[block_id(pos_ref, shape, *e)] = result[tab_ref[pairs + k]]
        for k, e in enumerate(late):
            out_ref[block_id(pos_ref, shape, *e)] = result[2 * pairs + k]
        return
    lane = lax.broadcasted_iota(jnp.int32, (ROWS, LANES), 1)
    scal_out[...] = jnp.where(lane == 0, rr, d_obs_d)
    fields = [functools.partial(lambda ref, p: ref[p], ref) for ref in r_out]
    project(pos_ref, parts, fields, (total(one), total(two), total(three)), acc, outs)


def shift(v, axis, k):
    n = lax.axis_size(axis)
    return lax.ppermute(v, axis, [(i, (i + k) % n) for i in range(n)])


def swap(v):
    return lax.ppermute(v, "c", [(0, 1), (1, 0)])


EVEN = ((0, 1), (1, 0), (2, 3), (3, 2))
ODD = ((1, 2), (2, 1), (3, 0), (0, 3))


def meet(v, partners):
    return v + lax.ppermute(v, "x", partners)


def total_over_gauges(keep_0, keep_1, send_0, send_1):
    sum_0, sum_1 = keep_0 + swap(send_0), keep_1 + swap(send_1)
    sum_0, sum_1 = meet(sum_0, EVEN), meet(sum_1, ODD)
    sum_0, sum_1 = meet(sum_0, ODD), meet(sum_1, EVEN)
    return sum_0, sum_1, swap(sum_0), swap(sum_1)


def to_all(v, axis):
    n = lax.axis_size(axis)
    return lax.all_to_all(jnp.broadcast_to(v[None], (n,) + v.shape), axis, 0, 0, tiled=True)


def gather(anomalies, pay):
    own = to_all(anomalies, "y")
    below, above = own, own
    early = [own]
    for step in range((lax.axis_size("z") - 1) // 2):
        if step == 2:
            below, above, pay = lax.optimization_barrier((below, above, pay))
        below, above = shift(below, "z", 1), shift(above, "z", -1)
        early += [below, above]
    nz, nc = lax.axis_size("z"), lax.axis_size("c")
    ways = [
        (z * nc + c, (z + (1 if c == 0 else -1)) % nz * nc + c) for z in range(nz) for c in range(nc)
    ]
    far = jnp.where(lax.axis_index("c") == 0, below, above)
    return early, [lax.ppermute(far, ("z", "c"), ways)], pay


def local(anomalies, innovations, obs_var, basins, taper_mask):
    blk, members = anomalies.shape
    shape = tuple(lax.axis_size(a) for a in PEERS)
    peers = shape[0] * shape[1]
    nx, nc = lax.axis_size("x"), lax.axis_size("c")
    me_x, me_c = lax.axis_index("x"), lax.axis_index("c")
    nblocks = taper_mask.shape[0]

    near = taper_mask != 0
    place = jnp.arange(nblocks, dtype=jnp.int32)
    leader = jnp.min(jnp.where(near, place[None, :], nblocks), axis=1)
    leads = (leader == place)[None, :] & (place[None, :] < leader[:, None])
    gid = jnp.sum(leads.astype(jnp.int32), axis=1)
    gid = gid.reshape(nx, shape[0], nc, shape[1])
    gid = lax.dynamic_slice(gid, (me_x, 0, me_c, 0), (1, shape[0], 1, shape[1])).reshape(peers)
    gid = jnp.minimum(gid, GROUPS - 1)
    pos = jnp.stack([me_c, lax.axis_index("z")]).astype(jnp.int32)

    lanes = ((0, 0), (0, LANES - blk))
    field = jnp.pad(innovations.T, lanes).reshape(peers, ROWS, LANES)
    extra = jnp.stack([obs_var, basins.astype(jnp.float32)])
    extra = jnp.pad(extra, lanes)
    pay = jnp.concatenate([field, jnp.broadcast_to(extra[None], (peers, 2, LANES))], 1)
    early, late, pay = gather(anomalies, pay)
    pay = lax.all_to_all(pay, PEERS, 0, 0, tiled=True)

    smem = pl.BlockSpec(memory_space=pltpu.SMEM)
    vmem = pl.BlockSpec(memory_space=pltpu.VMEM)
    f32 = functools.partial(jax.ShapeDtypeStruct, dtype=jnp.float32)
    b16 = functools.partial(jax.ShapeDtypeStruct, dtype=jnp.bfloat16)
    rows = BASINS * ROWS
    n_late = shape[0]
    n_early = peers - n_late
    pairs = (n_early + GROUPS) // 2
    shards = [f32((rows + ROWS, members)), f32((rows, members))] * 2
    state = [f32((pairs, ROWS, 2 * LANES)), f32((n_late, ROWS, LANES))]
    sums = (GROUPS, 2, rows // 2, members)

    def params(mib):
        return pltpu.CompilerParams(vmem_limit_bytes=mib * 2**20)

    tab, gauges, anoms, turned = pl.pallas_call(
        functools.partial(pack_kernel, shape),
        out_shape=(
            jax.ShapeDtypeStruct((pairs + peers,), jnp.int32),
            f32((2 * pairs + n_late, 2 * ROWS, LANES)),
            b16((pairs, 4 * LANES, members)),
            b16((pairs, members, 4 * LANES)),
        ),
        in_specs=[smem, smem] + [vmem] * (1 + len(early)),
        out_specs=(smem, vmem, vmem, vmem),
        scratch_shapes=[pltpu.SMEM((GROUPS,), jnp.int32)],
        compiler_params=params(20),
        cost_estimate=pl.CostEstimate(
            flops=n_early * blk * members * 8, bytes_accessed=n_early * blk * members * 12,
            transcendentals=0,
        ),
        name="pack",
    )(pos, gid, pay, *early)
    late_anoms, late_turned, *parts = pl.pallas_call(
        functools.partial(first_kernel, shape),
        out_shape=(
            b16((n_late, 2 * LANES, members)),
            b16((n_late, members, 2 * LANES)),
            *shards,
        ),
        in_specs=[smem, smem] + [vmem] * (3 + len(late)),
        out_specs=(vmem,) * 6,
        scratch_shapes=[pltpu.VMEM(sums, jnp.float32)],
        compiler_params=params(20),
        name="project",
    )(pos, tab, gauges, anoms, turned, *late)
    common = (pos, tab, gauges, anoms, turned, late_anoms, late_turned)
    carried = ()
    for step in range(ITERS):
        first, last = step == 0, step + 1 == ITERS
        args = (*common, *total_over_gauges(*parts), *carried)
        if last:
            shapes = [f32((peers, 2 * ROWS, LANES))]
            more = [pltpu.VMEM((2 * pairs + n_late, 2 * ROWS, LANES), jnp.float32)]
        else:
            shapes = [*state, *state, f32(sums), f32((ROWS, LANES)), *shards]
            shapes += [] if first else state
            more = []
        has_d = step > 1
        out = pl.pallas_call(
            functools.partial(step_kernel, shape, members, first, last if has_d or first else None),
            out_shape=shapes,
            in_specs=[smem, smem] + [vmem] * (len(args) - 2),
            out_specs=[vmem] * len(shapes),
            scratch_shapes=[
                pltpu.VMEM(sums, jnp.bfloat16),
                pltpu.VMEM(sums, jnp.bfloat16),
                pltpu.VMEM(sums, jnp.float32),
            ] + more,
            compiler_params=params(20),
            name="finish" if last else "step",
        )(*args)
        if not last:
            parts = out[6:10]
            carried = (*out[:6], *out[10:])
    back = lax.all_to_all(out[0], PEERS, 0, 0, tiled=True)
    solution_field, residual = pl.pallas_call(
        out_kernel,
        out_shape=(f32((blk, members)), f32((blk, members))),
        in_specs=[vmem],
        out_specs=(vmem, vmem),
        compiler_params=params(20),
        name="out",
    )(back)
    return solution_field, residual


def solution(mesh):
    fine = Mesh(mesh.devices.reshape(8, 4, 4, 2), ("z", "x", "y", "c"))
    split_all = ("x", "y", "c", "z")
    placed = (P(split_all, None), P(split_all, None), P(split_all), P(split_all), P())
    return jax.shard_map(
        local,
        mesh=fine,
        in_specs=placed,
        out_specs=(P(split_all, None), P(split_all, None)),
        check_vma=False,
    )
```

```python
import functools

import jax
import jax.numpy as jnp
from jax import lax
from jax.experimental import pallas as pl
from jax.experimental.pallas import tpu as pltpu
from jax.sharding import Mesh
from jax.sharding import PartitionSpec as P

ITERS = 3
BASINS = 16
GROUPS = 4
far_weight = 0.3

LANES = 128
ROWS = 8
PEERS = ("y", "z")
EARLY = (0, -1, 1, -2, 2, -3, 3)


def split(v):
    high = v.astype(jnp.bfloat16)
    return high, (v - high.astype(jnp.float32)).astype(jnp.bfloat16)


def block_id(pos_ref, shape, y, step):
    nz = shape[1]
    return y * nz + lax.rem(pos_ref[1] + (step + nz), nz)


def early_blocks(shape):
    return [(y, step) for step in EARLY for y in range(shape[0])]


def late_blocks(shape):
    ny, nz = shape
    return [(y, nz // 2) for y in range(ny)]


def pack_kernel(shape, *refs):
    pos_ref, gid_ref, pay_ref = refs[:3]
    tab_ref, gauge_ref, anom_ref, turn_ref, count = refs[-5:]
    pieces = refs[3:-5]
    ny = shape[0]
    pairs = anom_ref.shape[0]
    early = early_blocks(shape)
    ids = [block_id(pos_ref, shape, *e) for e in early]
    for g in range(GROUPS):
        count[g] = 0
    for i in ids:
        g = gid_ref[i]
        count[g] = count[g] + 1
    for p in range(pairs):
        tab_ref[p] = 0
    start = jnp.int32(0)
    empty = []
    for g in range(GROUPS):
        n = count[g]
        count[g] = 2 * start

        def mark(p, carry, g=g):
            tab_ref[p] = g
            return carry

        end = start + lax.div(n + 1, 2)
        lax.fori_loop(start, end, mark, 0)
        empty.append((lax.rem(n, 2) == 1, 2 * end - 1))
        start = end

    def put(s, value):
        high, low = split(value)
        p, h = lax.div(s, 2), lax.rem(s, 2)
        first = pl.ds(pl.multiple_of(h * LANES, LANES), LANES)
        second = pl.ds(pl.multiple_of((2 + h) * LANES, LANES), LANES)
        anom_ref[p, first] = high
        anom_ref[p, second] = low
        high, low = split(value.T)
        turn_ref[p, :, first] = high
        turn_ref[p, :, second] = low

    blank = jnp.zeros((LANES, anom_ref.shape[2]), jnp.float32)
    for odd, s in empty:
        pl.when(odd)(functools.partial(put, s, blank))

    def clear(s, carry):
        put(s, blank)
        return carry

    lax.fori_loop(2 * start, 2 * pairs, clear, 0)
    gauge_ref[...] = jnp.zeros_like(gauge_ref)
    rest = blank[pieces[0].shape[1] :]
    for k, i in enumerate(ids):
        g = gid_ref[i]
        s = count[g]
        count[g] = s + 1
        tab_ref[pairs + k] = s
        gauge_ref[s] = pay_ref[i]
        put(s, jnp.concatenate([pieces[k // ny][k % ny], rest], 0))
    for k, e in enumerate(late_blocks(shape)):
        i = block_id(pos_ref, shape, *e)
        tab_ref[pairs + len(ids) + k] = gid_ref[i]
        gauge_ref[2 * pairs + k] = pay_ref[i]


def out_kernel(back_ref, x_ref, r_ref):
    for out, rows in ((x_ref, slice(0, ROWS)), (r_ref, slice(ROWS, 2 * ROWS))):
        for k in range(0, back_ref.shape[0], LANES // ROWS):
            tile = back_ref[k : k + LANES // ROWS, rows].reshape(LANES, LANES).T
            out[:, k * ROWS : k * ROWS + LANES] = tile[: out.shape[0]]


class Part:
    def __init__(self, tab_ref, anom_ref, turn_ref, gauge_ref, pairs, early):
        self.count, self.width = anom_ref.shape[0], anom_ref.shape[1] // 2
        self.tab_ref, self.anom_ref, self.turn_ref = tab_ref, anom_ref, turn_ref
        self.gauge_ref = gauge_ref
        self.paired = self.width == 2 * LANES
        self.first_group = 0 if self.paired else pairs + early
        self.first_slot = 0 if self.paired else 2 * pairs

    def group(self, p):
        return self.tab_ref[self.first_group + p]

    def gauges(self, p, rows):
        if self.paired:
            return jnp.concatenate([self.gauge_ref[2 * p, rows], self.gauge_ref[2 * p + 1, rows]], 1)
        return self.gauge_ref[self.first_slot + p, rows]

    def field(self, p):
        return self.gauges(p, slice(0, ROWS))

    def obs(self, p):
        return self.gauges(p, slice(ROWS, ROWS + 1))

    def same_basin(self, p):
        basin = self.gauges(p, slice(ROWS + 1, ROWS + 2))[None]
        ids = lax.broadcasted_iota(jnp.int32, (BASINS, ROWS, self.width), 0)
        return ids.astype(jnp.float32) == basin


def project(pos_ref, parts, fields, sums, acc, outs):
    rows = BASINS * ROWS
    acc[...] = jnp.zeros_like(acc)
    for part, field in zip(parts, fields):
        width = part.width
        for p in range(part.count):
            near = part.same_basin(p)
            v = field(p)
            v_high = v.astype(jnp.bfloat16).astype(jnp.float32)
            high, low = (
                jnp.where(near, u[None], 0.0).reshape(rows, width).astype(jnp.bfloat16)
                for u in (v_high, v - v_high)
            )
            both = jnp.dot(
                jnp.concatenate([high, low], 0), part.anom_ref[p, :width],
                preferred_element_type=jnp.float32,
            )
            third = jnp.dot(high, part.anom_ref[p, width:], preferred_element_type=jnp.float32)
            g = part.group(p)
            acc[g] = acc[g] + (both[:rows] + both[rows:] + third).reshape(acc.shape[1:])
    lane = lax.broadcasted_iota(jnp.int32, (ROWS, acc.shape[3]), 1)
    row = jnp.zeros((ROWS, acc.shape[3]), jnp.float32)
    for place, value in enumerate(sums):
        row = jnp.where(lane == place, value, row)
    me_c, half = pos_ref[0], rows // 2
    for side in range(2):
        core = me_c if side == 0 else 1 - me_c
        for g in range(GROUPS):
            out = outs[2 * side + g // 2]
            out[g % 2 * half : (g % 2 + 1) * half] = acc[g, core]
        outs[2 * side][2 * half :] = row


def lane_sum(v):
    return jnp.sum(v, axis=1, keepdims=True)


def total(values):
    return functools.reduce(lambda a, b: a + b, values)


def first_kernel(shape, *refs):
    pos_ref, tab_ref, gauge_ref, anom_ref, turn_ref = refs[:5]
    late_ref, late_turn, *outs, acc = refs[-7:]
    pieces = refs[5:-7]
    pairs = anom_ref.shape[0]
    early, late = early_blocks(shape), late_blocks(shape)
    rest = jnp.zeros((LANES - pieces[0].shape[1], pieces[0].shape[2]), jnp.float32)
    half = pieces[0].shape[0]
    for k in range(len(late)):
        value = jnp.concatenate([pieces[k // half][k % half], rest], 0)
        late_ref[k, :LANES], late_ref[k, LANES:] = split(value)
        late_turn[k, :, :LANES], late_turn[k, :, LANES:] = split(value.T)
    parts = [
        Part(tab_ref, a, t, gauge_ref, pairs, len(early))
        for a, t in ((anom_ref, turn_ref), (late_ref, late_turn))
    ]
    one, two = [], []
    for part in parts:
        squares = [part.field(p) * part.field(p) for p in range(part.count)]
        one.append(lane_sum(total(squares)))
        two.append(lane_sum(total([s * part.obs(p) for p, s in enumerate(squares)])))
    fields = [part.field for part in parts]
    project(pos_ref, parts, fields, (total(one), total(two)), acc, outs)


def step_kernel(shape, members, first, last, *refs):
    refs = list(refs)

    def take(n):
        taken = refs[:n]
        del refs[:n]
        return taken

    pos_ref, tab_ref, gauge_ref, anom_ref, turn_ref, late_ref, late_turn = take(7)
    own, other = take(2), take(2)
    if not first:
        x_in, r_in, dir_in, scal_in = take(2), take(2), *take(2)
        d_in = take(0 if last is None else 2)
    if last:
        (out_ref,) = take(1)
        e_high, e_low, dir_sum, result = refs
    else:
        x_out, r_out, dir_out, scal_out, outs = take(2), take(2), *take(2), take(4)
        d_out = [] if first else take(2)
        e_high, e_low, acc = refs
        dir_sum = dir_out
    pairs = anom_ref.shape[0]
    wide = anom_ref.shape[2]
    rows = BASINS * ROWS
    early, late = early_blocks(shape), late_blocks(shape)
    parts = [
        Part(tab_ref, a, t, gauge_ref, pairs, len(early))
        for a, t in ((anom_ref, turn_ref), (late_ref, late_turn))
    ]

    me_c, half = pos_ref[0], rows // 2
    row = own[0][2 * half :]
    rr, r_obs_r, r_obs_d = row[:, 0:1], row[:, 1:2], row[:, 2:3]
    if first:
        d_obs_d = r_obs_r
    else:
        beta = rr / scal_in[:, 0:1]
        d_obs_d = r_obs_r + 2.0 * beta * r_obs_d + beta * beta * scal_in[:, 1:2]
    curve = jnp.zeros((ROWS, wide), jnp.float32)
    for g in range(GROUPS):
        halves = []
        for side, core in ((own, me_c), (other, 1 - me_c)):
            d_h = side[g // 2][g % 2 * half : (g % 2 + 1) * half].reshape(-1, ROWS, wide)
            if not first:
                d_h = d_h + beta[None] * dir_in[g, core].reshape(-1, ROWS, wide)
            dir_sum[g, core] = d_h.reshape(half, wide)
            halves.append((core, d_h))
        every = sum(jnp.sum(d_h, axis=0) for _, d_h in halves)
        for core, d_h in halves:
            e_h = (1.0 - far_weight) / (members - 1) * d_h + far_weight / (members - 1) * every[None]
            curve = curve + jnp.sum(d_h * e_h, axis=0)
            e_high[g, core], e_low[g, core] = split(e_h.reshape(half, wide))
    alpha = rr / (lane_sum(curve) + d_obs_d)

    one, two, three = [], [], []
    for k, part in enumerate(parts):
        width = part.width
        squares, weighted, crossed = [], [], []
        for p in range(part.count):
            g = part.group(p)
            e_g = e_high[g].reshape(rows, wide)
            both = jnp.dot(
                jnp.concatenate([e_g.reshape(rows, wide), e_low[g].reshape(rows, wide)], 0),
                part.turn_ref[p, :, :width],
                preferred_element_type=jnp.float32,
            )
            third = jnp.dot(
                e_g, part.turn_ref[p, :, width:], preferred_element_type=jnp.float32
            )
            every = (both[:rows] + both[rows:] + third).reshape(-1, ROWS, width)
            image = jnp.sum(jnp.where(part.same_basin(p), every, 0.0), axis=0)
            obs = part.obs(p)
            if first:
                r = part.field(p)
                d = r
            else:
                r = r_in[k][p]
                d = r + beta * (d_in[k][p] if d_in else part.field(p))
            image = image + obs * d
            x = alpha * d
            if not first:
                x = x_in[k][p] + x
            r = r - alpha * image
            if last:
                for h in range(width // LANES):
                    lanes = slice(h * LANES, (h + 1) * LANES)
                    s = part.first_slot + p * (width // LANES) + h
                    result[s, :ROWS] = x[:, lanes]
                    result[s, ROWS:] = r[:, lanes]
                continue
            x_out[k][p] = x
            r_out[k][p] = r
            if d_out:
                d_out[k][p] = d
            squares.append(r * r)
            weighted.append(r * r * obs)
            crossed.append(r * d * obs)
        if not last:
            one.append(lane_sum(total(squares)))
            two.append(lane_sum(total(weighted)))
            three.append(lane_sum(total(crossed)))
    if last:
        for k, e in enumerate(early):
            out_ref[block_id(pos_ref, shape, *e)] = result[tab_ref[pairs + k]]
        for k, e in enumerate(late):
            out_ref[block_id(pos_ref, shape, *e)] = result[2 * pairs + k]
        return
    lane = lax.broadcasted_iota(jnp.int32, (ROWS, LANES), 1)
    scal_out[...] = jnp.where(lane == 0, rr, d_obs_d)
    fields = [functools.partial(lambda ref, p: ref[p], ref) for ref in r_out]
    project(pos_ref, parts, fields, (total(one), total(two), total(three)), acc, outs)


def shift(v, axis, k):
    n = lax.axis_size(axis)
    return lax.ppermute(v, axis, [(i, (i + k) % n) for i in range(n)])


def swap(v):
    return lax.ppermute(v, "c", [(0, 1), (1, 0)])


EVEN = ((0, 1), (1, 0), (2, 3), (3, 2))
ODD = ((1, 2), (2, 1), (3, 0), (0, 3))


def meet(v, partners):
    return v + lax.ppermute(v, "x", partners)


def total_over_gauges(keep_0, keep_1, send_0, send_1):
    sum_0, sum_1 = keep_0 + swap(send_0), keep_1 + swap(send_1)
    sum_0, sum_1 = meet(sum_0, EVEN), meet(sum_1, ODD)
    sum_0, sum_1 = meet(sum_0, ODD), meet(sum_1, EVEN)
    return sum_0, sum_1, swap(sum_0), swap(sum_1)


def to_all(v, axis):
    n = lax.axis_size(axis)
    return lax.all_to_all(jnp.broadcast_to(v[None], (n,) + v.shape), axis, 0, 0, tiled=True)


def gather(anomalies, pay):
    own = to_all(anomalies, "y")
    below, above = own, own
    early = [own]
    for step in range((lax.axis_size("z") - 1) // 2):
        if step == 1:
            below, above, pay = lax.optimization_barrier((below, above, pay))
        below, above = shift(below, "z", 1), shift(above, "z", -1)
        early += [below, above]
    nz, nc = lax.axis_size("z"), lax.axis_size("c")
    ways = [
        (z * nc + c, (z + (1 if c == 0 else -1)) % nz * nc + c) for z in range(nz) for c in range(nc)
    ]
    far = jnp.where(lax.axis_index("c") == 0, below, above)
    return early, [lax.ppermute(far, ("z", "c"), ways)], pay


def local(anomalies, innovations, obs_var, basins, taper_mask):
    blk, members = anomalies.shape
    shape = tuple(lax.axis_size(a) for a in PEERS)
    peers = shape[0] * shape[1]
    nx, nc = lax.axis_size("x"), lax.axis_size("c")
    me_x, me_c = lax.axis_index("x"), lax.axis_index("c")
    nblocks = taper_mask.shape[0]

    near = taper_mask != 0
    place = jnp.arange(nblocks, dtype=jnp.int32)
    leader = jnp.min(jnp.where(near, place[None, :], nblocks), axis=1)
    leads = (leader == place)[None, :] & (place[None, :] < leader[:, None])
    gid = jnp.sum(leads.astype(jnp.int32), axis=1)
    gid = gid.reshape(nx, shape[0], nc, shape[1])
    gid = lax.dynamic_slice(gid, (me_x, 0, me_c, 0), (1, shape[0], 1, shape[1])).reshape(peers)
    gid = jnp.minimum(gid, GROUPS - 1)
    pos = jnp.stack([me_c, lax.axis_index("z")]).astype(jnp.int32)

    lanes = ((0, 0), (0, LANES - blk))
    field = jnp.pad(innovations.T, lanes).reshape(peers, ROWS, LANES)
    extra = jnp.stack([obs_var, basins.astype(jnp.float32)])
    extra = jnp.pad(extra, ((0, ROWS - 2), (0, LANES - blk)))
    pay = jnp.concatenate([field, jnp.broadcast_to(extra[None], (peers, ROWS, LANES))], 1)
    early, late, pay = gather(anomalies, pay)
    pay = lax.all_to_all(pay, PEERS, 0, 0, tiled=True)

    smem = pl.BlockSpec(memory_space=pltpu.SMEM)
    vmem = pl.BlockSpec(memory_space=pltpu.VMEM)
    f32 = functools.partial(jax.ShapeDtypeStruct, dtype=jnp.float32)
    b16 = functools.partial(jax.ShapeDtypeStruct, dtype=jnp.bfloat16)
    rows = BASINS * ROWS
    n_late = shape[0]
    n_early = peers - n_late
    pairs = (n_early + GROUPS) // 2
    shards = [f32((rows + ROWS, members)), f32((rows, members))] * 2
    state = [f32((pairs, ROWS, 2 * LANES)), f32((n_late, ROWS, LANES))]
    sums = (GROUPS, 2, rows // 2, members)

    def params(mib):
        return pltpu.CompilerParams(vmem_limit_bytes=mib * 2**20)

    tab, gauges, anoms, turned = pl.pallas_call(
        functools.partial(pack_kernel, shape),
        out_shape=(
            jax.ShapeDtypeStruct((pairs + peers,), jnp.int32),
            f32((2 * pairs + n_late, 2 * ROWS, LANES)),
            b16((pairs, 4 * LANES, members)),
            b16((pairs, members, 4 * LANES)),
        ),
        in_specs=[smem, smem] + [vmem] * (1 + len(early)),
        out_specs=(smem, vmem, vmem, vmem),
        scratch_shapes=[pltpu.SMEM((GROUPS,), jnp.int32)],
        compiler_params=params(20),
        cost_estimate=pl.CostEstimate(
            flops=n_early * blk * members * 8, bytes_accessed=n_early * blk * members * 12,
            transcendentals=0,
        ),
        name="pack",
    )(pos, gid, pay, *early)
    late_anoms, late_turned, *parts = pl.pallas_call(
        functools.partial(first_kernel, shape),
        out_shape=(
            b16((n_late, 2 * LANES, members)),
            b16((n_late, members, 2 * LANES)),
            *shards,
        ),
        in_specs=[smem, smem] + [vmem] * (3 + len(late)),
        out_specs=(vmem,) * 6,
        scratch_shapes=[pltpu.VMEM(sums, jnp.float32)],
        compiler_params=params(20),
        name="project",
    )(pos, tab, gauges, anoms, turned, *late)
    common = (pos, tab, gauges, anoms, turned, late_anoms, late_turned)
    carried = ()
    for step in range(ITERS):
        first, last = step == 0, step + 1 == ITERS
        args = (*common, *total_over_gauges(*parts), *carried)
        if last:
            shapes = [f32((peers, 2 * ROWS, LANES))]
            more = [pltpu.VMEM((2 * pairs + n_late, 2 * ROWS, LANES), jnp.float32)]
        else:
            shapes = [*state, *state, f32(sums), f32((ROWS, LANES)), *shards]
            shapes += [] if first else state
            more = []
        has_d = step > 1
        out = pl.pallas_call(
            functools.partial(step_kernel, shape, members, first, last if has_d or first else None),
            out_shape=shapes,
            in_specs=[smem, smem] + [vmem] * (len(args) - 2),
            out_specs=[vmem] * len(shapes),
            scratch_shapes=[
                pltpu.VMEM(sums, jnp.bfloat16),
                pltpu.VMEM(sums, jnp.bfloat16),
                pltpu.VMEM(sums, jnp.float32),
            ] + more,
            compiler_params=params(20),
            name="finish" if last else "step",
        )(*args)
        if not last:
            parts = out[6:10]
            carried = (*out[:6], *out[10:])
    back = lax.all_to_all(out[0], PEERS, 0, 0, tiled=True)
    solution_field, residual = pl.pallas_call(
        out_kernel,
        out_shape=(f32((blk, members)), f32((blk, members))),
        in_specs=[vmem],
        out_specs=(vmem, vmem),
        compiler_params=params(20),
        name="out",
    )(back)
    return solution_field, residual


def solution(mesh):
    fine = Mesh(mesh.devices.reshape(8, 4, 4, 2), ("z", "x", "y", "c"))
    split_all = ("x", "y", "c", "z")
    placed = (P(split_all, None), P(split_all, None), P(split_all), P(split_all), P())
    return jax.shard_map(
        local,
        mesh=fine,
        in_specs=placed,
        out_specs=(P(split_all, None), P(split_all, None)),
        check_vma=False,
    )
```
